512 devices in a mesh: ctx: 64 (over z_hi, x, y, core), head: 8 (over z_lo).
Axes of the slice: x: 4, y: 4, z: 16 (z_hi: 2, z_lo: 8; z = z_hi * 8 + z_lo), core: 2. Of those that a mesh axis runs over, the one named last changes fastest.
Arguments:
- q_nope: bfloat16 [2048, 8192], P('ctx', 'head'), may hold values from -4 to 4
- q_rope: bfloat16 [2048, 4096], P('ctx', 'head'), may hold values from -240 to 240
- prefix_latent: bfloat16 [2048, 512], P('ctx'), may hold values from -4 to 4
- prefix_rope: bfloat16 [2048, 64], P('ctx'), may hold values from -4 to 4
- group_latent: bfloat16 [2048, 512], P('ctx'), may hold values from -4 to 4
- group_rope: bfloat16 [2048, 64], P('ctx'), may hold values from -6 to 6
- lengths: int32 [64], P('ctx'), may hold values from 1 to 32, 1024 in all
- offset: int32 [1], replicated, may hold values from 0 to 4095
- w_uk: bfloat16 [64, 128, 512], P('head'), may hold values from -0.5 to 0.5
- w_uv: bfloat16 [64, 512, 128], P('head'), may hold values from -1 to 1
- w_out: bfloat16 [8192, 7168], P('head', 'ctx'), may hold values from -0.25 to 0.25
Outputs:
- mixed: bfloat16 [2048, 7168], P('head', 'ctx')
The draws below stay inside these ranges and needn't reach their ends.
All inputs are finite; a program needn't handle non-finite values. No bound on the sum of `lengths` on one device may be relied on, other than what follows from the above.
Results may differ from the reference program's by a relative error of at most 0.02.
Values may be sent and summed in bfloat16 or wider, within the bound.
A program may use at most 64 MiB of HBM per device.

```python
import math
import jax
import jax.numpy as jnp
import numpy as np
from jax import lax

D = 7168
LAT = 512
ROPE = 64
NOPE = 128
VD = 128
TOK_DEV = 32
PREFIX_DEV = 32
HEADS = 64
TOKENS = 2048
PREFIX = 2048
N_CTX = 64


def shared_rope(key):
    base_keys = jnp.clip(jax.random.normal(jax.random.fold_in(key, 101), (TOKENS, ROPE), jnp.float32), -4.0, 4.0)
    return base_keys


def draw_group_rope(key, part):
    base_keys = shared_rope(key)
    return base_keys.astype(jnp.bfloat16)


def draw_q_rope(key, part):
    key = jax.random.fold_in(key, 9)
    queries = jnp.clip(jax.random.normal(key, (TOKENS // 2, 2, HEADS, ROPE), jnp.float32), -4.0, 4.0)
    return queries.reshape(TOKENS, HEADS * ROPE).astype(jnp.bfloat16)


def shard_levels(own_key, shape, pieces, least, top_value):
    gain, own = 1.0, jax.random.fold_in(own_key, 6)
    for dim, parts in pieces:
        heights = jnp.exp(jax.random.uniform(jax.random.fold_in(own, dim), (parts,), jnp.float32, least / len(pieces), top_value / len(pieces)))
        gain = gain * jnp.repeat(heights, shape[dim] // parts).reshape([-1 if axis == dim else 1 for axis in range(len(shape))])
    return gain


def profile(number_of, total, most, lean):
    weights = [(1 << 20) // math.isqrt(grade ** lean) + 1 for grade in range(2, number_of + 1)]
    surplus, given = total - most - (number_of - 1), [1] * (number_of - 1)
    while surplus > 0:
        movable = [i for i in range(number_of - 1) if given[i] < most]
        mass, budget = sum([weights[i] for i in movable]), surplus
        for i in movable:
            more = min(most - given[i], max(1, budget * weights[i] // mass), surplus)
            given[i] = given[i] + more
            surplus = surplus - more
    return np.array([most] + given)


def uneven_parts(own_key, amount, total, bound, slope):
    if amount == 2:
        one = jax.random.randint(own_key, (), max(1, total - bound), min(bound, total - 1) + 1)
        return jnp.stack([one, total - one])
    sizes = jnp.asarray(profile(amount, total, bound, slope), jnp.int32)
    twos = (amount - 1) // 2
    donor, sink = sizes[1:1 + 2 * twos:2], sizes[2:2 + 2 * twos:2]
    room = jnp.minimum(donor - 1, bound - sink)
    passed = jax.random.randint(jax.random.fold_in(own_key, 1), (twos,), 0, 1 << 20) % (room + 1)
    sizes = sizes.at[1:1 + 2 * twos:2].set(donor - passed).at[2:2 + 2 * twos:2].set(sink + passed)
    return sizes[jax.random.permutation(jax.random.fold_in(own_key, 2), amount)]


def normal_values(rng, shape, width, limit, pieces=(), held_as=jnp.bfloat16):
    loudness = shard_levels(rng, shape, pieces, -0.22, 0.18) if pieces else 1.0
    values = jax.random.normal(rng, shape, jnp.float32) * width * loudness
    return jnp.minimum(jnp.maximum(values, -limit), limit).astype(held_as)


def setup_inputs(seed: int = 0) -> dict:
    streams_of = jax.random.split(jax.random.key(seed), 12)
    return {
        "q_nope": normal_values(streams_of[0], (TOKENS, HEADS * NOPE), 1.0, 4.0, ((0, 64), (1, 8))),
        "q_rope": draw_q_rope(jax.random.fold_in(streams_of[11], 71), 0),
        "prefix_latent": normal_values(streams_of[2], (PREFIX, LAT), 1.0, 4.0, ((0, 64),)),
        "prefix_rope": normal_values(streams_of[3], (PREFIX, ROPE), 1.0, 4.0, ((0, 64),)),
        "group_latent": normal_values(streams_of[4], (TOKENS, LAT), 1.0, 4.0, ((0, 64),)),
        "group_rope": draw_group_rope(jax.random.fold_in(streams_of[11], 71), 0),
        "lengths": uneven_parts(streams_of[6], N_CTX, N_CTX * PREFIX_DEV // 2, PREFIX_DEV, 2).astype(jnp.int32),
        "offset": jax.random.randint(streams_of[7], (1,), 0, 4096).astype(jnp.int32),
        "w_uk": normal_values(streams_of[8], (HEADS, NOPE, LAT), NOPE ** -0.5, 0.5, ((0, 8),)),
        "w_uv": normal_values(streams_of[9], (HEADS, LAT, VD), (LAT // 16) ** -0.5, 1.0, ((0, 8),)),
        "w_out": normal_values(streams_of[10], (HEADS * VD, D), (HEADS * VD // 16) ** -0.5, 0.25, ((0, 8), (1, 64))),
    }


def rotate(vectors, positions):
    half_width = vectors.shape[-1] // 2
    frequency = 10000.0 ** (-2.0 * jnp.arange(half_width, dtype=jnp.float32) / vectors.shape[-1])
    angles = positions[:, None] * frequency[None, :]
    shape_out = (angles.shape[0],) + (1,) * (vectors.ndim - 2) + (half_width,)
    cosine = jnp.cos(angles).reshape(shape_out)
    sine_part = jnp.sin(angles).reshape(shape_out)
    first_half = vectors[..., :half_width]
    second_half = vectors[..., half_width:]
    return jnp.concatenate([first_half * cosine - second_half * sine_part, first_half * sine_part + second_half * cosine], axis=-1)


def reference(q_nope, q_rope, prefix_latent, prefix_rope, group_latent, group_rope, lengths, offset, w_uk, w_uv, w_out):
    score_scale = (NOPE + ROPE) ** -0.5
    positions = (offset[0] + jnp.arange(TOKENS, dtype=jnp.int32)).astype(jnp.float32)
    query_rot = rotate(q_rope.reshape(TOKENS, HEADS, ROPE).astype(jnp.float32), positions).astype(jnp.bfloat16)
    key_rot = rotate(group_rope.astype(jnp.float32), positions).astype(jnp.bfloat16)
    query_lat = jnp.einsum("thn,hnl->thl", q_nope.reshape(TOKENS, HEADS, NOPE).astype(jnp.float32), w_uk.astype(jnp.float32)).astype(jnp.bfloat16)
    all_latent = jnp.concatenate([prefix_latent, group_latent], axis=0)
    all_rope = jnp.concatenate([prefix_rope, key_rot], axis=0)
    prefix_index = jnp.arange(PREFIX, dtype=jnp.int32)
    prefix_ok = (prefix_index % PREFIX_DEV) < lengths[prefix_index // PREFIX_DEV]
    group_index = jnp.arange(TOKENS, dtype=jnp.int32)

    def one_block(block_index):
        start_token = block_index * TOK_DEV
        query_block = lax.dynamic_slice_in_dim(query_lat, start_token, TOK_DEV, 0).reshape(TOK_DEV * HEADS, LAT)
        rope_block = lax.dynamic_slice_in_dim(query_rot, start_token, TOK_DEV, 0).reshape(TOK_DEV * HEADS, ROPE)
        scores = jnp.dot(query_block, all_latent.T, preferred_element_type=jnp.float32)
        scores = (scores + jnp.dot(rope_block, all_rope.T, preferred_element_type=jnp.float32)) * score_scale
        tok_rows = jnp.repeat(start_token + jnp.arange(TOK_DEV, dtype=jnp.int32), HEADS)
        group_ok = group_index[None, :] <= tok_rows[:, None]
        allowed = jnp.concatenate([jnp.broadcast_to(prefix_ok[None, :], (TOK_DEV * HEADS, PREFIX)), group_ok], axis=1)
        scores = jnp.where(allowed, scores, -1e30)
        row_max = jnp.max(scores, axis=1, keepdims=True)
        weights = jnp.where(allowed, jnp.exp(scores - row_max), 0.0)
        total_sum = jnp.sum(weights, axis=1)
        latent_out = jnp.dot(weights.astype(jnp.bfloat16), all_latent, preferred_element_type=jnp.float32) / total_sum[:, None]
        return latent_out.astype(jnp.bfloat16).reshape(TOK_DEV, HEADS, LAT)

    latent_out = lax.map(one_block, jnp.arange(N_CTX, dtype=jnp.int32)).reshape(TOKENS, HEADS, LAT)
    values_out = jnp.einsum("thl,hlv->thv", latent_out.astype(jnp.float32), w_uv.astype(jnp.float32)).astype(jnp.bfloat16)
    values_out = values_out.reshape(TOKENS, HEADS * VD)
    return jnp.dot(values_out, w_out, preferred_element_type=jnp.float32).astype(jnp.bfloat16)
```

```python
import functools
import math

import jax
import jax.numpy as jnp
import numpy as np
from jax import lax
from jax.experimental import pallas as pl
from jax.experimental.pallas import tpu as pltpu
from jax.sharding import PartitionSpec as P

ROPE = 64
NOPE = 128
VD = 128
NX = 4
NY = 4
HIDDEN = -1e30
MESH = pl.DeviceIdType.MESH


class Place:
    def __init__(self, heads):
        c = lax.axis_index("ctx")
        self.heads = heads
        self.head = lax.axis_index("head")
        self.core = lax.rem(c, 2)
        self.y = lax.rem(lax.div(c, 2), NY)
        self.x = lax.rem(lax.div(c, 2 * NY), NX)
        self.zh = lax.div(c, 2 * NX * NY)

    def ctx(self, zh=None, x=None, y=None, core=None):
        zh = self.zh if zh is None else zh
        x = self.x if x is None else x
        y = self.y if y is None else y
        core = self.core if core is None else core
        return ((zh * NX + x) * NY + y) * 2 + core

    def along(self, axis, step):
        if axis == 0:
            return (self.ctx(x=lax.rem(self.x + step + NX, NX)), self.head)
        return (self.ctx(y=lax.rem(self.y + step + NY, NY)), self.head)

    def sibling(self):
        return (self.ctx(core=1 - self.core), self.head)

    def across(self, head=None):
        return (self.ctx(zh=1 - self.zh), self.head if head is None else head)


    def up(self, step):
        z = lax.rem(self.zh * self.heads + self.head + step + 2 * self.heads, 2 * self.heads)
        return lax.div(z, self.heads), lax.rem(z, self.heads)


def greet(devices):
    barrier = pltpu.get_barrier_semaphore()
    for device in devices:
        pl.semaphore_signal(barrier, inc=1, device_id=device, device_id_type=MESH)


def plane_peers(place):
    return [place.along(axis, step) for axis in (0, 1) for step in (1, -1, 2)] + [place.sibling()]


RING = 16
OFFSETS = (0, -1, 1, 2)
STEPS = (1, -1, 2)


class Gather:
    def __init__(self, place, buf, ring_send, ring_recv, pair_send, pair_recv):
        self.place = place
        self.buf = buf
        self.ring_send, self.ring_recv = ring_send, ring_recv
        self.pair_send, self.pair_recv = pair_send, pair_recv

    def zh(self, plane):
        return self.place.zh if plane == 0 else 1 - self.place.zh

    def cell(self, kind, plane, first, second):
        place = self.place
        dx, dy = (second, first) if kind == 0 else (first, second)
        x = lax.rem(place.x + dx + NX, NX)
        y = lax.rem(place.y + dy + NY, NY)
        return self.buf.at[kind, self.zh(plane), x, y, place.core]

    def line(self, kind, plane, second):
        place, zh = self.place, self.zh(plane)
        if kind == 0:
            return self.buf.at[kind, zh, lax.rem(place.x + second + NX, NX), pl.ds(0, NY), place.core]
        return self.buf.at[kind, zh, pl.ds(0, NX), lax.rem(place.y + second + NY, NY), place.core]

    def copy(self, ref, kind, plane, slot, device):
        index = (kind * 2 + plane) * RING + slot
        return pltpu.make_async_remote_copy(
            src_ref=ref,
            dst_ref=ref,
            send_sem=self.ring_send.at[index],
            recv_sem=self.ring_recv.at[index],
            device_id=device,
            device_id_type=MESH,
        )

    def first(self, kind, plane, i):
        return self.copy(self.cell(kind, plane, 0, 0), kind, plane, i, self.place.along(1 - kind, STEPS[i]))

    def second(self, kind, plane, o, direction):
        ref = self.cell(kind, plane, OFFSETS[o], 0)
        return self.copy(ref, kind, plane, 3 + 2 * o + direction, self.place.along(kind, STEPS[direction]))

    def relay(self, kind, plane, o):
        direction = o // 2
        ref = self.cell(kind, plane, OFFSETS[o], -STEPS[direction])
        return self.copy(ref, kind, plane, 11 + o, self.place.along(kind, STEPS[direction]))

    def pair(self, kind, plane, piece):
        ref = self.line(kind, plane, OFFSETS[piece])
        index = (kind * 2 + plane) * 4 + piece
        return pltpu.make_async_remote_copy(
            src_ref=ref,
            dst_ref=ref,
            send_sem=self.pair_send.at[index],
            recv_sem=self.pair_recv.at[index],
            device_id=self.place.sibling(),
            device_id_type=MESH,
        )

    def start(self, plane):
        for i in range(3):
            for kind in (0, 1):
                self.first(kind, plane, i).start()
        for direction in (0, 1):
            for kind in (0, 1):
                self.second(kind, plane, 0, direction).start()

    def spread(self, plane):
        for i in range(3):
            for kind in (0, 1):
                self.first(kind, plane, i).wait_recv()
                for direction in (0, 1):
                    self.second(kind, plane, 1 + i, direction).start()
        for kind in (0, 1):
            self.pair(kind, plane, 0).start()

    def hand_on(self, plane):
        for o in range(4):
            for kind in (0, 1):
                for direction in (0, 1):
                    self.second(kind, plane, o, direction).wait_recv()
                self.relay(kind, plane, o).start()
        for piece in (1, 2):
            for kind in (0, 1):
                self.pair(kind, plane, piece).start()

    def complete(self, plane):
        for kind in (0, 1):
            for o in range(4):
                self.relay(kind, plane, o).wait_recv()
            self.pair(kind, plane, 3).start()

    def from_sibling(self, plane):
        for kind in (0, 1):
            for piece in range(4):
                self.pair(kind, plane, piece).wait_recv()

    def finish(self, plane):
        for kind in (0, 1):
            for i in range(3):
                self.first(kind, plane, i).wait_send()
            for o in range(4):
                for direction in (0, 1):
                    self.second(kind, plane, o, direction).wait_send()
                self.relay(kind, plane, o).wait_send()
                self.pair(kind, plane, o).wait_send()


def last_dims(a, b):
    return lax.dot_general(a, b, (((1,), (1,)), ((), ())), preferred_element_type=jnp.float32)


def cos_sin(angle):
    turns = jnp.floor(angle * (2.0 / math.pi) + 0.5)
    rest = ((angle - turns * 1.5703125) - turns * 4.837512969970703125e-4) - turns * 7.54978995489188216e-8
    square = rest * rest
    sine = ((-1.9515295891e-4 * square + 8.3321608736e-3) * square - 1.6666654611e-1) * square * rest + rest
    cosine = (2.443315711809948e-5 * square - 1.388731625493765e-3) * square + 4.166664568298827e-2
    cosine = cosine * square * square - 0.5 * square + 1.0
    quarter = jnp.bitwise_and(turns.astype(jnp.int32), 3)
    swap = jnp.bitwise_and(quarter, 1) == 1
    cos_part = jnp.where(swap, sine, cosine)
    sin_part = jnp.where(swap, cosine, sine)
    cos_part = jnp.where(jnp.logical_or(quarter == 1, quarter == 2), -cos_part, cos_part)
    sin_part = jnp.where(quarter >= 2, -sin_part, sin_part)
    return cos_part, sin_part


def kernel(
    heads,
    lengths,
    offset,
    q_nope_any,
    q_rope_any,
    prefix_latent,
    prefix_rope_any,
    group_latent,
    group_rope_any,
    frequency_any,
    w_uk_any,
    w_uv_any,
    w_out_any,
    mixed,
    keys,
    query,
    row_max,
    row_sum,
    accum,
    outs,
    staged,
    passing,
    w_out,
    shares,
    arrived,
    q_nope,
    q_rope,
    prefix_rope,
    group_rope,
    w_uk,
    w_uv,
    frequency,
    load_sem,
    k_ring_send,
    k_ring_recv,
    k_pair_send,
    k_pair_recv,
    k_cross_send,
    k_cross_recv,
    o_ring_send,
    o_ring_recv,
    o_pair_send,
    o_pair_recv,
    leg_send,
    leg_recv,
    o_cross_send,
    o_cross_recv,
    swap_send,
    swap_recv,
    w_send,
    w_recv,
    share_send,
    share_recv,
):
    place = Place(heads)
    rows, lat = prefix_latent.shape
    h_dev = w_uk.shape[0]
    width = keys.shape[-1]
    half = staged.shape[-1]
    half_heads = heads // 2
    me = place.ctx()
    own = (place.zh, place.x, place.y, place.core)
    odd = lax.rem(place.head, 2)
    paired = place.head + 1 - 2 * odd
    stays = place.core == odd
    moves = place.core != odd
    is_end = jnp.logical_or(place.head == 0, place.head == heads - 1)

    quarter = heads // 2
    legs = []
    for step in (quarter, -quarter):
        leg_zh, leg_head = place.up(step)
        legs.append((place.ctx(zh=leg_zh), leg_head))
    swap_device = (place.ctx(core=1 - place.core), paired)
    swap_across = (place.ctx(zh=1 - place.zh, core=1 - place.core), paired)
    others = [(me, lax.rem(place.head + j, heads)) for j in range(1, heads)]
    far_end = jnp.where(place.head < half_heads, heads - 1, 0)
    served = [jnp.where(place.head == 0, heads - 1 - j, j) for j in range(half_heads)]
    peers = plane_peers(place) + others + [place.across(far_end)]

    greet(peers)

    @pl.when(stays)
    def _():
        greet(legs)

    @pl.when(moves)
    def _():
        greet([swap_device, swap_across])

    @pl.when(is_end)
    def _():
        greet([place.across(head) for head in served])

    loads = [
        pltpu.make_async_copy(src, dst, load_sem.at[i])
        for i, (src, dst) in enumerate(
            (
                (prefix_latent, keys.at[(0,) + own + (slice(None), pl.ds(0, lat))]),
                (group_latent, keys.at[(1,) + own + (slice(None), pl.ds(0, lat))]),
                (q_nope_any, q_nope),
                (q_rope_any, q_rope),
                (prefix_rope_any, prefix_rope),
                (group_rope_any, group_rope),
                (w_uk_any, w_uk),
                (w_uv_any, w_uv),
                (w_out_any, w_out.at[odd]),
                (frequency_any, frequency),
            )
        )
    ]
    for load in loads:
        load.start()
    lane = lax.broadcasted_iota(jnp.int32, (rows, 128), 1)
    row = lax.broadcasted_iota(jnp.int32, (rows, 128), 0)
    for i in (9, 4, 5):
        loads[i].wait()
    positions = (offset[0] + me * rows + row).astype(jnp.float32)
    cos_part, sin_part = cos_sin(positions * frequency[...])
    first_half = lax.rem(lane, ROPE) < ROPE // 2
    sin_part = jnp.where(first_half, -sin_part, sin_part)

    def turn(tile):
        swapped = jnp.where(first_half, pltpu.roll(tile, 128 - ROPE // 2, 1), pltpu.roll(tile, ROPE // 2, 1))
        return tile * cos_part + swapped * sin_part

    def twice(ref):
        value = ref[...].astype(jnp.float32)
        return jnp.concatenate([value, value], axis=1)

    flags = jnp.where(jnp.logical_and(lane == ROPE, row >= lengths[0]), HIDDEN, 0.0)
    tail = pl.ds(lat, width - lat)
    keys[(0,) + own + (slice(None), tail)] = jnp.where(lane < ROPE, twice(prefix_rope), flags).astype(jnp.bfloat16)
    keys[(1,) + own + (slice(None), tail)] = jnp.where(lane < ROPE, turn(twice(group_rope)), 0.0).astype(jnp.bfloat16)
    loads[0].wait()
    loads[1].wait()

    pl.semaphore_wait(pltpu.get_barrier_semaphore(), len(peers) + 2 + half_heads * is_end.astype(jnp.int32))

    gather = Gather(place, keys, k_ring_send, k_ring_recv, k_pair_send, k_pair_recv)

    def key_cross(kind, j):
        ref = keys.at[(kind,) + own]
        return pltpu.make_async_remote_copy(
            src_ref=ref,
            dst_ref=ref,
            send_sem=k_cross_send.at[kind * half_heads + j],
            recv_sem=k_cross_recv.at[kind],
            device_id=place.across(served[j]),
            device_id_type=MESH,
        )

    @pl.when(is_end)
    def _():
        for j in reversed(range(half_heads)):
            for kind in (0, 1):
                key_cross(kind, j).start()

    gather.start(0)

    loads[2].wait()
    loads[3].wait()
    loads[6].wait()
    one = jnp.where(lane == ROPE, 1.0, 0.0)
    for pair in range(h_dev // 2):
        tile = q_rope[:, pair * 128 : (pair + 1) * 128].astype(jnp.float32)
        turned = turn(tile)
        for side in (0, 1):
            head = 2 * pair + side
            if side == 1:
                turned = pltpu.roll(turned, ROPE, 1)
            query[pl.ds(head * rows, rows), pl.ds(lat, width - lat)] = jnp.where(lane < ROPE, turned, one).astype(
                jnp.bfloat16
            )
            query[pl.ds(head * rows, rows), pl.ds(0, lat)] = jnp.dot(
                q_nope[:, head * NOPE : (head + 1) * NOPE], w_uk[head], preferred_element_type=jnp.float32
            ).astype(jnp.bfloat16)

    row_max[...] = jnp.full(row_max.shape, HIDDEN, jnp.float32)
    row_sum[...] = jnp.zeros(row_sum.shape, jnp.float32)
    accum[...] = jnp.zeros(accum.shape, jnp.float32)
    scale = (NOPE + ROPE) ** -0.5 * math.log2(math.e)
    q_rows = h_dev * rows
    chunk = NX * NY * rows
    my_token = me * rows + lax.rem(lax.broadcasted_iota(jnp.int32, (q_rows, 1), 0), rows)

    def attend(kind, zh, core):
        part = keys[kind, zh, :, :, core].reshape(chunk, width)
        scores = last_dims(query[...], part) * scale
        if kind == 1:
            index = lax.broadcasted_iota(jnp.int32, (1, chunk), 1)
            place_of = (zh * NX * NY + lax.div(index, rows)) * 2 + core
            key_token = place_of * rows + lax.rem(index, rows)
            scores = jnp.where(key_token <= my_token, scores, HIDDEN)
        old_max = row_max[...]
        new_max = jnp.maximum(old_max, jnp.max(scores, axis=1, keepdims=True))
        weights = jnp.exp2(scores - new_max)
        factor = jnp.exp2(old_max - new_max)
        row_max[...] = new_max
        row_sum[...] = row_sum[...] * factor + jnp.sum(weights, axis=1, keepdims=True)
        accum[...] = accum[...] * factor + jnp.dot(
            weights.astype(jnp.bfloat16), part[:, :lat], preferred_element_type=jnp.float32
        )

    w_copy = pltpu.make_async_remote_copy(
        src_ref=w_out_any,
        dst_ref=w_out.at[odd],
        send_sem=w_send,
        recv_sem=w_recv,
        device_id=(me, paired),
        device_id_type=MESH,
    )

    gather.spread(0)
    gather.hand_on(0)
    for kind in (0, 1):
        key_cross(kind, 0).wait_recv()
    gather.start(1)
    w_copy.start()
    gather.complete(0)
    gather.spread(1)
    attend(0, place.zh, place.core)
    gather.hand_on(1)
    attend(1, place.zh, place.core)
    gather.from_sibling(0)
    attend(0, place.zh, 1 - place.core)
    gather.complete(1)
    attend(1, place.zh, 1 - place.core)
    attend(0, 1 - place.zh, place.core)
    attend(1, 1 - place.zh, place.core)
    gather.from_sibling(1)
    attend(0, 1 - place.zh, 1 - place.core)
    attend(1, 1 - place.zh, 1 - place.core)

    loads[7].wait()
    latent_out = (accum[...] / row_sum[...]).astype(jnp.bfloat16)
    per_kind = half // VD
    for head in range(h_dev):
        staged[head // per_kind, :, pl.ds((head % per_kind) * VD, VD)] = jnp.dot(
            latent_out[head * rows : (head + 1) * rows], w_uv[head], preferred_element_type=jnp.float32
        ).astype(jnp.bfloat16)

    slot = (place.x, place.y, place.core)
    new_slot = (place.x, place.y, 1 - place.core)

    def leg(kind):
        return pltpu.make_async_remote_copy(
            src_ref=staged.at[kind],
            dst_ref=passing.at[kind],
            send_sem=leg_send.at[kind],
            recv_sem=leg_recv.at[kind],
            device_id=legs[kind],
            device_id_type=MESH,
        )

    def second_leg(kind):
        end_zh = place.up(quarter if kind == 0 else -quarter)[0]
        return pltpu.make_async_remote_copy(
            src_ref=passing.at[kind],
            dst_ref=outs.at[(kind, 1 - end_zh) + slot],
            send_sem=o_cross_send.at[kind],
            recv_sem=o_cross_recv.at[kind],
            device_id=legs[kind],
            device_id_type=MESH,
        )

    def swap(kind):
        return pltpu.make_async_remote_copy(
            src_ref=staged.at[kind],
            dst_ref=outs.at[(kind, place.zh) + new_slot],
            send_sem=swap_send.at[kind],
            recv_sem=swap_recv.at[kind],
            device_id=swap_device,
            device_id_type=MESH,
        )

    def direct(kind):
        return pltpu.make_async_remote_copy(
            src_ref=staged.at[kind],
            dst_ref=outs.at[(kind, place.zh) + new_slot],
            send_sem=o_cross_send.at[kind],
            recv_sem=o_cross_recv.at[kind],
            device_id=swap_across,
            device_id_type=MESH,
        )

    @pl.when(stays)
    def _():
        for kind in (0, 1):
            leg(kind).start()
        for kind in (0, 1):
            outs[(kind, place.zh) + slot] = staged[kind]

    @pl.when(moves)
    def _():
        for kind in (0, 1):
            swap(kind).start()
        for kind in (0, 1):
            direct(kind).start()
        for kind in (0, 1):
            swap(kind).wait_recv()

    spread = Gather(place, outs, o_ring_send, o_ring_recv, o_pair_send, o_pair_recv)
    spread.start(0)
    gather.finish(0)

    @pl.when(stays)
    def _():
        for kind in (0, 1):
            leg(kind).wait_recv()
            second_leg(kind).start()

    block = shares.shape[-1]

    def share(target, source):
        return pltpu.make_async_remote_copy(
            src_ref=shares.at[target],
            dst_ref=arrived.at[source],
            send_sem=share_send.at[target],
            recv_sem=share_recv.at[source],
            device_id=(me, target),
            device_id_type=MESH,
        )

    def send_shares(zh):
        total = jnp.zeros((NX * block, w_out.shape[1]), jnp.float32)
        for kind in (0, 1):
            for plane in (0, 1):
                tokens = outs[kind, zh, :, :, plane].reshape(NX * block, half)
                total = total + last_dims(tokens, w_out[plane, :, kind * half : (kind + 1) * half])
        for x in range(NX):
            target = zh * NX + x
            shares[target] = total[x * block : (x + 1) * block].T.astype(jnp.bfloat16)

            @pl.when(target != place.head)
            def _():
                share(target, place.head).start()

    spread.spread(0)
    gather.finish(1)
    spread.hand_on(0)
    for kind in (0, 1):
        direct(kind).wait_recv()
    spread.start(1)
    spread.complete(0)
    spread.spread(1)
    loads[8].wait()
    w_copy.wait_recv()
    spread.from_sibling(0)
    send_shares(place.zh)
    spread.hand_on(1)
    spread.complete(1)
    spread.from_sibling(1)
    send_shares(1 - place.zh)
    spread.finish(0)
    spread.finish(1)

    arrived[place.head] = shares[place.head]
    for source in range(heads):

        @pl.when(source != place.head)
        def _():
            share(source, source).wait_recv()

    total = jnp.zeros(mixed.shape, jnp.float32)
    source_lane = lax.broadcasted_iota(jnp.int32, (block, mixed.shape[1]), 0)
    token = lax.broadcasted_iota(jnp.int32, (block, mixed.shape[1]), 1)
    for plane in (0, 1):
        part = jnp.zeros(shares.shape[1:], jnp.float32)
        for source in range(plane, heads, 2):
            part = part + arrived[source].astype(jnp.float32)
        lane_of = lax.div(token, 2 * rows) * rows + lax.rem(token, rows)
        here = jnp.logical_and(lane_of == source_lane, lax.rem(lax.div(token, rows), 2) == plane)
        total = total + jnp.dot(
            part.astype(jnp.bfloat16), jnp.where(here, 1.0, 0.0).astype(jnp.bfloat16), preferred_element_type=jnp.float32
        )
    mixed[...] = total.astype(jnp.bfloat16)

    w_copy.wait_send()

    @pl.when(is_end)
    def _():
        for j in range(half_heads):
            for kind in (0, 1):
                key_cross(kind, j).wait_send()

    @pl.when(stays)
    def _():
        for kind in (0, 1):
            leg(kind).wait_send()
            second_leg(kind).wait_send()

    @pl.when(moves)
    def _():
        for kind in (0, 1):
            swap(kind).wait_send()
            direct(kind).wait_send()

    for target in range(heads):

        @pl.when(target != place.head)
        def _():
            share(target, place.head).wait_send()


def gather_scratch():
    return [
        pltpu.SemaphoreType.DMA((4 * RING,)),
        pltpu.SemaphoreType.DMA((4 * RING,)),
        pltpu.SemaphoreType.DMA((16,)),
        pltpu.SemaphoreType.DMA((16,)),
    ]


def on_device(
    heads,
    q_nope,
    q_rope,
    prefix_latent,
    prefix_rope,
    group_latent,
    group_rope,
    lengths,
    offset,
    w_uk,
    w_uv,
    w_out,
):
    rows, lat = prefix_latent.shape
    h_dev = w_uk.shape[0]
    q_rows = rows * h_dev
    width = lat + 128
    columns = w_out.shape[1]
    half = h_dev * VD // 2
    frequency = 10000.0 ** (-2.0 * (np.arange(128) % (ROPE // 2)) / ROPE)
    frequency = jnp.asarray(frequency[None, :], jnp.float32)

    tokens = rows * 2 * 2 * NX * NY
    block = rows * NY
    vmem = pl.BlockSpec(memory_space=pltpu.VMEM)
    smem = pl.BlockSpec(memory_space=pltpu.SMEM)
    anywhere = pl.BlockSpec(memory_space=pl.ANY)
    dma = pltpu.SemaphoreType.DMA
    mixed = pl.pallas_call(
        functools.partial(kernel, heads),
        out_shape=jax.ShapeDtypeStruct((columns, tokens // heads), jnp.bfloat16),
        in_specs=[smem] * 2 + [anywhere] * 10,
        out_specs=vmem,
        scratch_shapes=[
            pltpu.VMEM((2, 2, NX, NY, 2, rows, width), jnp.bfloat16),
            pltpu.VMEM((q_rows, width), jnp.bfloat16),
            pltpu.VMEM((q_rows, 1), jnp.float32),
            pltpu.VMEM((q_rows, 1), jnp.float32),
            pltpu.VMEM((q_rows, lat), jnp.float32),
            pltpu.VMEM((2, 2, NX, NY, 2, rows, half), jnp.bfloat16),
            pltpu.VMEM((2, rows, half), jnp.bfloat16),
            pltpu.VMEM((2, rows, half), jnp.bfloat16),
            pltpu.VMEM((2, columns, 2 * half), jnp.bfloat16),
            pltpu.VMEM((heads, columns, block), jnp.bfloat16),
            pltpu.VMEM((heads, columns, block), jnp.bfloat16),
            pltpu.VMEM(q_nope.shape, jnp.bfloat16),
            pltpu.VMEM(q_rope.shape, jnp.bfloat16),
            pltpu.VMEM(prefix_rope.shape, jnp.bfloat16),
            pltpu.VMEM(group_rope.shape, jnp.bfloat16),
            pltpu.VMEM(w_uk.shape, jnp.bfloat16),
            pltpu.VMEM(w_uv.shape, jnp.bfloat16),
            pltpu.VMEM((1, 128), jnp.float32),
            dma((10,)),
        ]
        + gather_scratch()
        + [dma((heads,)), dma((2,))]
        + gather_scratch()
        + [dma((2,)), dma((2,)), dma((2,)), dma((2,)), dma((2,)), dma((2,))]
        + [dma(()), dma(()), dma((heads,)), dma((heads,))],
        compiler_params=pltpu.CompilerParams(
            collective_id=0, has_side_effects=True, vmem_limit_bytes=60 * 1024 * 1024
        ),
        name="attention_and_output",
    )(
        lengths,
        offset,
        q_nope,
        q_rope,
        prefix_latent,
        prefix_rope,
        group_latent,
        group_rope,
        frequency,
        w_uk,
        w_uv,
        w_out.T,
    )
    return mixed.T


def solution(mesh):
    return jax.shard_map(
        functools.partial(on_device, mesh.shape["head"]),
        mesh=mesh,
        in_specs=(
            P("ctx", "head"),
            P("ctx", "head"),
            P("ctx", None),
            P("ctx", None),
            P("ctx", None),
            P("ctx", None),
            P("ctx"),
            P(),
            P("head", None, None),
            P("head", None, None),
            P("head", "ctx"),
        ),
        out_specs=P("head", "ctx"),
        check_vma=False,
    )
```

```python
import functools
import math

import jax
import jax.numpy as jnp
import numpy as np
from jax import lax
from jax.experimental import pallas as pl
from jax.experimental.pallas import tpu as pltpu
from jax.sharding import PartitionSpec as P

ROPE = 64
NOPE = 128
VD = 128
NX = 4
NY = 4
HIDDEN = -1e30
UNUSED = 1024.0
MESH = pl.DeviceIdType.MESH


class Place:
    def __init__(self, heads):
        c = lax.axis_index("ctx")
        self.heads = heads
        self.head = lax.axis_index("head")
        self.core = lax.rem(c, 2)
        self.y = lax.rem(lax.div(c, 2), NY)
        self.x = lax.rem(lax.div(c, 2 * NY), NX)
        self.zh = lax.div(c, 2 * NX * NY)

    def ctx(self, zh=None, x=None, y=None, core=None):
        zh = self.zh if zh is None else zh
        x = self.x if x is None else x
        y = self.y if y is None else y
        core = self.core if core is None else core
        return ((zh * NX + x) * NY + y) * 2 + core

    def along(self, axis, step):
        if axis == 0:
            return (self.ctx(x=lax.rem(self.x + step + NX, NX)), self.head)
        return (self.ctx(y=lax.rem(self.y + step + NY, NY)), self.head)

    def sibling(self):
        return (self.ctx(core=1 - self.core), self.head)

    def across(self, head=None):
        return (self.ctx(zh=1 - self.zh), self.head if head is None else head)


    def up(self, step):
        z = lax.rem(self.zh * self.heads + self.head + step + 2 * self.heads, 2 * self.heads)
        return lax.div(z, self.heads), lax.rem(z, self.heads)


def greet(devices):
    barrier = pltpu.get_barrier_semaphore()
    for device in devices:
        pl.semaphore_signal(barrier, inc=1, device_id=device, device_id_type=MESH)


def plane_peers(place):
    return [place.along(axis, step) for axis in (0, 1) for step in (1, -1, 2)] + [place.sibling()]


RING = 16
OFFSETS = (0, -1, 1, 2)
STEPS = (1, -1, 2)


class Gather:
    def __init__(self, place, buf, ring_send, ring_recv, pair_send, pair_recv):
        self.place = place
        self.buf = buf
        self.ring_send, self.ring_recv = ring_send, ring_recv
        self.pair_send, self.pair_recv = pair_send, pair_recv

    def zh(self, plane):
        return self.place.zh if plane == 0 else 1 - self.place.zh

    def cell(self, kind, plane, first, second):
        place = self.place
        dx, dy = (second, first) if kind == 0 else (first, second)
        x = lax.rem(place.x + dx + NX, NX)
        y = lax.rem(place.y + dy + NY, NY)
        return self.buf.at[kind, self.zh(plane), x, y, place.core]

    def line(self, kind, plane, second):
        place, zh = self.place, self.zh(plane)
        if kind == 0:
            return self.buf.at[kind, zh, lax.rem(place.x + second + NX, NX), pl.ds(0, NY), place.core]
        return self.buf.at[kind, zh, pl.ds(0, NX), lax.rem(place.y + second + NY, NY), place.core]

    def copy(self, ref, kind, plane, slot, device):
        index = (kind * 2 + plane) * RING + slot
        return pltpu.make_async_remote_copy(
            src_ref=ref,
            dst_ref=ref,
            send_sem=self.ring_send.at[index],
            recv_sem=self.ring_recv.at[index],
            device_id=device,
            device_id_type=MESH,
        )

    def first(self, kind, plane, i):
        return self.copy(self.cell(kind, plane, 0, 0), kind, plane, i, self.place.along(1 - kind, STEPS[i]))

    def second(self, kind, plane, o, direction):
        ref = self.cell(kind, plane, OFFSETS[o], 0)
        return self.copy(ref, kind, plane, 3 + 2 * o + direction, self.place.along(kind, STEPS[direction]))

    def relay(self, kind, plane, o):
        direction = o // 2
        ref = self.cell(kind, plane, OFFSETS[o], -STEPS[direction])
        return self.copy(ref, kind, plane, 11 + o, self.place.along(kind, STEPS[direction]))

    def pair(self, kind, plane, piece):
        ref = self.line(kind, plane, OFFSETS[piece])
        index = (kind * 2 + plane) * 4 + piece
        return pltpu.make_async_remote_copy(
            src_ref=ref,
            dst_ref=ref,
            send_sem=self.pair_send.at[index],
            recv_sem=self.pair_recv.at[index],
            device_id=self.place.sibling(),
            device_id_type=MESH,
        )

    def start(self, plane):
        for i in range(3):
            for kind in (0, 1):
                self.first(kind, plane, i).start()
        for direction in (0, 1):
            for kind in (0, 1):
                self.second(kind, plane, 0, direction).start()

    def spread(self, plane):
        for i in range(3):
            for kind in (0, 1):
                self.first(kind, plane, i).wait_recv()
                for direction in (0, 1):
                    self.second(kind, plane, 1 + i, direction).start()
        for kind in (0, 1):
            self.pair(kind, plane, 0).start()

    def hand_on(self, plane, offsets=(0, 1, 2, 3)):
        for o in offsets:
            for kind in (0, 1):
                for direction in (0, 1):
                    self.second(kind, plane, o, direction).wait_recv()
                self.relay(kind, plane, o).start()

    def hand_over(self, plane):
        for piece in (1, 2):
            for kind in (0, 1):
                self.pair(kind, plane, piece).start()

    def complete(self, plane):
        for kind in (0, 1):
            for o in range(4):
                self.relay(kind, plane, o).wait_recv()
            self.pair(kind, plane, 3).start()

    def from_sibling(self, plane, pieces=(0, 1, 2, 3)):
        for kind in (0, 1):
            for piece in pieces:
                self.pair(kind, plane, piece).wait_recv()

    def finish(self, plane):
        for kind in (0, 1):
            for i in range(3):
                self.first(kind, plane, i).wait_send()
            for o in range(4):
                for direction in (0, 1):
                    self.second(kind, plane, o, direction).wait_send()
                self.relay(kind, plane, o).wait_send()
                self.pair(kind, plane, o).wait_send()


def last_dims(a, b):
    return lax.dot_general(a, b, (((1,), (1,)), ((), ())), preferred_element_type=jnp.float32)


def cos_sin(angle):
    turns = jnp.floor(angle * (2.0 / math.pi) + 0.5)
    rest = ((angle - turns * 1.5703125) - turns * 4.837512969970703125e-4) - turns * 7.54978995489188216e-8
    square = rest * rest
    sine = ((-1.9515295891e-4 * square + 8.3321608736e-3) * square - 1.6666654611e-1) * square * rest + rest
    cosine = (2.443315711809948e-5 * square - 1.388731625493765e-3) * square + 4.166664568298827e-2
    cosine = cosine * square * square - 0.5 * square + 1.0
    quarter = jnp.bitwise_and(turns.astype(jnp.int32), 3)
    swap = jnp.bitwise_and(quarter, 1) == 1
    cos_part = jnp.where(swap, sine, cosine)
    sin_part = jnp.where(swap, cosine, sine)
    cos_part = jnp.where(jnp.logical_or(quarter == 1, quarter == 2), -cos_part, cos_part)
    sin_part = jnp.where(quarter >= 2, -sin_part, sin_part)
    return cos_part, sin_part


def kernel(
    heads,
    lengths,
    offset,
    q_nope_any,
    q_rope_any,
    prefix_latent,
    prefix_rope_any,
    group_latent,
    group_rope_any,
    frequency_any,
    w_uk_any,
    w_uv_any,
    w_out_any,
    mixed,
    keys,
    prefix_query,
    group_query,
    row_max,
    row_sum,
    accum,
    outs,
    staged,
    passing,
    w_out,
    shares,
    arrived,
    q_nope,
    q_rope,
    prefix_rope,
    group_rope,
    w_uk,
    w_uv,
    frequency,
    load_sem,
    k_ring_send,
    k_ring_recv,
    k_pair_send,
    k_pair_recv,
    k_cross_send,
    k_cross_recv,
    o_ring_send,
    o_ring_recv,
    o_pair_send,
    o_pair_recv,
    leg_send,
    leg_recv,
    o_cross_send,
    o_cross_recv,
    swap_send,
    swap_recv,
    w_send,
    w_recv,
    share_send,
    share_recv,
):
    place = Place(heads)
    rows, lat = prefix_latent.shape
    h_dev = w_uk.shape[0]
    part = rows // 2
    half = staged.shape[-1]
    half_heads = heads // 2
    me = place.ctx()
    own = (place.zh, place.x, place.y, place.core)
    odd = lax.rem(place.head, 2)
    paired = place.head + 1 - 2 * odd
    stays = place.core == odd
    moves = place.core != odd
    is_end = jnp.logical_or(place.head == 0, place.head == heads - 1)

    quarter = heads // 2
    legs = []
    for step in (quarter, -quarter):
        leg_zh, leg_head = place.up(step)
        legs.append((place.ctx(zh=leg_zh), leg_head))
    swap_device = (place.ctx(core=1 - place.core), paired)
    swap_across = (place.ctx(zh=1 - place.zh, core=1 - place.core), paired)
    others = [(me, lax.rem(place.head + j, heads)) for j in range(1, heads)]
    far_end = jnp.where(place.head < half_heads, heads - 1, 0)
    served = [jnp.where(place.head == 0, heads - 1 - j, j) for j in range(half_heads)]
    peers = plane_peers(place) + others + [place.across(far_end)]

    greet(peers)

    @pl.when(stays)
    def _():
        greet(legs)

    @pl.when(moves)
    def _():
        greet([swap_device, swap_across])

    @pl.when(is_end)
    def _():
        greet([place.across(head) for head in served])

    loads = [
        pltpu.make_async_copy(src, dst, load_sem.at[i])
        for i, (src, dst) in enumerate(
            (
                (prefix_latent.at[pl.ds(0, part)], keys.at[(0,) + own + (slice(None), pl.ds(0, lat))]),
                (group_latent.at[pl.ds(0, part)], keys.at[(0,) + own + (slice(None), pl.ds(lat + 128, lat))]),
                (q_nope_any, q_nope),
                (q_rope_any, q_rope),
                (prefix_rope_any, prefix_rope),
                (group_rope_any, group_rope),
                (w_uk_any, w_uk),
                (w_uv_any, w_uv),
                (w_out_any, w_out.at[odd]),
                (frequency_any, frequency),
                (prefix_latent.at[pl.ds(part, part)], keys.at[(1,) + own + (slice(None), pl.ds(0, lat))]),
                (group_latent.at[pl.ds(part, part)], keys.at[(1,) + own + (slice(None), pl.ds(lat + 128, lat))]),
            )
        )
    ]
    for load in loads:
        load.start()
    lane = lax.broadcasted_iota(jnp.int32, (rows, 128), 1)
    row = lax.broadcasted_iota(jnp.int32, (rows, 128), 0)
    for i in (9, 4, 5):
        loads[i].wait()
    positions = (offset[0] + me * rows + row).astype(jnp.float32)
    cos_part, sin_part = cos_sin(positions * frequency[...])
    first_half = lax.rem(lane, ROPE) < ROPE // 2
    sin_part = jnp.where(first_half, -sin_part, sin_part)

    def turn(tile):
        swapped = jnp.where(first_half, pltpu.roll(tile, 128 - ROPE // 2, 1), pltpu.roll(tile, ROPE // 2, 1))
        return tile * cos_part + swapped * sin_part

    def twice(ref):
        value = ref[...].astype(jnp.float32)
        return jnp.concatenate([value, value], axis=1)

    unused = jnp.where(lane == 0, UNUSED, 0.0)
    ropes = jnp.where(row < lengths[0], twice(prefix_rope), unused)
    ropes = jnp.where(lane < ROPE, ropes, turn(twice(group_rope))).astype(jnp.bfloat16)
    for kind in (0, 1):
        keys[(kind,) + own + (slice(None), pl.ds(lat, 128))] = ropes[kind * part : (kind + 1) * part]
    for i in (0, 1, 10, 11):
        loads[i].wait()

    pl.semaphore_wait(pltpu.get_barrier_semaphore(), len(peers) + 2 + half_heads * is_end.astype(jnp.int32))

    gather = Gather(place, keys, k_ring_send, k_ring_recv, k_pair_send, k_pair_recv)

    def key_cross(kind, j):
        ref = keys.at[(kind,) + own]
        return pltpu.make_async_remote_copy(
            src_ref=ref,
            dst_ref=ref,
            send_sem=k_cross_send.at[kind * half_heads + j],
            recv_sem=k_cross_recv.at[kind],
            device_id=place.across(served[j]),
            device_id_type=MESH,
        )

    @pl.when(is_end)
    def _():
        for j in reversed(range(half_heads)):
            for kind in (0, 1):
                key_cross(kind, j).start()

    gather.start(0)

    q_rows = h_dev * rows
    loads[2].wait()
    loads[3].wait()
    loads[6].wait()
    mark = jnp.logical_and(lane[:16] == 0, row[:16] == 0)
    prefix_query[pl.ds(q_rows, 16), pl.ds(0, lat)] = jnp.zeros((16, lat), jnp.bfloat16)
    prefix_query[pl.ds(q_rows, 16), pl.ds(lat, 128)] = jnp.where(mark, 1.0, 0.0).astype(jnp.bfloat16)
    for pair in range(h_dev // 2):
        turned = turn(q_rope[:, pair * 128 : (pair + 1) * 128].astype(jnp.float32))
        other = pltpu.roll(turned, ROPE, 1)
        for side in (0, 1):
            head = 2 * pair + side
            at = pl.ds(head * rows, rows)
            low_part, high_part = (turned, other) if side == 0 else (other, turned)
            prefix_query[at, pl.ds(lat, 128)] = jnp.where(lane < ROPE, low_part, 0.0).astype(jnp.bfloat16)
            group_query[at, pl.ds(0, 128)] = jnp.where(lane >= ROPE, high_part, 0.0).astype(jnp.bfloat16)
            latent = jnp.dot(
                q_nope[:, head * NOPE : (head + 1) * NOPE], w_uk[head], preferred_element_type=jnp.float32
            ).astype(jnp.bfloat16)
            prefix_query[at, pl.ds(0, lat)] = latent
            group_query[at, pl.ds(128, lat)] = latent

    row_max[...] = jnp.full(row_max.shape, HIDDEN, jnp.float32)
    row_sum[...] = jnp.zeros(row_sum.shape, jnp.float32)
    accum[...] = jnp.zeros(accum.shape, jnp.float32)
    scale = (NOPE + ROPE) ** -0.5 * math.log2(math.e)
    my_token = me * rows + lax.rem(lax.broadcasted_iota(jnp.int32, (q_rows, 1), 0), rows)

    def attend(plane, lines):
        zh = gather.zh(plane)
        span = NY * part
        index = lax.broadcasted_iota(jnp.int32, (1, span * len(lines)), 1)
        inside = lax.rem(index, span)
        key_token = jnp.zeros(index.shape, jnp.int32)
        blocks = []
        for i, (kind, step, sibling) in enumerate(lines):
            core = 1 - place.core if sibling else place.core
            if kind == 0:
                x = lax.rem(place.x + step + NX, NX)
                blocks.append(keys[0, zh, x, :, core])
                first, stride = place.ctx(zh=zh, x=x, y=0, core=core), 2
            else:
                y = lax.rem(place.y + step + NY, NY)
                blocks.append(keys[1, zh, :, y, core])
                first, stride = place.ctx(zh=zh, x=0, y=y, core=core), 2 * NY
            token = (first + stride * lax.div(inside, part)) * rows + kind * part + lax.rem(inside, part)
            key_token = jnp.where(lax.div(index, span) == i, token, key_token)
        rows_in = jnp.concatenate([block.reshape(span, block.shape[-1]) for block in blocks], axis=0)
        prefix_all = last_dims(prefix_query[...], rows_in[:, : lat + 128])
        hidden = prefix_all[q_rows : q_rows + 1] > UNUSED / 2
        prefix_scores = jnp.where(hidden, HIDDEN, prefix_all[:q_rows] * scale)
        group_scores = last_dims(group_query[...], rows_in[:, lat:]) * scale
        group_scores = jnp.where(key_token <= my_token, group_scores, HIDDEN)
        old_max = row_max[...]
        new_max = jnp.max(jnp.maximum(prefix_scores, group_scores), axis=1, keepdims=True)
        new_max = jnp.maximum(old_max, new_max)
        prefix_weights = jnp.exp2(prefix_scores - new_max)
        group_weights = jnp.exp2(group_scores - new_max)
        factor = jnp.exp2(old_max - new_max)
        row_max[...] = new_max
        row_sum[...] = row_sum[...] * factor + jnp.sum(prefix_weights + group_weights, axis=1, keepdims=True)
        taken = jnp.dot(prefix_weights.astype(jnp.bfloat16), rows_in[:, :lat], preferred_element_type=jnp.float32)
        taken = taken + jnp.dot(
            group_weights.astype(jnp.bfloat16), rows_in[:, lat + 128 :], preferred_element_type=jnp.float32
        )
        accum[...] = accum[...] * factor + taken

    w_copy = pltpu.make_async_remote_copy(
        src_ref=w_out_any,
        dst_ref=w_out.at[odd],
        send_sem=w_send,
        recv_sem=w_recv,
        device_id=(me, paired),
        device_id_type=MESH,
    )

    def whole(kind, sibling):
        return [(kind, step, sibling) for step in OFFSETS]

    near = OFFSETS[:3]
    gather.spread(0)
    gather.hand_on(0)
    gather.hand_over(0)
    for kind in (0, 1):
        key_cross(kind, 0).wait_recv()
    gather.start(1)
    w_copy.start()
    gather.complete(0)
    attend(0, whole(0, False))
    gather.spread(1)
    attend(0, whole(1, False))
    gather.hand_on(1, (0,))
    gather.from_sibling(0)
    attend(0, whole(0, True))
    gather.hand_on(1, (1, 2))
    attend(0, whole(1, True))
    gather.hand_on(1, (3,))
    gather.hand_over(1)
    attend(1, [(kind, step, False) for kind in (0, 1) for step in near])
    gather.complete(1)
    gather.from_sibling(1, (0, 1, 2))
    attend(1, [(kind, step, True) for kind in (0, 1) for step in near])
    gather.from_sibling(1, (3,))
    attend(1, [(kind, 2, sibling) for kind in (0, 1) for sibling in (False, True)])

    loads[7].wait()
    latent_out = (accum[...] / row_sum[...]).astype(jnp.bfloat16)
    per_kind = half // VD
    for head in range(h_dev):
        staged[head // per_kind, :, pl.ds((head % per_kind) * VD, VD)] = jnp.dot(
            latent_out[head * rows : (head + 1) * rows], w_uv[head], preferred_element_type=jnp.float32
        ).astype(jnp.bfloat16)

    slot = (place.x, place.y, place.core)
    new_slot = (place.x, place.y, 1 - place.core)

    def leg(kind):
        return pltpu.make_async_remote_copy(
            src_ref=staged.at[kind],
            dst_ref=passing.at[kind],
            send_sem=leg_send.at[kind],
            recv_sem=leg_recv.at[kind],
            device_id=legs[kind],
            device_id_type=MESH,
        )

    def second_leg(kind):
        end_zh = place.up(quarter if kind == 0 else -quarter)[0]
        return pltpu.make_async_remote_copy(
            src_ref=passing.at[kind],
            dst_ref=outs.at[(kind, 1 - end_zh) + slot],
            send_sem=o_cross_send.at[kind],
            recv_sem=o_cross_recv.at[kind],
            device_id=legs[kind],
            device_id_type=MESH,
        )

    def swap(kind):
        return pltpu.make_async_remote_copy(
            src_ref=staged.at[kind],
            dst_ref=outs.at[(kind, place.zh) + new_slot],
            send_sem=swap_send.at[kind],
            recv_sem=swap_recv.at[kind],
            device_id=swap_device,
            device_id_type=MESH,
        )

    def direct(kind):
        return pltpu.make_async_remote_copy(
            src_ref=staged.at[kind],
            dst_ref=outs.at[(kind, place.zh) + new_slot],
            send_sem=o_cross_send.at[kind],
            recv_sem=o_cross_recv.at[kind],
            device_id=swap_across,
            device_id_type=MESH,
        )

    @pl.when(stays)
    def _():
        for kind in (0, 1):
            leg(kind).start()
        for kind in (0, 1):
            outs[(kind, place.zh) + slot] = staged[kind]

    @pl.when(moves)
    def _():
        for kind in (0, 1):
            swap(kind).start()
        for kind in (0, 1):
            direct(kind).start()
        for kind in (0, 1):
            swap(kind).wait_recv()

    spread = Gather(place, outs, o_ring_send, o_ring_recv, o_pair_send, o_pair_recv)
    spread.start(0)
    gather.finish(0)

    @pl.when(stays)
    def _():
        for kind in (0, 1):
            leg(kind).wait_recv()
            second_leg(kind).start()

    block = shares.shape[-1]

    def share(target, source):
        return pltpu.make_async_remote_copy(
            src_ref=shares.at[target],
            dst_ref=arrived.at[source],
            send_sem=share_send.at[target],
            recv_sem=share_recv.at[source],
            device_id=(me, target),
            device_id_type=MESH,
        )

    def part_share(zh, plane):
        total = jnp.zeros((NX * block, w_out.shape[1]), jnp.float32)
        for kind in (0, 1):
            tokens = outs[kind, zh, :, :, plane].reshape(NX * block, half)
            total = total + last_dims(tokens, w_out[plane, :, kind * half : (kind + 1) * half])
        return total

    def send_shares(plane):
        zh = spread.zh(plane)
        total = part_share(zh, place.core)
        spread.from_sibling(plane)
        total = total + part_share(zh, 1 - place.core)
        for x in range(NX):
            target = zh * NX + x
            shares[target] = total[x * block : (x + 1) * block].T.astype(jnp.bfloat16)

            @pl.when(target != place.head)
            def _():
                share(target, place.head).start()

    spread.spread(0)
    gather.finish(1)
    spread.hand_on(0)
    spread.hand_over(0)
    for kind in (0, 1):
        direct(kind).wait_recv()
    spread.start(1)
    spread.complete(0)
    spread.spread(1)
    loads[8].wait()
    w_copy.wait_recv()
    send_shares(0)
    spread.hand_on(1)
    spread.hand_over(1)
    spread.complete(1)
    send_shares(1)
    spread.finish(0)
    spread.finish(1)

    arrived[place.head] = shares[place.head]
    for source in range(heads):

        @pl.when(source != place.head)
        def _():
            share(source, source).wait_recv()

    total = jnp.zeros(mixed.shape, jnp.float32)
    source_lane = lax.broadcasted_iota(jnp.int32, (block, mixed.shape[1]), 0)
    token = lax.broadcasted_iota(jnp.int32, (block, mixed.shape[1]), 1)
    for plane in (0, 1):
        part = jnp.zeros(shares.shape[1:], jnp.float32)
        for source in range(plane, heads, 2):
            part = part + arrived[source].astype(jnp.float32)
        lane_of = lax.div(token, 2 * rows) * rows + lax.rem(token, rows)
        here = jnp.logical_and(lane_of == source_lane, lax.rem(lax.div(token, rows), 2) == plane)
        total = total + jnp.dot(
            part.astype(jnp.bfloat16), jnp.where(here, 1.0, 0.0).astype(jnp.bfloat16), preferred_element_type=jnp.float32
        )
    mixed[...] = total.astype(jnp.bfloat16)

    w_copy.wait_send()

    @pl.when(is_end)
    def _():
        for j in range(half_heads):
            for kind in (0, 1):
                key_cross(kind, j).wait_send()

    @pl.when(stays)
    def _():
        for kind in (0, 1):
            leg(kind).wait_send()
            second_leg(kind).wait_send()

    @pl.when(moves)
    def _():
        for kind in (0, 1):
            swap(kind).wait_send()
            direct(kind).wait_send()

    for target in range(heads):

        @pl.when(target != place.head)
        def _():
            share(target, place.head).wait_send()


def gather_scratch():
    return [
        pltpu.SemaphoreType.DMA((4 * RING,)),
        pltpu.SemaphoreType.DMA((4 * RING,)),
        pltpu.SemaphoreType.DMA((16,)),
        pltpu.SemaphoreType.DMA((16,)),
    ]


def on_device(
    heads,
    q_nope,
    q_rope,
    prefix_latent,
    prefix_rope,
    group_latent,
    group_rope,
    lengths,
    offset,
    w_uk,
    w_uv,
    w_out,
):
    rows, lat = prefix_latent.shape
    h_dev = w_uk.shape[0]
    q_rows = rows * h_dev
    width = 2 * lat + 128
    columns = w_out.shape[1]
    half = h_dev * VD // 2
    frequency = 10000.0 ** (-2.0 * (np.arange(128) % (ROPE // 2)) / ROPE)
    frequency = jnp.asarray(frequency[None, :], jnp.float32)

    tokens = rows * 2 * 2 * NX * NY
    block = rows * NY
    vmem = pl.BlockSpec(memory_space=pltpu.VMEM)
    smem = pl.BlockSpec(memory_space=pltpu.SMEM)
    anywhere = pl.BlockSpec(memory_space=pl.ANY)
    dma = pltpu.SemaphoreType.DMA
    mixed = pl.pallas_call(
        functools.partial(kernel, heads),
        out_shape=jax.ShapeDtypeStruct((columns, tokens // heads), jnp.bfloat16),
        in_specs=[smem] * 2 + [anywhere] * 10,
        out_specs=vmem,
        scratch_shapes=[
            pltpu.VMEM((2, 2, NX, NY, 2, rows // 2, width), jnp.bfloat16),
            pltpu.VMEM((q_rows + 16, lat + 128), jnp.bfloat16),
            pltpu.VMEM((q_rows, lat + 128), jnp.bfloat16),
            pltpu.VMEM((q_rows, 1), jnp.float32),
            pltpu.VMEM((q_rows, 1), jnp.float32),
            pltpu.VMEM((q_rows, lat), jnp.float32),
            pltpu.VMEM((2, 2, NX, NY, 2, rows, half), jnp.bfloat16),
            pltpu.VMEM((2, rows, half), jnp.bfloat16),
            pltpu.VMEM((2, rows, half), jnp.bfloat16),
            pltpu.VMEM((2, columns, 2 * half), jnp.bfloat16),
            pltpu.VMEM((heads, columns, block), jnp.bfloat16),
            pltpu.VMEM((heads, columns, block), jnp.bfloat16),
            pltpu.VMEM(q_nope.shape, jnp.bfloat16),
            pltpu.VMEM(q_rope.shape, jnp.bfloat16),
            pltpu.VMEM(prefix_rope.shape, jnp.bfloat16),
            pltpu.VMEM(group_rope.shape, jnp.bfloat16),
            pltpu.VMEM(w_uk.shape, jnp.bfloat16),
            pltpu.VMEM(w_uv.shape, jnp.bfloat16),
            pltpu.VMEM((1, 128), jnp.float32),
            dma((12,)),
        ]
        + gather_scratch()
        + [dma((heads,)), dma((2,))]
        + gather_scratch()
        + [dma((2,)), dma((2,)), dma((2,)), dma((2,)), dma((2,)), dma((2,))]
        + [dma(()), dma(()), dma((heads,)), dma((heads,))],
        compiler_params=pltpu.CompilerParams(
            collective_id=0, has_side_effects=True, vmem_limit_bytes=60 * 1024 * 1024
        ),
        name="attention_and_output",
    )(
        lengths,
        offset,
        q_nope,
        q_rope,
        prefix_latent,
        prefix_rope,
        group_latent,
        group_rope,
        frequency,
        w_uk,
        w_uv,
        w_out.T,
    )
    return mixed.T


def solution(mesh):
    return jax.shard_map(
        functools.partial(on_device, mesh.shape["head"]),
        mesh=mesh,
        in_specs=(
            P("ctx", "head"),
            P("ctx", "head"),
            P("ctx", None),
            P("ctx", None),
            P("ctx", None),
            P("ctx", None),
            P("ctx"),
            P(),
            P("head", None, None),
            P("head", None, None),
            P("head", "ctx"),
        ),
        out_specs=P("head", "ctx"),
        check_vma=False,
    )
```

```python
import functools
import math

import jax
import jax.numpy as jnp
import numpy as np
from jax import lax
from jax.experimental import pallas as pl
from jax.experimental.pallas import tpu as pltpu
from jax.sharding import PartitionSpec as P

ROPE = 64
NOPE = 128
VD = 128
NX = 4
NY = 4
HIDDEN = -1e30
UNUSED = 1024.0
MESH = pl.DeviceIdType.MESH


class Place:
    def __init__(self, heads):
        c = lax.axis_index("ctx")
        self.heads = heads
        self.head = lax.axis_index("head")
        self.core = lax.rem(c, 2)
        self.y = lax.rem(lax.div(c, 2), NY)
        self.x = lax.rem(lax.div(c, 2 * NY), NX)
        self.zh = lax.div(c, 2 * NX * NY)

    def ctx(self, zh=None, x=None, y=None, core=None):
        zh = self.zh if zh is None else zh
        x = self.x if x is None else x
        y = self.y if y is None else y
        core = self.core if core is None else core
        return ((zh * NX + x) * NY + y) * 2 + core

    def along(self, axis, step):
        if axis == 0:
            return (self.ctx(x=lax.rem(self.x + step + NX, NX)), self.head)
        return (self.ctx(y=lax.rem(self.y + step + NY, NY)), self.head)

    def sibling(self):
        return (self.ctx(core=1 - self.core), self.head)

    def across(self, head=None):
        return (self.ctx(zh=1 - self.zh), self.head if head is None else head)


    def up(self, step):
        z = lax.rem(self.zh * self.heads + self.head + step + 2 * self.heads, 2 * self.heads)
        return lax.div(z, self.heads), lax.rem(z, self.heads)


def greet(devices):
    barrier = pltpu.get_barrier_semaphore()
    for device in devices:
        pl.semaphore_signal(barrier, inc=1, device_id=device, device_id_type=MESH)


def plane_peers(place):
    return [place.along(axis, step) for axis in (0, 1) for step in (1, -1, 2)] + [place.sibling()]


RING = 16
OFFSETS = (0, -1, 1, 2)
STEPS = (1, -1, 2)


class Gather:
    def __init__(self, place, buf, ring_send, ring_recv, pair_send, pair_recv):
        self.place = place
        self.buf = buf
        self.ring_send, self.ring_recv = ring_send, ring_recv
        self.pair_send, self.pair_recv = pair_send, pair_recv

    def zh(self, plane):
        return self.place.zh if plane == 0 else 1 - self.place.zh

    def cell(self, kind, plane, first, second):
        place = self.place
        dx, dy = (second, first) if kind == 0 else (first, second)
        x = lax.rem(place.x + dx + NX, NX)
        y = lax.rem(place.y + dy + NY, NY)
        return self.buf.at[kind, self.zh(plane), x, y, place.core]

    def line(self, kind, plane, second):
        place, zh = self.place, self.zh(plane)
        if kind == 0:
            return self.buf.at[kind, zh, lax.rem(place.x + second + NX, NX), pl.ds(0, NY), place.core]
        return self.buf.at[kind, zh, pl.ds(0, NX), lax.rem(place.y + second + NY, NY), place.core]

    def copy(self, ref, kind, plane, slot, device):
        index = (kind * 2 + plane) * RING + slot
        return pltpu.make_async_remote_copy(
            src_ref=ref,
            dst_ref=ref,
            send_sem=self.ring_send.at[index],
            recv_sem=self.ring_recv.at[index],
            device_id=device,
            device_id_type=MESH,
        )

    def first(self, kind, plane, i):
        return self.copy(self.cell(kind, plane, 0, 0), kind, plane, i, self.place.along(1 - kind, STEPS[i]))

    def second(self, kind, plane, o, direction):
        ref = self.cell(kind, plane, OFFSETS[o], 0)
        return self.copy(ref, kind, plane, 3 + 2 * o + direction, self.place.along(kind, STEPS[direction]))

    def relay(self, kind, plane, o):
        direction = o // 2
        ref = self.cell(kind, plane, OFFSETS[o], -STEPS[direction])
        return self.copy(ref, kind, plane, 11 + o, self.place.along(kind, STEPS[direction]))

    def pair(self, kind, plane, piece):
        ref = self.line(kind, plane, OFFSETS[piece])
        index = (kind * 2 + plane) * 4 + piece
        return pltpu.make_async_remote_copy(
            src_ref=ref,
            dst_ref=ref,
            send_sem=self.pair_send.at[index],
            recv_sem=self.pair_recv.at[index],
            device_id=self.place.sibling(),
            device_id_type=MESH,
        )

    def start(self, plane):
        for i in range(3):
            for kind in (0, 1):
                self.first(kind, plane, i).start()
        for direction in (0, 1):
            for kind in (0, 1):
                self.second(kind, plane, 0, direction).start()

    def spread(self, plane):
        for i in range(3):
            for kind in (0, 1):
                self.first(kind, plane, i).wait_recv()
                for direction in (0, 1):
                    self.second(kind, plane, 1 + i, direction).start()
        for kind in (0, 1):
            self.pair(kind, plane, 0).start()

    def hand_on(self, plane, offsets=(0, 1, 2, 3)):
        for o in offsets:
            for kind in (0, 1):
                for direction in (0, 1):
                    self.second(kind, plane, o, direction).wait_recv()
                self.relay(kind, plane, o).start()

    def hand_over(self, plane):
        for piece in (1, 2):
            for kind in (0, 1):
                self.pair(kind, plane, piece).start()

    def complete(self, plane):
        for kind in (0, 1):
            for o in range(4):
                self.relay(kind, plane, o).wait_recv()
            self.pair(kind, plane, 3).start()

    def from_sibling(self, plane, pieces=(0, 1, 2, 3)):
        for kind in (0, 1):
            for piece in pieces:
                self.pair(kind, plane, piece).wait_recv()

    def finish(self, plane):
        for kind in (0, 1):
            for i in range(3):
                self.first(kind, plane, i).wait_send()
            for o in range(4):
                for direction in (0, 1):
                    self.second(kind, plane, o, direction).wait_send()
                self.relay(kind, plane, o).wait_send()
                self.pair(kind, plane, o).wait_send()


def last_dims(a, b):
    return lax.dot_general(a, b, (((1,), (1,)), ((), ())), preferred_element_type=jnp.float32)


def cos_sin(angle):
    turns = jnp.floor(angle * (2.0 / math.pi) + 0.5)
    rest = ((angle - turns * 1.5703125) - turns * 4.837512969970703125e-4) - turns * 7.54978995489188216e-8
    square = rest * rest
    sine = ((-1.9515295891e-4 * square + 8.3321608736e-3) * square - 1.6666654611e-1) * square * rest + rest
    cosine = (2.443315711809948e-5 * square - 1.388731625493765e-3) * square + 4.166664568298827e-2
    cosine = cosine * square * square - 0.5 * square + 1.0
    quarter = jnp.bitwise_and(turns.astype(jnp.int32), 3)
    swap = jnp.bitwise_and(quarter, 1) == 1
    cos_part = jnp.where(swap, sine, cosine)
    sin_part = jnp.where(swap, cosine, sine)
    cos_part = jnp.where(jnp.logical_or(quarter == 1, quarter == 2), -cos_part, cos_part)
    sin_part = jnp.where(quarter >= 2, -sin_part, sin_part)
    return cos_part, sin_part


def kernel(
    heads,
    lengths,
    offset,
    q_nope_any,
    q_rope_any,
    prefix_latent,
    prefix_rope_any,
    group_latent,
    group_rope_any,
    frequency_any,
    w_uk_any,
    w_uv_any,
    w_out_any,
    mixed,
    keys,
    prefix_query,
    group_query,
    row_max,
    row_sum,
    accum,
    outs,
    staged,
    passing,
    w_out,
    shares,
    arrived,
    passed,
    q_nope,
    q_rope,
    prefix_rope,
    group_rope,
    w_uk,
    w_uv,
    frequency,
    load_sem,
    k_ring_send,
    k_ring_recv,
    k_pair_send,
    k_pair_recv,
    k_cross_send,
    k_cross_recv,
    o_ring_send,
    o_ring_recv,
    o_pair_send,
    o_pair_recv,
    leg_send,
    leg_recv,
    o_cross_send,
    o_cross_recv,
    swap_send,
    swap_recv,
    w_send,
    w_recv,
    share_send,
    share_recv,
    hop_send,
    hop_recv,
):
    place = Place(heads)
    rows, lat = prefix_latent.shape
    h_dev = w_uk.shape[0]
    part = rows // 2
    half = staged.shape[-1]
    half_heads = heads // 2
    me = place.ctx()
    own = (place.zh, place.x, place.y, place.core)
    odd = lax.rem(place.head, 2)
    paired = place.head + 1 - 2 * odd
    stays = place.core == odd
    moves = place.core != odd
    is_end = jnp.logical_or(place.head == 0, place.head == heads - 1)

    quarter = heads // 2
    legs = []
    for step in (quarter, -quarter):
        leg_zh, leg_head = place.up(step)
        legs.append((place.ctx(zh=leg_zh), leg_head))
    swap_device = (place.ctx(core=1 - place.core), paired)
    swap_across = (place.ctx(zh=1 - place.zh, core=1 - place.core), paired)
    others = [(me, lax.rem(place.head + j, heads)) for j in range(1, heads)]
    far_end = jnp.where(place.head < half_heads, heads - 1, 0)
    served = [jnp.where(place.head == 0, heads - 1 - j, j) for j in range(half_heads)]
    peers = plane_peers(place) + others + [place.across(far_end)]

    greet(peers)

    @pl.when(stays)
    def _():
        greet(legs)

    @pl.when(moves)
    def _():
        greet([swap_device, swap_across])

    @pl.when(is_end)
    def _():
        greet([place.across(head) for head in served])

    loads = [
        pltpu.make_async_copy(src, dst, load_sem.at[i])
        for i, (src, dst) in enumerate(
            (
                (prefix_latent.at[pl.ds(0, part)], keys.at[(0,) + own + (slice(None), pl.ds(0, lat))]),
                (group_latent.at[pl.ds(0, part)], keys.at[(0,) + own + (slice(None), pl.ds(lat + 128, lat))]),
                (q_nope_any, q_nope),
                (q_rope_any, q_rope),
                (prefix_rope_any, prefix_rope),
                (group_rope_any, group_rope),
                (w_uk_any, w_uk),
                (w_uv_any, w_uv),
                (w_out_any, w_out.at[odd]),
                (frequency_any, frequency),
                (prefix_latent.at[pl.ds(part, part)], keys.at[(1,) + own + (slice(None), pl.ds(0, lat))]),
                (group_latent.at[pl.ds(part, part)], keys.at[(1,) + own + (slice(None), pl.ds(lat + 128, lat))]),
            )
        )
    ]
    for load in loads:
        load.start()
    lane = lax.broadcasted_iota(jnp.int32, (rows, 128), 1)
    row = lax.broadcasted_iota(jnp.int32, (rows, 128), 0)
    for i in (9, 4, 5):
        loads[i].wait()
    positions = (offset[0] + me * rows + row).astype(jnp.float32)
    cos_part, sin_part = cos_sin(positions * frequency[...])
    first_half = lax.rem(lane, ROPE) < ROPE // 2
    sin_part = jnp.where(first_half, -sin_part, sin_part)

    def turn(tile):
        swapped = jnp.where(first_half, pltpu.roll(tile, 128 - ROPE // 2, 1), pltpu.roll(tile, ROPE // 2, 1))
        return tile * cos_part + swapped * sin_part

    def twice(ref):
        value = ref[...].astype(jnp.float32)
        return jnp.concatenate([value, value], axis=1)

    unused = jnp.where(lane == 0, UNUSED, 0.0)
    ropes = jnp.where(row < lengths[0], twice(prefix_rope), unused)
    ropes = jnp.where(lane < ROPE, ropes, turn(twice(group_rope))).astype(jnp.bfloat16)
    for kind in (0, 1):
        keys[(kind,) + own + (slice(None), pl.ds(lat, 128))] = ropes[kind * part : (kind + 1) * part]
    for i in (0, 1, 10, 11):
        loads[i].wait()

    pl.semaphore_wait(pltpu.get_barrier_semaphore(), len(peers) + 2 + half_heads * is_end.astype(jnp.int32))

    gather = Gather(place, keys, k_ring_send, k_ring_recv, k_pair_send, k_pair_recv)

    def key_cross(kind, j):
        ref = keys.at[(kind,) + own]
        return pltpu.make_async_remote_copy(
            src_ref=ref,
            dst_ref=ref,
            send_sem=k_cross_send.at[kind * half_heads + j],
            recv_sem=k_cross_recv.at[kind],
            device_id=place.across(served[j]),
            device_id_type=MESH,
        )

    @pl.when(is_end)
    def _():
        for j in reversed(range(half_heads)):
            for kind in (0, 1):
                key_cross(kind, j).start()

    gather.start(0)

    scale = (NOPE + ROPE) ** -0.5 * math.log2(math.e)

    q_rows = h_dev * rows
    loads[2].wait()
    loads[3].wait()
    loads[6].wait()
    mark = jnp.logical_and(lane[:16] == 0, row[:16] == 0)
    prefix_query[pl.ds(q_rows, 16), pl.ds(0, lat)] = jnp.zeros((16, lat), jnp.bfloat16)
    prefix_query[pl.ds(q_rows, 16), pl.ds(lat, 128)] = jnp.where(mark, 1.0, 0.0).astype(jnp.bfloat16)
    for pair in range(h_dev // 2):
        turned = turn(q_rope[:, pair * 128 : (pair + 1) * 128].astype(jnp.float32)) * scale
        other = pltpu.roll(turned, ROPE, 1)
        for side in (0, 1):
            head = 2 * pair + side
            at = pl.ds(head * rows, rows)
            low_part, high_part = (turned, other) if side == 0 else (other, turned)
            prefix_query[at, pl.ds(lat, 128)] = jnp.where(lane < ROPE, low_part, 0.0).astype(jnp.bfloat16)
            group_query[at, pl.ds(0, 128)] = jnp.where(lane >= ROPE, high_part, 0.0).astype(jnp.bfloat16)
            latent = jnp.dot(
                q_nope[:, head * NOPE : (head + 1) * NOPE], w_uk[head], preferred_element_type=jnp.float32
            )
            latent = (latent * scale).astype(jnp.bfloat16)
            prefix_query[at, pl.ds(0, lat)] = latent
            group_query[at, pl.ds(128, lat)] = latent

    row_max[...] = jnp.full(row_max.shape, HIDDEN, jnp.float32)
    row_sum[...] = jnp.zeros(row_sum.shape, jnp.float32)
    accum[...] = jnp.zeros(accum.shape, jnp.float32)
    my_token = me * rows + lax.rem(lax.broadcasted_iota(jnp.int32, (q_rows, 1), 0), rows)

    def attend(plane, lines):
        zh = gather.zh(plane)
        span = NY * part
        index = lax.broadcasted_iota(jnp.int32, (1, span * len(lines)), 1)
        inside = lax.rem(index, span)
        key_token = jnp.zeros(index.shape, jnp.int32)
        blocks = []
        for i, (kind, step, sibling) in enumerate(lines):
            core = 1 - place.core if sibling else place.core
            if kind == 0:
                x = lax.rem(place.x + step + NX, NX)
                blocks.append(keys[0, zh, x, :, core])
                first, stride = place.ctx(zh=zh, x=x, y=0, core=core), 2
            else:
                y = lax.rem(place.y + step + NY, NY)
                blocks.append(keys[1, zh, :, y, core])
                first, stride = place.ctx(zh=zh, x=0, y=y, core=core), 2 * NY
            token = (first + stride * lax.div(inside, part)) * rows + kind * part + lax.rem(inside, part)
            key_token = jnp.where(lax.div(index, span) == i, token, key_token)
        rows_in = jnp.concatenate([block.reshape(span, block.shape[-1]) for block in blocks], axis=0)
        prefix_all = last_dims(prefix_query[...], rows_in[:, : lat + 128])
        hidden = prefix_all[q_rows : q_rows + 1] > UNUSED / 2
        prefix_scores = jnp.where(hidden, HIDDEN, prefix_all[:q_rows])
        group_scores = last_dims(group_query[...], rows_in[:, lat:])
        group_scores = jnp.where(key_token <= my_token, group_scores, HIDDEN)
        old_max = row_max[...]
        new_max = jnp.max(jnp.maximum(prefix_scores, group_scores), axis=1, keepdims=True)
        new_max = jnp.maximum(old_max, new_max)
        prefix_weights = jnp.exp2(prefix_scores - new_max)
        group_weights = jnp.exp2(group_scores - new_max)
        factor = jnp.exp2(old_max - new_max)
        row_max[...] = new_max
        weights = prefix_weights + group_weights
        lanes = weights[:, :128]
        for j in range(1, weights.shape[1] // 128):
            lanes = lanes + weights[:, j * 128 : (j + 1) * 128]
        row_sum[...] = row_sum[...] * factor + lanes
        taken = jnp.dot(prefix_weights.astype(jnp.bfloat16), rows_in[:, :lat], preferred_element_type=jnp.float32)
        taken = taken + jnp.dot(
            group_weights.astype(jnp.bfloat16), rows_in[:, lat + 128 :], preferred_element_type=jnp.float32
        )
        accum[...] = accum[...] * factor + taken

    w_copy = pltpu.make_async_remote_copy(
        src_ref=w_out_any,
        dst_ref=w_out.at[odd],
        send_sem=w_send,
        recv_sem=w_recv,
        device_id=(me, paired),
        device_id_type=MESH,
    )

    def pick(steps, sibling):
        return [(kind, step, sibling) for kind in (0, 1) for step in steps]

    gather.spread(0)
    attend(0, pick((0,), False))
    gather.hand_on(0)
    gather.hand_over(0)
    for kind in (0, 1):
        key_cross(kind, 0).wait_recv()
    gather.start(1)
    w_copy.start()
    attend(0, pick((-1, 1), False))
    gather.complete(0)
    gather.spread(1)
    gather.from_sibling(0, (0, 1, 2))
    attend(0, pick((0, -1), True))
    gather.hand_on(1, (0,))
    attend(0, [(kind, 2, False) for kind in (0, 1)] + [(kind, 1, True) for kind in (0, 1)])
    gather.hand_on(1, (1, 2))
    gather.hand_on(1, (3,))
    gather.hand_over(1)
    attend(1, pick((0, -1, 1), False))
    gather.complete(1)
    gather.from_sibling(0, (3,))
    gather.from_sibling(1, (0, 1, 2))
    attend(1, pick((0, -1, 1), True))
    attend(0, pick((2,), True))
    gather.from_sibling(1, (3,))
    attend(1, pick((2,), False) + pick((2,), True))

    loads[7].wait()
    latent_out = (accum[...] / jnp.sum(row_sum[...], axis=1, keepdims=True)).astype(jnp.bfloat16)
    per_kind = half // VD
    for head in range(h_dev):
        staged[head // per_kind, :, pl.ds((head % per_kind) * VD, VD)] = jnp.dot(
            latent_out[head * rows : (head + 1) * rows], w_uv[head], preferred_element_type=jnp.float32
        ).astype(jnp.bfloat16)

    slot = (place.x, place.y, place.core)
    new_slot = (place.x, place.y, 1 - place.core)

    def leg(kind):
        return pltpu.make_async_remote_copy(
            src_ref=staged.at[kind],
            dst_ref=passing.at[kind],
            send_sem=leg_send.at[kind],
            recv_sem=leg_recv.at[kind],
            device_id=legs[kind],
            device_id_type=MESH,
        )

    def second_leg(kind):
        end_zh = place.up(quarter if kind == 0 else -quarter)[0]
        return pltpu.make_async_remote_copy(
            src_ref=passing.at[kind],
            dst_ref=outs.at[(kind, 1 - end_zh) + slot],
            send_sem=o_cross_send.at[kind],
            recv_sem=o_cross_recv.at[kind],
            device_id=legs[kind],
            device_id_type=MESH,
        )

    def swap(kind):
        return pltpu.make_async_remote_copy(
            src_ref=staged.at[kind],
            dst_ref=outs.at[(kind, place.zh) + new_slot],
            send_sem=swap_send.at[kind],
            recv_sem=swap_recv.at[kind],
            device_id=swap_device,
            device_id_type=MESH,
        )

    def direct(kind):
        return pltpu.make_async_remote_copy(
            src_ref=staged.at[kind],
            dst_ref=outs.at[(kind, place.zh) + new_slot],
            send_sem=o_cross_send.at[kind],
            recv_sem=o_cross_recv.at[kind],
            device_id=swap_across,
            device_id_type=MESH,
        )

    @pl.when(stays)
    def _():
        for kind in (0, 1):
            leg(kind).start()
        for kind in (0, 1):
            outs[(kind, place.zh) + slot] = staged[kind]

    @pl.when(moves)
    def _():
        for kind in (0, 1):
            swap(kind).start()
        for kind in (0, 1):
            direct(kind).start()
        for kind in (0, 1):
            swap(kind).wait_recv()

    spread = Gather(place, outs, o_ring_send, o_ring_recv, o_pair_send, o_pair_recv)
    spread.start(0)
    gather.finish(0)

    @pl.when(stays)
    def _():
        for kind in (0, 1):
            leg(kind).wait_recv()
            second_leg(kind).start()

    block = shares.shape[-1]

    quad = heads // 2
    my_quad = lax.div(place.head, quad)
    inner = jnp.logical_and(place.head >= quad // 2, place.head < quad + quad // 2)
    outer = jnp.logical_not(inner)

    def share(target, slot):
        return pltpu.make_async_remote_copy(
            src_ref=shares.at[target],
            dst_ref=arrived.at[slot],
            send_sem=share_send.at[target],
            recv_sem=share_recv.at[slot],
            device_id=(me, target),
            device_id_type=MESH,
        )

    def near_share(target):
        return share(target, lax.rem(place.head, quad))

    def far_share(target):
        return share(target, quad + lax.rem(place.head, 2))

    def hop(target, x):
        return pltpu.make_async_remote_copy(
            src_ref=shares.at[target],
            dst_ref=passed.at[x],
            send_sem=hop_send.at[x],
            recv_sem=hop_recv.at[x],
            device_id=(me, jnp.where(place.head < quad, place.head + 2, place.head - 2)),
            device_id_type=MESH,
        )

    def part_share(zh, plane):
        total = jnp.zeros((NX * block, w_out.shape[1]), jnp.float32)
        for kind in (0, 1):
            tokens = outs[kind, zh, :, :, plane].reshape(NX * block, half)
            total = total + last_dims(tokens, w_out[plane, :, kind * half : (kind + 1) * half])
        return total

    def send_shares(plane):
        zh = spread.zh(plane)
        total = part_share(zh, place.core)
        spread.from_sibling(plane)
        total = total + part_share(zh, 1 - place.core)
        for x in range(NX):
            target = zh * NX + x
            shares[target] = total[x * block : (x + 1) * block].T.astype(jnp.bfloat16)

            @pl.when(jnp.logical_and(my_quad == zh, target != place.head))
            def _():
                near_share(target).start()

            @pl.when(jnp.logical_and(my_quad != zh, outer))
            def _():
                hop(target, x).start()

    def forward_shares(plane):
        zh = spread.zh(plane)

        @pl.when(jnp.logical_and(my_quad != zh, inner))
        def _():
            for x in range(NX):
                target = zh * NX + x
                hop(target, x).wait_recv()
                total = shares[target].astype(jnp.float32) + passed[x].astype(jnp.float32)
                shares[target] = total.astype(jnp.bfloat16)
                far_share(target).start()

    spread.spread(0)
    gather.finish(1)
    spread.hand_on(0)
    spread.hand_over(0)
    for kind in (0, 1):
        direct(kind).wait_recv()
    spread.start(1)
    spread.complete(0)
    spread.spread(1)
    loads[8].wait()
    w_copy.wait_recv()
    send_shares(0)
    spread.hand_on(1, (0, 1))
    spread.hand_on(1, (2, 3))
    spread.hand_over(1)
    forward_shares(0)
    spread.complete(1)
    send_shares(1)
    forward_shares(1)
    spread.finish(0)
    spread.finish(1)

    own_slot = lax.rem(place.head, quad)
    arrived[own_slot] = shares[place.head]
    for source in range(quad):

        @pl.when(source != own_slot)
        def _():
            share(place.head, source).wait_recv()

    for source in (quad, quad + 1):
        share(place.head, source).wait_recv()

    total = jnp.zeros(mixed.shape, jnp.float32)
    source_lane = lax.broadcasted_iota(jnp.int32, (block, mixed.shape[1]), 0)
    token = lax.broadcasted_iota(jnp.int32, (block, mixed.shape[1]), 1)
    for plane in (0, 1):
        summed = jnp.zeros(shares.shape[1:], jnp.float32)
        for source in range(plane, quad + 2, 2):
            summed = summed + arrived[source].astype(jnp.float32)
        lane_of = lax.div(token, 2 * rows) * rows + lax.rem(token, rows)
        here = jnp.logical_and(lane_of == source_lane, lax.rem(lax.div(token, rows), 2) == plane)
        total = total + jnp.dot(
            summed.astype(jnp.bfloat16), jnp.where(here, 1.0, 0.0).astype(jnp.bfloat16), preferred_element_type=jnp.float32
        )
    mixed[...] = total.astype(jnp.bfloat16)

    w_copy.wait_send()

    @pl.when(is_end)
    def _():
        for j in range(half_heads):
            for kind in (0, 1):
                key_cross(kind, j).wait_send()

    @pl.when(stays)
    def _():
        for kind in (0, 1):
            leg(kind).wait_send()
            second_leg(kind).wait_send()

    @pl.when(moves)
    def _():
        for kind in (0, 1):
            swap(kind).wait_send()
            direct(kind).wait_send()

    for x in range(NX):

        @pl.when(x != own_slot)
        def _():
            near_share(my_quad * quad + x).wait_send()

        @pl.when(inner)
        def _():
            far_share((1 - my_quad) * quad + x).wait_send()

        @pl.when(outer)
        def _():
            hop((1 - my_quad) * quad + x, x).wait_send()


def gather_scratch():
    return [
        pltpu.SemaphoreType.DMA((4 * RING,)),
        pltpu.SemaphoreType.DMA((4 * RING,)),
        pltpu.SemaphoreType.DMA((16,)),
        pltpu.SemaphoreType.DMA((16,)),
    ]


def on_device(
    heads,
    q_nope,
    q_rope,
    prefix_latent,
    prefix_rope,
    group_latent,
    group_rope,
    lengths,
    offset,
    w_uk,
    w_uv,
    w_out,
):
    rows, lat = prefix_latent.shape
    h_dev = w_uk.shape[0]
    q_rows = rows * h_dev
    width = 2 * lat + 128
    columns = w_out.shape[1]
    half = h_dev * VD // 2
    frequency = 10000.0 ** (-2.0 * (np.arange(128) % (ROPE // 2)) / ROPE)
    frequency = jnp.asarray(frequency[None, :], jnp.float32)

    tokens = rows * 2 * 2 * NX * NY
    block = rows * NY
    vmem = pl.BlockSpec(memory_space=pltpu.VMEM)
    smem = pl.BlockSpec(memory_space=pltpu.SMEM)
    anywhere = pl.BlockSpec(memory_space=pl.ANY)
    dma = pltpu.SemaphoreType.DMA
    mixed = pl.pallas_call(
        functools.partial(kernel, heads),
        out_shape=pltpu.VMEM((columns, tokens // heads), jnp.bfloat16),
        in_specs=[smem] * 2 + [anywhere] * 10,
        out_specs=vmem,
        scratch_shapes=[
            pltpu.VMEM((2, 2, NX, NY, 2, rows // 2, width), jnp.bfloat16),
            pltpu.VMEM((q_rows + 16, lat + 128), jnp.bfloat16),
            pltpu.VMEM((q_rows, lat + 128), jnp.bfloat16),
            pltpu.VMEM((q_rows, 1), jnp.float32),
            pltpu.VMEM((q_rows, 128), jnp.float32),
            pltpu.VMEM((q_rows, lat), jnp.float32),
            pltpu.VMEM((2, 2, NX, NY, 2, rows, half), jnp.bfloat16),
            pltpu.VMEM((2, rows, half), jnp.bfloat16),
            pltpu.VMEM((2, rows, half), jnp.bfloat16),
            pltpu.VMEM((2, columns, 2 * half), jnp.bfloat16),
            pltpu.VMEM((heads, columns, block), jnp.bfloat16),
            pltpu.VMEM((heads // 2 + 2, columns, block), jnp.bfloat16),
            pltpu.VMEM((NX, columns, block), jnp.bfloat16),
            pltpu.VMEM(q_nope.shape, jnp.bfloat16),
            pltpu.VMEM(q_rope.shape, jnp.bfloat16),
            pltpu.VMEM(prefix_rope.shape, jnp.bfloat16),
            pltpu.VMEM(group_rope.shape, jnp.bfloat16),
            pltpu.VMEM(w_uk.shape, jnp.bfloat16),
            pltpu.VMEM(w_uv.shape, jnp.bfloat16),
            pltpu.VMEM((1, 128), jnp.float32),
            dma((12,)),
        ]
        + gather_scratch()
        + [dma((heads,)), dma((2,))]
        + gather_scratch()
        + [dma((2,)), dma((2,)), dma((2,)), dma((2,)), dma((2,)), dma((2,))]
        + [dma(()), dma(()), dma((heads,)), dma((heads // 2 + 2,)), dma((NX,)), dma((NX,))],
        compiler_params=pltpu.CompilerParams(
            collective_id=0, has_side_effects=True, vmem_limit_bytes=60 * 1024 * 1024
        ),
        name="attention_and_output",
    )(
        lengths,
        offset,
        q_nope,
        q_rope,
        prefix_latent,
        prefix_rope,
        group_latent,
        group_rope,
        frequency,
        w_uk,
        w_uv,
        w_out.T,
    )
    return mixed.T


def solution(mesh):
    return jax.shard_map(
        functools.partial(on_device, mesh.shape["head"]),
        mesh=mesh,
        in_specs=(
            P("ctx", "head"),
            P("ctx", "head"),
            P("ctx", None),
            P("ctx", None),
            P("ctx", None),
            P("ctx", None),
            P("ctx"),
            P(),
            P("head", None, None),
            P("head", None, None),
            P("head", "ctx"),
        ),
        out_specs=P("head", "ctx"),
        check_vma=False,
    )
```

```python
import functools
import math

import jax
import jax.numpy as jnp
import numpy as np
from jax import lax
from jax.experimental import pallas as pl
from jax.experimental.pallas import tpu as pltpu
from jax.sharding import PartitionSpec as P

ROPE = 64
NOPE = 128
VD = 128
NX = 4
NY = 4
HIDDEN = -1e30
UNUSED = 1024.0
MESH = pl.DeviceIdType.MESH


class Place:
    def __init__(self, heads):
        c = lax.axis_index("ctx")
        self.heads = heads
        self.head = lax.axis_index("head")
        self.core = lax.rem(c, 2)
        self.y = lax.rem(lax.div(c, 2), NY)
        self.x = lax.rem(lax.div(c, 2 * NY), NX)
        self.zh = lax.div(c, 2 * NX * NY)

    def ctx(self, zh=None, x=None, y=None, core=None):
        zh = self.zh if zh is None else zh
        x = self.x if x is None else x
        y = self.y if y is None else y
        core = self.core if core is None else core
        return ((zh * NX + x) * NY + y) * 2 + core

    def along(self, axis, step):
        if axis == 0:
            return (self.ctx(x=lax.rem(self.x + step + NX, NX)), self.head)
        return (self.ctx(y=lax.rem(self.y + step + NY, NY)), self.head)

    def sibling(self):
        return (self.ctx(core=1 - self.core), self.head)

    def across(self, head=None):
        return (self.ctx(zh=1 - self.zh), self.head if head is None else head)


    def up(self, step):
        z = lax.rem(self.zh * self.heads + self.head + step + 2 * self.heads, 2 * self.heads)
        return lax.div(z, self.heads), lax.rem(z, self.heads)


def greet(devices):
    barrier = pltpu.get_barrier_semaphore()
    for device in devices:
        pl.semaphore_signal(barrier, inc=1, device_id=device, device_id_type=MESH)


def plane_peers(place):
    return [place.along(axis, step) for axis in (0, 1) for step in (1, -1, 2)] + [place.sibling()]


RING = 16
OFFSETS = (0, -1, 1, 2)
STEPS = (1, -1, 2)


class Gather:
    def __init__(self, place, buf, ring_send, ring_recv, pair_send, pair_recv):
        self.place = place
        self.buf = buf
        self.ring_send, self.ring_recv = ring_send, ring_recv
        self.pair_send, self.pair_recv = pair_send, pair_recv

    def zh(self, plane):
        return self.place.zh if plane == 0 else 1 - self.place.zh

    def cell(self, kind, plane, first, second):
        place = self.place
        dx, dy = (second, first) if kind == 0 else (first, second)
        x = lax.rem(place.x + dx + NX, NX)
        y = lax.rem(place.y + dy + NY, NY)
        return self.buf.at[kind, self.zh(plane), x, y, place.core]

    def line(self, kind, plane, second):
        place, zh = self.place, self.zh(plane)
        if kind == 0:
            return self.buf.at[kind, zh, lax.rem(place.x + second + NX, NX), pl.ds(0, NY), place.core]
        return self.buf.at[kind, zh, pl.ds(0, NX), lax.rem(place.y + second + NY, NY), place.core]

    def copy(self, ref, kind, plane, slot, device):
        index = (kind * 2 + plane) * RING + slot
        return pltpu.make_async_remote_copy(
            src_ref=ref,
            dst_ref=ref,
            send_sem=self.ring_send.at[index],
            recv_sem=self.ring_recv.at[index],
            device_id=device,
            device_id_type=MESH,
        )

    def first(self, kind, plane, i):
        return self.copy(self.cell(kind, plane, 0, 0), kind, plane, i, self.place.along(1 - kind, STEPS[i]))

    def second(self, kind, plane, o, direction):
        ref = self.cell(kind, plane, OFFSETS[o], 0)
        return self.copy(ref, kind, plane, 3 + 2 * o + direction, self.place.along(kind, STEPS[direction]))

    def relay(self, kind, plane, o):
        direction = o // 2
        ref = self.cell(kind, plane, OFFSETS[o], -STEPS[direction])
        return self.copy(ref, kind, plane, 11 + o, self.place.along(kind, STEPS[direction]))

    def pair(self, kind, plane, piece):
        ref = self.line(kind, plane, OFFSETS[piece])
        index = (kind * 2 + plane) * 4 + piece
        return pltpu.make_async_remote_copy(
            src_ref=ref,
            dst_ref=ref,
            send_sem=self.pair_send.at[index],
            recv_sem=self.pair_recv.at[index],
            device_id=self.place.sibling(),
            device_id_type=MESH,
        )

    def start(self, plane):
        for i in range(3):
            for kind in (0, 1):
                self.first(kind, plane, i).start()
        for direction in (0, 1):
            for kind in (0, 1):
                self.second(kind, plane, 0, direction).start()

    def spread(self, plane):
        for i in range(3):
            for kind in (0, 1):
                self.first(kind, plane, i).wait_recv()
                for direction in (0, 1):
                    self.second(kind, plane, 1 + i, direction).start()
        for kind in (0, 1):
            self.pair(kind, plane, 0).start()

    def hand_on(self, plane, offsets=(0, 1, 2, 3)):
        for o in offsets:
            for kind in (0, 1):
                for direction in (0, 1):
                    self.second(kind, plane, o, direction).wait_recv()
                self.relay(kind, plane, o).start()

    def hand_over(self, plane):
        for piece in (1, 2):
            for kind in (0, 1):
                self.pair(kind, plane, piece).start()

    def complete(self, plane):
        for kind in (0, 1):
            for o in range(4):
                self.relay(kind, plane, o).wait_recv()
            self.pair(kind, plane, 3).start()

    def from_sibling(self, plane, pieces=(0, 1, 2, 3)):
        for kind in (0, 1):
            for piece in pieces:
                self.pair(kind, plane, piece).wait_recv()

    def finish(self, plane):
        for kind in (0, 1):
            for i in range(3):
                self.first(kind, plane, i).wait_send()
            for o in range(4):
                for direction in (0, 1):
                    self.second(kind, plane, o, direction).wait_send()
                self.relay(kind, plane, o).wait_send()
                self.pair(kind, plane, o).wait_send()


def last_dims(a, b):
    return lax.dot_general(a, b, (((1,), (1,)), ((), ())), preferred_element_type=jnp.float32)


def cos_sin(angle):
    turns = jnp.floor(angle * (2.0 / math.pi) + 0.5)
    rest = ((angle - turns * 1.5703125) - turns * 4.837512969970703125e-4) - turns * 7.54978995489188216e-8
    square = rest * rest
    sine = ((-1.9515295891e-4 * square + 8.3321608736e-3) * square - 1.6666654611e-1) * square * rest + rest
    cosine = (2.443315711809948e-5 * square - 1.388731625493765e-3) * square + 4.166664568298827e-2
    cosine = cosine * square * square - 0.5 * square + 1.0
    quarter = jnp.bitwise_and(turns.astype(jnp.int32), 3)
    swap = jnp.bitwise_and(quarter, 1) == 1
    cos_part = jnp.where(swap, sine, cosine)
    sin_part = jnp.where(swap, cosine, sine)
    cos_part = jnp.where(jnp.logical_or(quarter == 1, quarter == 2), -cos_part, cos_part)
    sin_part = jnp.where(quarter >= 2, -sin_part, sin_part)
    return cos_part, sin_part


def kernel(
    heads,
    lengths,
    offset,
    q_nope_any,
    q_rope_any,
    prefix_latent,
    prefix_rope_any,
    group_latent,
    group_rope_any,
    frequency_any,
    w_uk_any,
    w_uv_any,
    w_out_any,
    mixed,
    keys,
    prefix_query,
    group_query,
    row_max,
    row_sum,
    accum,
    outs,
    staged,
    passing,
    w_out,
    shares,
    arrived,
    passed,
    q_nope,
    q_rope,
    prefix_rope,
    group_rope,
    w_uk,
    w_uv,
    frequency,
    load_sem,
    k_ring_send,
    k_ring_recv,
    k_pair_send,
    k_pair_recv,
    k_cross_send,
    k_cross_recv,
    o_ring_send,
    o_ring_recv,
    o_pair_send,
    o_pair_recv,
    leg_send,
    leg_recv,
    o_cross_send,
    o_cross_recv,
    swap_send,
    swap_recv,
    w_send,
    w_recv,
    share_send,
    share_recv,
    hop_send,
    hop_recv,
):
    place = Place(heads)
    rows, lat = prefix_latent.shape
    h_dev = w_uk.shape[0]
    part = rows // 2
    half = staged.shape[-1]
    half_heads = heads // 2
    me = place.ctx()
    own = (place.zh, place.x, place.y, place.core)
    odd = lax.rem(place.head, 2)
    paired = place.head + 1 - 2 * odd
    stays = place.core == odd
    moves = place.core != odd
    is_end = jnp.logical_or(place.head == 0, place.head == heads - 1)

    quarter = heads // 2
    legs = []
    for step in (quarter, -quarter):
        leg_zh, leg_head = place.up(step)
        legs.append((place.ctx(zh=leg_zh), leg_head))
    swap_device = (place.ctx(core=1 - place.core), paired)
    swap_across = (place.ctx(zh=1 - place.zh, core=1 - place.core), paired)
    others = [(me, lax.rem(place.head + j, heads)) for j in range(1, heads)]
    far_end = jnp.where(place.head < half_heads, heads - 1, 0)
    served = [jnp.where(place.head == 0, heads - 1 - j, j) for j in range(half_heads)]
    peers = plane_peers(place) + others + [place.across(far_end)]

    greet(peers)

    @pl.when(stays)
    def _():
        greet(legs)

    @pl.when(moves)
    def _():
        greet([swap_device, swap_across])

    @pl.when(is_end)
    def _():
        greet([place.across(head) for head in served])

    loads = [
        pltpu.make_async_copy(src, dst, load_sem.at[i])
        for i, (src, dst) in enumerate(
            (
                (prefix_latent.at[pl.ds(0, part)], keys.at[(0,) + own + (slice(None), pl.ds(0, lat))]),
                (group_latent.at[pl.ds(0, part)], keys.at[(0,) + own + (slice(None), pl.ds(lat + 128, lat))]),
                (q_nope_any, q_nope),
                (q_rope_any, q_rope),
                (prefix_rope_any, prefix_rope),
                (group_rope_any, group_rope),
                (w_uk_any, w_uk),
                (w_uv_any, w_uv),
                (w_out_any, w_out.at[odd]),
                (frequency_any, frequency),
                (prefix_latent.at[pl.ds(part, part)], keys.at[(1,) + own + (slice(None), pl.ds(0, lat))]),
                (group_latent.at[pl.ds(part, part)], keys.at[(1,) + own + (slice(None), pl.ds(lat + 128, lat))]),
            )
        )
    ]
    for load in loads:
        load.start()
    lane = lax.broadcasted_iota(jnp.int32, (rows, 128), 1)
    row = lax.broadcasted_iota(jnp.int32, (rows, 128), 0)
    for i in (9, 4, 5):
        loads[i].wait()
    positions = (offset[0] + me * rows + row).astype(jnp.float32)
    cos_part, sin_part = cos_sin(positions * frequency[...])
    first_half = lax.rem(lane, ROPE) < ROPE // 2
    sin_part = jnp.where(first_half, -sin_part, sin_part)

    def turn(tile):
        swapped = jnp.where(first_half, pltpu.roll(tile, 128 - ROPE // 2, 1), pltpu.roll(tile, ROPE // 2, 1))
        return tile * cos_part + swapped * sin_part

    def twice(ref):
        value = ref[...].astype(jnp.float32)
        return jnp.concatenate([value, value], axis=1)

    unused = jnp.where(lane == 0, UNUSED, 0.0)
    ropes = jnp.where(row < lengths[0], twice(prefix_rope), unused)
    ropes = jnp.where(lane < ROPE, ropes, turn(twice(group_rope))).astype(jnp.bfloat16)
    for kind in (0, 1):
        keys[(kind,) + own + (slice(None), pl.ds(lat, 128))] = ropes[kind * part : (kind + 1) * part]
    for i in (0, 1, 10, 11):
        loads[i].wait()

    pl.semaphore_wait(pltpu.get_barrier_semaphore(), len(peers) + 2 + half_heads * is_end.astype(jnp.int32))

    gather = Gather(place, keys, k_ring_send, k_ring_recv, k_pair_send, k_pair_recv)

    def key_cross(kind, j):
        ref = keys.at[(kind,) + own]
        return pltpu.make_async_remote_copy(
            src_ref=ref,
            dst_ref=ref,
            send_sem=k_cross_send.at[kind * half_heads + j],
            recv_sem=k_cross_recv.at[kind],
            device_id=place.across(served[j]),
            device_id_type=MESH,
        )

    @pl.when(is_end)
    def _():
        for j in reversed(range(half_heads)):
            for kind in (0, 1):
                key_cross(kind, j).start()

    gather.start(0)

    scale = (NOPE + ROPE) ** -0.5 * math.log2(math.e)

    q_rows = h_dev * rows
    loads[2].wait()
    loads[3].wait()
    loads[6].wait()
    mark = jnp.logical_and(lane[:16] == 0, row[:16] == 0)
    prefix_query[pl.ds(q_rows, 16), pl.ds(0, lat)] = jnp.zeros((16, lat), jnp.bfloat16)
    prefix_query[pl.ds(q_rows, 16), pl.ds(lat, 128)] = jnp.where(mark, 1.0, 0.0).astype(jnp.bfloat16)
    for pair in range(h_dev // 2):
        turned = turn(q_rope[:, pair * 128 : (pair + 1) * 128].astype(jnp.float32)) * scale
        other = pltpu.roll(turned, ROPE, 1)
        for side in (0, 1):
            head = 2 * pair + side
            at = pl.ds(head * rows, rows)
            low_part, high_part = (turned, other) if side == 0 else (other, turned)
            prefix_query[at, pl.ds(lat, 128)] = jnp.where(lane < ROPE, low_part, 0.0).astype(jnp.bfloat16)
            group_query[at, pl.ds(0, 128)] = jnp.where(lane >= ROPE, high_part, 0.0).astype(jnp.bfloat16)
            latent = jnp.dot(
                q_nope[:, head * NOPE : (head + 1) * NOPE], w_uk[head], preferred_element_type=jnp.float32
            )
            latent = (latent * scale).astype(jnp.bfloat16)
            prefix_query[at, pl.ds(0, lat)] = latent
            group_query[at, pl.ds(128, lat)] = latent

    row_max[...] = jnp.full(row_max.shape, HIDDEN, jnp.float32)
    row_sum[...] = jnp.zeros(row_sum.shape, jnp.float32)
    accum[...] = jnp.zeros(accum.shape, jnp.float32)
    my_token = me * rows + lax.rem(lax.broadcasted_iota(jnp.int32, (q_rows, 1), 0), rows)

    def attend(plane, lines):
        zh = gather.zh(plane)
        span = NY * part
        index = lax.broadcasted_iota(jnp.int32, (1, span * len(lines)), 1)
        inside = lax.rem(index, span)
        key_token = jnp.zeros(index.shape, jnp.int32)
        blocks = []
        for i, (kind, step, sibling) in enumerate(lines):
            core = 1 - place.core if sibling else place.core
            if kind == 0:
                x = lax.rem(place.x + step + NX, NX)
                blocks.append(keys[0, zh, x, :, core])
                first, stride = place.ctx(zh=zh, x=x, y=0, core=core), 2
            else:
                y = lax.rem(place.y + step + NY, NY)
                blocks.append(keys[1, zh, :, y, core])
                first, stride = place.ctx(zh=zh, x=0, y=y, core=core), 2 * NY
            token = (first + stride * lax.div(inside, part)) * rows + kind * part + lax.rem(inside, part)
            key_token = jnp.where(lax.div(index, span) == i, token, key_token)
        rows_in = jnp.concatenate([block.reshape(span, block.shape[-1]) for block in blocks], axis=0)
        prefix_all = last_dims(prefix_query[...], rows_in[:, : lat + 128])
        hidden = prefix_all[q_rows : q_rows + 1] > UNUSED / 2
        prefix_scores = jnp.where(hidden, HIDDEN, prefix_all[:q_rows])
        group_scores = last_dims(group_query[...], rows_in[:, lat:])
        group_scores = jnp.where(key_token <= my_token, group_scores, HIDDEN)
        for scores, values in ((prefix_scores, rows_in[:, :lat]), (group_scores, rows_in[:, lat + 128 :])):
            old_max = row_max[...]
            new_max = jnp.maximum(old_max, jnp.max(scores, axis=1, keepdims=True))
            weights = jnp.exp2(scores - new_max)
            factor = jnp.exp2(old_max - new_max)
            row_max[...] = new_max
            lanes = weights[:, :128]
            for j in range(1, weights.shape[1] // 128):
                lanes = lanes + weights[:, j * 128 : (j + 1) * 128]
            row_sum[...] = row_sum[...] * factor + lanes
            accum[...] = accum[...] * factor + jnp.dot(
                weights.astype(jnp.bfloat16), values, preferred_element_type=jnp.float32
            )

    w_copy = pltpu.make_async_remote_copy(
        src_ref=w_out_any,
        dst_ref=w_out.at[odd],
        send_sem=w_send,
        recv_sem=w_recv,
        device_id=(me, paired),
        device_id_type=MESH,
    )

    def pick(steps, sibling):
        return [(kind, step, sibling) for kind in (0, 1) for step in steps]

    gather.spread(0)
    attend(0, pick((0,), False))
    gather.hand_on(0)
    gather.hand_over(0)
    gather.from_sibling(0, (0,))
    attend(0, pick((0,), True))
    for kind in (0, 1):
        key_cross(kind, 0).wait_recv()
    gather.start(1)
    w_copy.start()
    gather.complete(0)
    attend(0, pick((-1, 1), False))
    gather.spread(1)
    gather.from_sibling(0, (1, 2))
    attend(0, pick((-1, 1), True))
    gather.hand_on(1, (0, 1))
    gather.from_sibling(0, (3,))
    attend(0, pick((2,), False) + pick((2,), True))
    gather.hand_on(1, (2, 3))
    gather.hand_over(1)
    attend(1, pick((0, -1, 1), False))
    gather.complete(1)
    gather.from_sibling(1, (0, 1, 2))
    attend(1, pick((0, -1, 1), True))
    gather.from_sibling(1, (3,))
    attend(1, pick((2,), False) + pick((2,), True))

    loads[7].wait()
    latent_out = (accum[...] / jnp.sum(row_sum[...], axis=1, keepdims=True)).astype(jnp.bfloat16)
    per_kind = half // VD

    def head_outputs(kind):
        for head in range(kind * per_kind, (kind + 1) * per_kind):
            staged[kind, :, pl.ds((head % per_kind) * VD, VD)] = jnp.dot(
                latent_out[head * rows : (head + 1) * rows], w_uv[head], preferred_element_type=jnp.float32
            ).astype(jnp.bfloat16)

    slot = (place.x, place.y, place.core)
    new_slot = (place.x, place.y, 1 - place.core)

    def leg(kind):
        return pltpu.make_async_remote_copy(
            src_ref=staged.at[kind],
            dst_ref=passing.at[kind],
            send_sem=leg_send.at[kind],
            recv_sem=leg_recv.at[kind],
            device_id=legs[kind],
            device_id_type=MESH,
        )

    def second_leg(kind):
        end_zh = place.up(quarter if kind == 0 else -quarter)[0]
        return pltpu.make_async_remote_copy(
            src_ref=passing.at[kind],
            dst_ref=outs.at[(kind, 1 - end_zh) + slot],
            send_sem=o_cross_send.at[kind],
            recv_sem=o_cross_recv.at[kind],
            device_id=legs[kind],
            device_id_type=MESH,
        )

    def swap(kind):
        return pltpu.make_async_remote_copy(
            src_ref=staged.at[kind],
            dst_ref=outs.at[(kind, place.zh) + new_slot],
            send_sem=swap_send.at[kind],
            recv_sem=swap_recv.at[kind],
            device_id=swap_device,
            device_id_type=MESH,
        )

    def direct(kind):
        return pltpu.make_async_remote_copy(
            src_ref=staged.at[kind],
            dst_ref=outs.at[(kind, place.zh) + new_slot],
            send_sem=o_cross_send.at[kind],
            recv_sem=o_cross_recv.at[kind],
            device_id=swap_across,
            device_id_type=MESH,
        )

    for kind in (0, 1):
        head_outputs(kind)

        @pl.when(stays)
        def _():
            leg(kind).start()
            outs[(kind, place.zh) + slot] = staged[kind]

        @pl.when(moves)
        def _():
            swap(kind).start()
            direct(kind).start()

    @pl.when(moves)
    def _():
        for kind in (0, 1):
            swap(kind).wait_recv()

    spread = Gather(place, outs, o_ring_send, o_ring_recv, o_pair_send, o_pair_recv)
    spread.start(0)
    gather.finish(0)

    @pl.when(stays)
    def _():
        for kind in (0, 1):
            leg(kind).wait_recv()
            second_leg(kind).start()

    block = shares.shape[-1]

    quad = heads // 2
    my_quad = lax.div(place.head, quad)
    inner = jnp.logical_and(place.head >= quad // 2, place.head < quad + quad // 2)
    outer = jnp.logical_not(inner)

    def share(target, slot):
        return pltpu.make_async_remote_copy(
            src_ref=shares.at[target],
            dst_ref=arrived.at[slot],
            send_sem=share_send.at[target],
            recv_sem=share_recv.at[slot],
            device_id=(me, target),
            device_id_type=MESH,
        )

    def near_share(target):
        return share(target, lax.rem(place.head, quad))

    def far_share(target):
        return share(target, quad + lax.rem(place.head, 2))

    def hop(target, x):
        return pltpu.make_async_remote_copy(
            src_ref=shares.at[target],
            dst_ref=passed.at[x],
            send_sem=hop_send.at[x],
            recv_sem=hop_recv.at[x],
            device_id=(me, jnp.where(place.head < quad, place.head + 2, place.head - 2)),
            device_id_type=MESH,
        )

    def part_share(zh, plane):
        total = jnp.zeros((NX * block, w_out.shape[1]), jnp.float32)
        for kind in (0, 1):
            tokens = outs[kind, zh, :, :, plane].reshape(NX * block, half)
            total = total + last_dims(tokens, w_out[plane, :, kind * half : (kind + 1) * half])
        return total

    def send_shares(plane):
        zh = spread.zh(plane)
        total = part_share(zh, place.core)
        spread.from_sibling(plane)
        total = total + part_share(zh, 1 - place.core)
        for x in range(NX):
            target = zh * NX + x
            shares[target] = total[x * block : (x + 1) * block].T.astype(jnp.bfloat16)

            @pl.when(jnp.logical_and(my_quad == zh, target != place.head))
            def _():
                near_share(target).start()

            @pl.when(jnp.logical_and(my_quad != zh, outer))
            def _():
                hop(target, x).start()

    def forward_shares(plane):
        zh = spread.zh(plane)

        @pl.when(jnp.logical_and(my_quad != zh, inner))
        def _():
            for x in range(NX):
                target = zh * NX + x
                hop(target, x).wait_recv()
                total = shares[target].astype(jnp.float32) + passed[x].astype(jnp.float32)
                shares[target] = total.astype(jnp.bfloat16)
                far_share(target).start()

    spread.spread(0)
    gather.finish(1)
    spread.hand_on(0)
    spread.hand_over(0)
    for kind in (0, 1):
        direct(kind).wait_recv()
    spread.start(1)
    spread.complete(0)
    spread.spread(1)
    loads[8].wait()
    w_copy.wait_recv()
    send_shares(0)
    spread.hand_on(1, (0, 1))
    spread.hand_on(1, (2, 3))
    spread.hand_over(1)
    forward_shares(0)
    spread.complete(1)
    send_shares(1)
    forward_shares(1)
    spread.finish(0)
    spread.finish(1)

    own_slot = lax.rem(place.head, quad)
    arrived[own_slot] = shares[place.head]
    for source in range(quad):

        @pl.when(source != own_slot)
        def _():
            share(place.head, source).wait_recv()

    for source in (quad, quad + 1):
        share(place.head, source).wait_recv()

    total = jnp.zeros(mixed.shape, jnp.float32)
    source_lane = lax.broadcasted_iota(jnp.int32, (block, mixed.shape[1]), 0)
    token = lax.broadcasted_iota(jnp.int32, (block, mixed.shape[1]), 1)
    for plane in (0, 1):
        summed = jnp.zeros(shares.shape[1:], jnp.float32)
        for source in range(plane, quad + 2, 2):
            summed = summed + arrived[source].astype(jnp.float32)
        lane_of = lax.div(token, 2 * rows) * rows + lax.rem(token, rows)
        here = jnp.logical_and(lane_of == source_lane, lax.rem(lax.div(token, rows), 2) == plane)
        total = total + jnp.dot(
            summed.astype(jnp.bfloat16), jnp.where(here, 1.0, 0.0).astype(jnp.bfloat16), preferred_element_type=jnp.float32
        )
    mixed[...] = total.astype(jnp.bfloat16)

    w_copy.wait_send()

    @pl.when(is_end)
    def _():
        for j in range(half_heads):
            for kind in (0, 1):
                key_cross(kind, j).wait_send()

    @pl.when(stays)
    def _():
        for kind in (0, 1):
            leg(kind).wait_send()
            second_leg(kind).wait_send()

    @pl.when(moves)
    def _():
        for kind in (0, 1):
            swap(kind).wait_send()
            direct(kind).wait_send()

    for x in range(NX):

        @pl.when(x != own_slot)
        def _():
            near_share(my_quad * quad + x).wait_send()

        @pl.when(inner)
        def _():
            far_share((1 - my_quad) * quad + x).wait_send()

        @pl.when(outer)
        def _():
            hop((1 - my_quad) * quad + x, x).wait_send()


def gather_scratch():
    return [
        pltpu.SemaphoreType.DMA((4 * RING,)),
        pltpu.SemaphoreType.DMA((4 * RING,)),
        pltpu.SemaphoreType.DMA((16,)),
        pltpu.SemaphoreType.DMA((16,)),
    ]


def on_device(
    heads,
    q_nope,
    q_rope,
    prefix_latent,
    prefix_rope,
    group_latent,
    group_rope,
    lengths,
    offset,
    w_uk,
    w_uv,
    w_out,
):
    rows, lat = prefix_latent.shape
    h_dev = w_uk.shape[0]
    q_rows = rows * h_dev
    width = 2 * lat + 128
    columns = w_out.shape[1]
    half = h_dev * VD // 2
    frequency = 10000.0 ** (-2.0 * (np.arange(128) % (ROPE // 2)) / ROPE)
    frequency = jnp.asarray(frequency[None, :], jnp.float32)

    tokens = rows * 2 * 2 * NX * NY
    block = rows * NY
    vmem = pl.BlockSpec(memory_space=pltpu.VMEM)
    smem = pl.BlockSpec(memory_space=pltpu.SMEM)
    anywhere = pl.BlockSpec(memory_space=pl.ANY)
    dma = pltpu.SemaphoreType.DMA
    mixed = pl.pallas_call(
        functools.partial(kernel, heads),
        out_shape=pltpu.VMEM((columns, tokens // heads), jnp.bfloat16),
        in_specs=[smem] * 2 + [anywhere] * 10,
        out_specs=vmem,
        scratch_shapes=[
            pltpu.VMEM((2, 2, NX, NY, 2, rows // 2, width), jnp.bfloat16),
            pltpu.VMEM((q_rows + 16, lat + 128), jnp.bfloat16),
            pltpu.VMEM((q_rows, lat + 128), jnp.bfloat16),
            pltpu.VMEM((q_rows, 1), jnp.float32),
            pltpu.VMEM((q_rows, 128), jnp.float32),
            pltpu.VMEM((q_rows, lat), jnp.float32),
            pltpu.VMEM((2, 2, NX, NY, 2, rows, half), jnp.bfloat16),
            pltpu.VMEM((2, rows, half), jnp.bfloat16),
            pltpu.VMEM((2, rows, half), jnp.bfloat16),
            pltpu.VMEM((2, columns, 2 * half), jnp.bfloat16),
            pltpu.VMEM((heads, columns, block), jnp.bfloat16),
            pltpu.VMEM((heads // 2 + 2, columns, block), jnp.bfloat16),
            pltpu.VMEM((NX, columns, block), jnp.bfloat16),
            pltpu.VMEM(q_nope.shape, jnp.bfloat16),
            pltpu.VMEM(q_rope.shape, jnp.bfloat16),
            pltpu.VMEM(prefix_rope.shape, jnp.bfloat16),
            pltpu.VMEM(group_rope.shape, jnp.bfloat16),
            pltpu.VMEM(w_uk.shape, jnp.bfloat16),
            pltpu.VMEM(w_uv.shape, jnp.bfloat16),
            pltpu.VMEM((1, 128), jnp.float32),
            dma((12,)),
        ]
        + gather_scratch()
        + [dma((heads,)), dma((2,))]
        + gather_scratch()
        + [dma((2,)), dma((2,)), dma((2,)), dma((2,)), dma((2,)), dma((2,))]
        + [dma(()), dma(()), dma((heads,)), dma((heads // 2 + 2,)), dma((NX,)), dma((NX,))],
        compiler_params=pltpu.CompilerParams(
            collective_id=0, has_side_effects=True, vmem_limit_bytes=60 * 1024 * 1024
        ),
        name="attention_and_output",
    )(
        lengths,
        offset,
        q_nope,
        q_rope,
        prefix_latent,
        prefix_rope,
        group_latent,
        group_rope,
        frequency,
        w_uk,
        w_uv,
        w_out.T,
    )
    return mixed.T


def solution(mesh):
    return jax.shard_map(
        functools.partial(on_device, mesh.shape["head"]),
        mesh=mesh,
        in_specs=(
            P("ctx", "head"),
            P("ctx", "head"),
            P("ctx", None),
            P("ctx", None),
            P("ctx", None),
            P("ctx", None),
            P("ctx"),
            P(),
            P("head", None, None),
            P("head", None, None),
            P("head", "ctx"),
        ),
        out_specs=P("head", "ctx"),
        check_vma=False,
    )
```

```python
import functools
import math

import jax
import jax.numpy as jnp
import numpy as np
from jax import lax
from jax.experimental import pallas as pl
from jax.experimental.pallas import tpu as pltpu
from jax.sharding import PartitionSpec as P

ROPE = 64
NOPE = 128
VD = 128
NX = 4
NY = 4
HIDDEN = -1e30
UNUSED = 1024.0
MESH = pl.DeviceIdType.MESH


class Place:
    def __init__(self, heads):
        c = lax.axis_index("ctx")
        self.heads = heads
        self.head = lax.axis_index("head")
        self.core = lax.rem(c, 2)
        self.y = lax.rem(lax.div(c, 2), NY)
        self.x = lax.rem(lax.div(c, 2 * NY), NX)
        self.zh = lax.div(c, 2 * NX * NY)

    def ctx(self, zh=None, x=None, y=None, core=None):
        zh = self.zh if zh is None else zh
        x = self.x if x is None else x
        y = self.y if y is None else y
        core = self.core if core is None else core
        return ((zh * NX + x) * NY + y) * 2 + core

    def along(self, axis, step):
        if axis == 0:
            return (self.ctx(x=lax.rem(self.x + step + NX, NX)), self.head)
        return (self.ctx(y=lax.rem(self.y + step + NY, NY)), self.head)

    def sibling(self):
        return (self.ctx(core=1 - self.core), self.head)

    def across(self, head=None):
        return (self.ctx(zh=1 - self.zh), self.head if head is None else head)


    def up(self, step):
        z = lax.rem(self.zh * self.heads + self.head + step + 2 * self.heads, 2 * self.heads)
        return lax.div(z, self.heads), lax.rem(z, self.heads)


def greet(devices):
    barrier = pltpu.get_barrier_semaphore()
    for device in devices:
        pl.semaphore_signal(barrier, inc=1, device_id=device, device_id_type=MESH)


def plane_peers(place):
    return [place.along(axis, step) for axis in (0, 1) for step in (1, -1, 2)] + [place.sibling()]


RING = 16
OFFSETS = (0, -1, 1, 2)
STEPS = (1, -1, 2)


class Gather:
    def __init__(self, place, buf, ring_send, ring_recv, pair_send, pair_recv):
        self.place = place
        self.buf = buf
        self.ring_send, self.ring_recv = ring_send, ring_recv
        self.pair_send, self.pair_recv = pair_send, pair_recv

    def zh(self, plane):
        return self.place.zh if plane == 0 else 1 - self.place.zh

    def cell(self, kind, plane, first, second):
        place = self.place
        dx, dy = (second, first) if kind == 0 else (first, second)
        x = lax.rem(place.x + dx + NX, NX)
        y = lax.rem(place.y + dy + NY, NY)
        return self.buf.at[kind, self.zh(plane), x, y, place.core]

    def line(self, kind, plane, second):
        place, zh = self.place, self.zh(plane)
        if kind == 0:
            return self.buf.at[kind, zh, lax.rem(place.x + second + NX, NX), pl.ds(0, NY), place.core]
        return self.buf.at[kind, zh, pl.ds(0, NX), lax.rem(place.y + second + NY, NY), place.core]

    def copy(self, ref, kind, plane, slot, device):
        index = (kind * 2 + plane) * RING + slot
        return pltpu.make_async_remote_copy(
            src_ref=ref,
            dst_ref=ref,
            send_sem=self.ring_send.at[index],
            recv_sem=self.ring_recv.at[index],
            device_id=device,
            device_id_type=MESH,
        )

    def first(self, kind, plane, i):
        return self.copy(self.cell(kind, plane, 0, 0), kind, plane, i, self.place.along(1 - kind, STEPS[i]))

    def second(self, kind, plane, o, direction):
        ref = self.cell(kind, plane, OFFSETS[o], 0)
        return self.copy(ref, kind, plane, 3 + 2 * o + direction, self.place.along(kind, STEPS[direction]))

    def relay(self, kind, plane, o):
        direction = o // 2
        ref = self.cell(kind, plane, OFFSETS[o], -STEPS[direction])
        return self.copy(ref, kind, plane, 11 + o, self.place.along(kind, STEPS[direction]))

    def pair(self, kind, plane, piece):
        ref = self.line(kind, plane, OFFSETS[piece])
        index = (kind * 2 + plane) * 4 + piece
        return pltpu.make_async_remote_copy(
            src_ref=ref,
            dst_ref=ref,
            send_sem=self.pair_send.at[index],
            recv_sem=self.pair_recv.at[index],
            device_id=self.place.sibling(),
            device_id_type=MESH,
        )

    def start(self, plane):
        for i in range(3):
            for kind in (0, 1):
                self.first(kind, plane, i).start()
        for direction in (0, 1):
            for kind in (0, 1):
                self.second(kind, plane, 0, direction).start()

    def spread(self, plane):
        for i in range(3):
            for kind in (0, 1):
                self.first(kind, plane, i).wait_recv()
                for direction in (0, 1):
                    self.second(kind, plane, 1 + i, direction).start()
        for kind in (0, 1):
            self.pair(kind, plane, 0).start()

    def hand_on(self, plane, offsets=(0, 1, 2, 3)):
        for o in offsets:
            for kind in (0, 1):
                for direction in (0, 1):
                    self.second(kind, plane, o, direction).wait_recv()
                self.relay(kind, plane, o).start()

    def hand_over(self, plane):
        for piece in (1, 2):
            for kind in (0, 1):
                self.pair(kind, plane, piece).start()

    def complete(self, plane):
        for kind in (0, 1):
            for o in range(4):
                self.relay(kind, plane, o).wait_recv()
            self.pair(kind, plane, 3).start()

    def from_sibling(self, plane, pieces=(0, 1, 2, 3)):
        for kind in (0, 1):
            for piece in pieces:
                self.pair(kind, plane, piece).wait_recv()

    def finish(self, plane):
        for kind in (0, 1):
            for i in range(3):
                self.first(kind, plane, i).wait_send()
            for o in range(4):
                for direction in (0, 1):
                    self.second(kind, plane, o, direction).wait_send()
                self.relay(kind, plane, o).wait_send()
                self.pair(kind, plane, o).wait_send()


def last_dims(a, b):
    return lax.dot_general(a, b, (((1,), (1,)), ((), ())), preferred_element_type=jnp.float32)


def cos_sin(angle):
    turns = jnp.floor(angle * (2.0 / math.pi) + 0.5)
    rest = ((angle - turns * 1.5703125) - turns * 4.837512969970703125e-4) - turns * 7.54978995489188216e-8
    square = rest * rest
    sine = ((-1.9515295891e-4 * square + 8.3321608736e-3) * square - 1.6666654611e-1) * square * rest + rest
    cosine = (2.443315711809948e-5 * square - 1.388731625493765e-3) * square + 4.166664568298827e-2
    cosine = cosine * square * square - 0.5 * square + 1.0
    quarter = jnp.bitwise_and(turns.astype(jnp.int32), 3)
    swap = jnp.bitwise_and(quarter, 1) == 1
    cos_part = jnp.where(swap, sine, cosine)
    sin_part = jnp.where(swap, cosine, sine)
    cos_part = jnp.where(jnp.logical_or(quarter == 1, quarter == 2), -cos_part, cos_part)
    sin_part = jnp.where(quarter >= 2, -sin_part, sin_part)
    return cos_part, sin_part


def kernel(
    heads,
    lengths,
    offset,
    q_nope_any,
    q_rope_any,
    prefix_latent,
    prefix_rope_any,
    group_latent,
    group_rope_any,
    frequency_any,
    w_uk_any,
    w_uv_any,
    w_out_any,
    mixed,
    keys,
    prefix_query,
    group_query,
    row_max,
    row_sum,
    accum,
    outs,
    staged,
    passing,
    w_out,
    shares,
    arrived,
    passed,
    own_part,
    q_nope,
    q_rope,
    prefix_rope,
    group_rope,
    w_uk,
    w_uv,
    frequency,
    load_sem,
    k_ring_send,
    k_ring_recv,
    k_pair_send,
    k_pair_recv,
    k_cross_send,
    k_cross_recv,
    o_ring_send,
    o_ring_recv,
    o_pair_send,
    o_pair_recv,
    leg_send,
    leg_recv,
    o_cross_send,
    o_cross_recv,
    swap_send,
    swap_recv,
    w_send,
    w_recv,
    share_send,
    share_recv,
    hop_send,
    hop_recv,
):
    place = Place(heads)
    rows, lat = prefix_latent.shape
    h_dev = w_uk.shape[0]
    part = rows // 2
    half = staged.shape[-1]
    half_heads = heads // 2
    me = place.ctx()
    own = (place.zh, place.x, place.y, place.core)
    odd = lax.rem(place.head, 2)
    paired = place.head + 1 - 2 * odd
    stays = place.core == odd
    moves = place.core != odd
    is_end = jnp.logical_or(place.head == 0, place.head == heads - 1)

    quarter = heads // 2
    legs = []
    for step in (quarter, -quarter):
        leg_zh, leg_head = place.up(step)
        legs.append((place.ctx(zh=leg_zh), leg_head))
    swap_device = (place.ctx(core=1 - place.core), paired)
    swap_across = (place.ctx(zh=1 - place.zh, core=1 - place.core), paired)
    others = [(me, lax.rem(place.head + j, heads)) for j in range(1, heads)]
    far_end = jnp.where(place.head < half_heads, heads - 1, 0)
    served = [jnp.where(place.head == 0, heads - 1 - j, j) for j in range(half_heads)]
    peers = plane_peers(place) + others + [place.across(far_end)]

    loads = [
        pltpu.make_async_copy(src, dst, load_sem.at[i])
        for i, (src, dst) in enumerate(
            (
                (prefix_latent.at[pl.ds(0, part)], keys.at[(0,) + own + (slice(None), pl.ds(0, lat))]),
                (group_latent.at[pl.ds(0, part)], keys.at[(0,) + own + (slice(None), pl.ds(lat + 128, lat))]),
                (q_nope_any, q_nope),
                (q_rope_any, q_rope),
                (prefix_rope_any, prefix_rope),
                (group_rope_any, group_rope),
                (w_uk_any, w_uk),
                (w_uv_any, w_uv),
                (w_out_any, w_out.at[odd]),
                (frequency_any, frequency),
                (prefix_latent.at[pl.ds(part, part)], keys.at[(1,) + own + (slice(None), pl.ds(0, lat))]),
                (group_latent.at[pl.ds(part, part)], keys.at[(1,) + own + (slice(None), pl.ds(lat + 128, lat))]),
            )
        )
    ]
    early = (9, 4, 5, 0, 1, 10, 11)
    greet(peers[:7])
    for i in early:
        loads[i].start()
    greet(peers[7:])

    @pl.when(stays)
    def _():
        greet(legs)

    @pl.when(moves)
    def _():
        greet([swap_device, swap_across])

    @pl.when(is_end)
    def _():
        greet([place.across(head) for head in served])

    for i, load in enumerate(loads):
        if i not in early:
            load.start()
    lane = lax.broadcasted_iota(jnp.int32, (rows, 128), 1)
    row = lax.broadcasted_iota(jnp.int32, (rows, 128), 0)
    for i in (9, 4, 5):
        loads[i].wait()
    positions = (offset[0] + me * rows + row).astype(jnp.float32)
    cos_part, sin_part = cos_sin(positions * frequency[...])
    first_half = lax.rem(lane, ROPE) < ROPE // 2
    sin_part = jnp.where(first_half, -sin_part, sin_part)

    def turn(tile):
        swapped = jnp.where(first_half, pltpu.roll(tile, 128 - ROPE // 2, 1), pltpu.roll(tile, ROPE // 2, 1))
        return tile * cos_part + swapped * sin_part

    def twice(ref):
        value = ref[...].astype(jnp.float32)
        return jnp.concatenate([value, value], axis=1)

    unused = jnp.where(lane == 0, UNUSED, 0.0)
    ropes = jnp.where(row < lengths[0], twice(prefix_rope), unused)
    ropes = jnp.where(lane < ROPE, ropes, turn(twice(group_rope))).astype(jnp.bfloat16)
    for kind in (0, 1):
        keys[(kind,) + own + (slice(None), pl.ds(lat, 128))] = ropes[kind * part : (kind + 1) * part]
    for i in (0, 1, 10, 11):
        loads[i].wait()

    pl.semaphore_wait(pltpu.get_barrier_semaphore(), len(peers) + 2 + half_heads * is_end.astype(jnp.int32))

    gather = Gather(place, keys, k_ring_send, k_ring_recv, k_pair_send, k_pair_recv)

    def key_cross(kind, j):
        ref = keys.at[(kind,) + own]
        return pltpu.make_async_remote_copy(
            src_ref=ref,
            dst_ref=ref,
            send_sem=k_cross_send.at[kind * half_heads + j],
            recv_sem=k_cross_recv.at[kind],
            device_id=place.across(served[j]),
            device_id_type=MESH,
        )

    @pl.when(is_end)
    def _():
        for j in reversed(range(half_heads)):
            for kind in (0, 1):
                key_cross(kind, j).start()

    gather.start(0)

    scale = (NOPE + ROPE) ** -0.5 * math.log2(math.e)

    q_rows = h_dev * rows
    loads[2].wait()
    loads[3].wait()
    loads[6].wait()
    mark = jnp.logical_and(lane[:16] == 0, row[:16] == 0)
    prefix_query[pl.ds(q_rows, 16), pl.ds(0, lat)] = jnp.zeros((16, lat), jnp.bfloat16)
    prefix_query[pl.ds(q_rows, 16), pl.ds(lat, 128)] = jnp.where(mark, 1.0, 0.0).astype(jnp.bfloat16)
    for pair in range(h_dev // 2):
        turned = turn(q_rope[:, pair * 128 : (pair + 1) * 128].astype(jnp.float32)) * scale
        other = pltpu.roll(turned, ROPE, 1)
        for side in (0, 1):
            head = 2 * pair + side
            at = pl.ds(head * rows, rows)
            low_part, high_part = (turned, other) if side == 0 else (other, turned)
            prefix_query[at, pl.ds(lat, 128)] = jnp.where(lane < ROPE, low_part, 0.0).astype(jnp.bfloat16)
            group_query[at, pl.ds(0, 128)] = jnp.where(lane >= ROPE, high_part, 0.0).astype(jnp.bfloat16)
            latent = jnp.dot(
                q_nope[:, head * NOPE : (head + 1) * NOPE], w_uk[head], preferred_element_type=jnp.float32
            )
            latent = (latent * scale).astype(jnp.bfloat16)
            prefix_query[at, pl.ds(0, lat)] = latent
            group_query[at, pl.ds(128, lat)] = latent

    row_max[...] = jnp.full(row_max.shape, HIDDEN, jnp.float32)
    row_sum[...] = jnp.zeros(row_sum.shape, jnp.float32)
    accum[...] = jnp.zeros(accum.shape, jnp.float32)
    my_token = me * rows + lax.rem(lax.broadcasted_iota(jnp.int32, (q_rows, 1), 0), rows)

    def attend(plane, lines):
        zh = gather.zh(plane)
        span = NY * part
        index = lax.broadcasted_iota(jnp.int32, (1, span * len(lines)), 1)
        inside = lax.rem(index, span)
        key_token = jnp.zeros(index.shape, jnp.int32)
        blocks = []
        for i, (kind, step, sibling) in enumerate(lines):
            core = 1 - place.core if sibling else place.core
            if kind == 0:
                x = lax.rem(place.x + step + NX, NX)
                blocks.append(keys[0, zh, x, :, core])
                first, stride = place.ctx(zh=zh, x=x, y=0, core=core), 2
            else:
                y = lax.rem(place.y + step + NY, NY)
                blocks.append(keys[1, zh, :, y, core])
                first, stride = place.ctx(zh=zh, x=0, y=y, core=core), 2 * NY
            token = (first + stride * lax.div(inside, part)) * rows + kind * part + lax.rem(inside, part)
            key_token = jnp.where(lax.div(index, span) == i, token, key_token)
        rows_in = jnp.concatenate([block.reshape(span, block.shape[-1]) for block in blocks], axis=0)
        prefix_all = last_dims(prefix_query[...], rows_in[:, : lat + 128])
        hidden = prefix_all[q_rows : q_rows + 1] > UNUSED / 2
        prefix_scores = jnp.where(hidden, HIDDEN, prefix_all[:q_rows])
        group_scores = last_dims(group_query[...], rows_in[:, lat:])
        group_scores = jnp.where(key_token <= my_token, group_scores, HIDDEN)
        old_max = row_max[...]
        new_max = jnp.max(jnp.maximum(prefix_scores, group_scores), axis=1, keepdims=True)
        new_max = jnp.maximum(old_max, new_max)
        prefix_weights = jnp.exp2(prefix_scores - new_max)
        group_weights = jnp.exp2(group_scores - new_max)
        factor = jnp.exp2(old_max - new_max)
        row_max[...] = new_max
        weights = prefix_weights + group_weights
        lanes = weights[:, :128]
        for j in range(1, weights.shape[1] // 128):
            lanes = lanes + weights[:, j * 128 : (j + 1) * 128]
        row_sum[...] = row_sum[...] * factor + lanes
        taken = jnp.dot(prefix_weights.astype(jnp.bfloat16), rows_in[:, :lat], preferred_element_type=jnp.float32)
        taken = taken + jnp.dot(
            group_weights.astype(jnp.bfloat16), rows_in[:, lat + 128 :], preferred_element_type=jnp.float32
        )
        accum[...] = accum[...] * factor + taken

    w_copy = pltpu.make_async_remote_copy(
        src_ref=w_out_any,
        dst_ref=w_out.at[odd],
        send_sem=w_send,
        recv_sem=w_recv,
        device_id=(me, paired),
        device_id_type=MESH,
    )

    def pick(steps, sibling):
        return [(kind, step, sibling) for kind in (0, 1) for step in steps]

    gather.spread(0)
    attend(0, pick((0,), False))
    gather.hand_on(0)
    gather.hand_over(0)
    for kind in (0, 1):
        key_cross(kind, 0).wait_recv()
    gather.start(1)
    w_copy.start()
    attend(0, pick((-1, 1), False))
    gather.complete(0)
    gather.spread(1)
    gather.from_sibling(0, (0, 1, 2))
    attend(0, pick((0, -1), True))
    gather.hand_on(1, (0,))
    attend(0, [(kind, 2, False) for kind in (0, 1)] + [(kind, 1, True) for kind in (0, 1)])
    gather.hand_on(1, (1, 2))
    gather.hand_on(1, (3,))
    gather.hand_over(1)
    attend(1, pick((0, -1, 1), False))
    gather.complete(1)
    gather.from_sibling(0, (3,))
    gather.from_sibling(1, (0, 1, 2))
    attend(1, pick((0, -1, 1), True))
    attend(0, pick((2,), True))
    gather.from_sibling(1, (3,))
    attend(1, pick((2,), False) + pick((2,), True))

    loads[7].wait()
    latent_out = (accum[...] / jnp.sum(row_sum[...], axis=1, keepdims=True)).astype(jnp.bfloat16)
    per_kind = half // VD

    def head_outputs(kind):
        for head in range(kind * per_kind, (kind + 1) * per_kind):
            staged[kind, :, pl.ds((head % per_kind) * VD, VD)] = jnp.dot(
                latent_out[head * rows : (head + 1) * rows], w_uv[head], preferred_element_type=jnp.float32
            ).astype(jnp.bfloat16)

    slot = (place.x, place.y, place.core)
    new_slot = (place.x, place.y, 1 - place.core)

    def leg(kind):
        return pltpu.make_async_remote_copy(
            src_ref=staged.at[kind],
            dst_ref=passing.at[kind],
            send_sem=leg_send.at[kind],
            recv_sem=leg_recv.at[kind],
            device_id=legs[kind],
            device_id_type=MESH,
        )

    def second_leg(kind):
        end_zh = place.up(quarter if kind == 0 else -quarter)[0]
        return pltpu.make_async_remote_copy(
            src_ref=passing.at[kind],
            dst_ref=outs.at[(kind, 1 - end_zh) + slot],
            send_sem=o_cross_send.at[kind],
            recv_sem=o_cross_recv.at[kind],
            device_id=legs[kind],
            device_id_type=MESH,
        )

    def swap(kind):
        return pltpu.make_async_remote_copy(
            src_ref=staged.at[kind],
            dst_ref=outs.at[(kind, place.zh) + new_slot],
            send_sem=swap_send.at[kind],
            recv_sem=swap_recv.at[kind],
            device_id=swap_device,
            device_id_type=MESH,
        )

    def direct(kind):
        return pltpu.make_async_remote_copy(
            src_ref=staged.at[kind],
            dst_ref=outs.at[(kind, place.zh) + new_slot],
            send_sem=o_cross_send.at[kind],
            recv_sem=o_cross_recv.at[kind],
            device_id=swap_across,
            device_id_type=MESH,
        )

    for kind in (0, 1):
        head_outputs(kind)

        @pl.when(stays)
        def _():
            leg(kind).start()
            outs[(kind, place.zh) + slot] = staged[kind]

        @pl.when(moves)
        def _():
            swap(kind).start()
            direct(kind).start()

    @pl.when(moves)
    def _():
        for kind in (0, 1):
            swap(kind).wait_recv()

    spread = Gather(place, outs, o_ring_send, o_ring_recv, o_pair_send, o_pair_recv)
    spread.start(0)
    gather.finish(0)

    @pl.when(stays)
    def _():
        for kind in (0, 1):
            leg(kind).wait_recv()
            second_leg(kind).start()

    block = shares.shape[-1]

    quad = heads // 2
    my_quad = lax.div(place.head, quad)
    inner = jnp.logical_and(place.head >= quad // 2, place.head < quad + quad // 2)
    outer = jnp.logical_not(inner)

    def share(target, slot):
        return pltpu.make_async_remote_copy(
            src_ref=shares.at[target],
            dst_ref=arrived.at[slot],
            send_sem=share_send.at[target],
            recv_sem=share_recv.at[slot],
            device_id=(me, target),
            device_id_type=MESH,
        )

    def near_share(target):
        return share(target, lax.rem(place.head, quad))

    def far_share(target):
        return share(target, quad + lax.rem(place.head, 2))

    def hop(target, x):
        return pltpu.make_async_remote_copy(
            src_ref=shares.at[target],
            dst_ref=passed.at[x],
            send_sem=hop_send.at[x],
            recv_sem=hop_recv.at[x],
            device_id=(me, jnp.where(place.head < quad, place.head + 2, place.head - 2)),
            device_id_type=MESH,
        )

    def part_share(zh, plane, first, count):
        total = jnp.zeros((count * block, w_out.shape[1]), jnp.float32)
        for kind in (0, 1):
            tokens = outs[kind, zh, pl.ds(first, count), :, plane].reshape(count * block, half)
            total = total + last_dims(tokens, w_out[plane, :, kind * half : (kind + 1) * half])
        return total

    def send_shares(plane):
        zh = spread.zh(plane)
        own_part[...] = part_share(zh, place.core, 0, NX)
        spread.from_sibling(plane)
        for x in range(NX):
            target = zh * NX + x
            if x % 2 == 0:
                total = part_share(zh, 1 - place.core, x, 2)
                total = total + own_part[x * block : (x + 2) * block]
            shares[target] = total[x % 2 * block : (x % 2 + 1) * block].T.astype(jnp.bfloat16)

            @pl.when(jnp.logical_and(my_quad == zh, target != place.head))
            def _():
                near_share(target).start()

            @pl.when(jnp.logical_and(my_quad != zh, outer))
            def _():
                hop(target, x).start()

    def forward_shares(plane):
        zh = spread.zh(plane)

        @pl.when(jnp.logical_and(my_quad != zh, inner))
        def _():
            for x in range(NX):
                target = zh * NX + x
                hop(target, x).wait_recv()
                total = shares[target].astype(jnp.float32) + passed[x].astype(jnp.float32)
                shares[target] = total.astype(jnp.bfloat16)
                far_share(target).start()

    spread.spread(0)
    gather.finish(1)
    spread.hand_on(0)
    spread.hand_over(0)
    for kind in (0, 1):
        direct(kind).wait_recv()
    spread.start(1)
    spread.complete(0)
    spread.spread(1)
    loads[8].wait()
    w_copy.wait_recv()
    send_shares(0)
    spread.hand_on(1, (0, 1))
    spread.hand_on(1, (2, 3))
    spread.hand_over(1)
    forward_shares(0)
    spread.complete(1)
    send_shares(1)
    forward_shares(1)
    spread.finish(0)
    spread.finish(1)

    own_slot = lax.rem(place.head, quad)
    arrived[own_slot] = shares[place.head]
    for source in range(quad):

        @pl.when(source != own_slot)
        def _():
            share(place.head, source).wait_recv()

    for source in (quad, quad + 1):
        share(place.head, source).wait_recv()

    total = jnp.zeros(mixed.shape, jnp.float32)
    source_lane = lax.broadcasted_iota(jnp.int32, (block, mixed.shape[1]), 0)
    token = lax.broadcasted_iota(jnp.int32, (block, mixed.shape[1]), 1)
    for plane in (0, 1):
        summed = jnp.zeros(shares.shape[1:], jnp.float32)
        for source in range(plane, quad + 2, 2):
            summed = summed + arrived[source].astype(jnp.float32)
        lane_of = lax.div(token, 2 * rows) * rows + lax.rem(token, rows)
        here = jnp.logical_and(lane_of == source_lane, lax.rem(lax.div(token, rows), 2) == plane)
        total = total + jnp.dot(
            summed.astype(jnp.bfloat16), jnp.where(here, 1.0, 0.0).astype(jnp.bfloat16), preferred_element_type=jnp.float32
        )
    mixed[...] = total.astype(jnp.bfloat16)

    w_copy.wait_send()

    @pl.when(is_end)
    def _():
        for j in range(half_heads):
            for kind in (0, 1):
                key_cross(kind, j).wait_send()

    @pl.when(stays)
    def _():
        for kind in (0, 1):
            leg(kind).wait_send()
            second_leg(kind).wait_send()

    @pl.when(moves)
    def _():
        for kind in (0, 1):
            swap(kind).wait_send()
            direct(kind).wait_send()

    for x in range(NX):

        @pl.when(x != own_slot)
        def _():
            near_share(my_quad * quad + x).wait_send()

        @pl.when(inner)
        def _():
            far_share((1 - my_quad) * quad + x).wait_send()

        @pl.when(outer)
        def _():
            hop((1 - my_quad) * quad + x, x).wait_send()


def gather_scratch():
    return [
        pltpu.SemaphoreType.DMA((4 * RING,)),
        pltpu.SemaphoreType.DMA((4 * RING,)),
        pltpu.SemaphoreType.DMA((16,)),
        pltpu.SemaphoreType.DMA((16,)),
    ]


def on_device(
    heads,
    q_nope,
    q_rope,
    prefix_latent,
    prefix_rope,
    group_latent,
    group_rope,
    lengths,
    offset,
    w_uk,
    w_uv,
    w_out,
):
    rows, lat = prefix_latent.shape
    h_dev = w_uk.shape[0]
    q_rows = rows * h_dev
    width = 2 * lat + 128
    columns = w_out.shape[1]
    half = h_dev * VD // 2
    frequency = 10000.0 ** (-2.0 * (np.arange(128) % (ROPE // 2)) / ROPE)
    frequency = jnp.asarray(frequency[None, :], jnp.float32)

    tokens = rows * 2 * 2 * NX * NY
    block = rows * NY
    vmem = pl.BlockSpec(memory_space=pltpu.VMEM)
    smem = pl.BlockSpec(memory_space=pltpu.SMEM)
    anywhere = pl.BlockSpec(memory_space=pl.ANY)
    dma = pltpu.SemaphoreType.DMA
    mixed = pl.pallas_call(
        functools.partial(kernel, heads),
        out_shape=pltpu.VMEM((columns, tokens // heads), jnp.bfloat16),
        in_specs=[smem] * 2 + [anywhere] * 10,
        out_specs=vmem,
        scratch_shapes=[
            pltpu.VMEM((2, 2, NX, NY, 2, rows // 2, width), jnp.bfloat16),
            pltpu.VMEM((q_rows + 16, lat + 128), jnp.bfloat16),
            pltpu.VMEM((q_rows, lat + 128), jnp.bfloat16),
            pltpu.VMEM((q_rows, 1), jnp.float32),
            pltpu.VMEM((q_rows, 128), jnp.float32),
            pltpu.VMEM((q_rows, lat), jnp.float32),
            pltpu.VMEM((2, 2, NX, NY, 2, rows, half), jnp.bfloat16),
            pltpu.VMEM((2, rows, half), jnp.bfloat16),
            pltpu.VMEM((2, rows, half), jnp.bfloat16),
            pltpu.VMEM((2, columns, 2 * half), jnp.bfloat16),
            pltpu.VMEM((heads, columns, block), jnp.bfloat16),
            pltpu.VMEM((heads // 2 + 2, columns, block), jnp.bfloat16),
            pltpu.VMEM((NX, columns, block), jnp.bfloat16),
            pltpu.VMEM((NX * block, columns), jnp.float32),
            pltpu.VMEM(q_nope.shape, jnp.bfloat16),
            pltpu.VMEM(q_rope.shape, jnp.bfloat16),
            pltpu.VMEM(prefix_rope.shape, jnp.bfloat16),
            pltpu.VMEM(group_rope.shape, jnp.bfloat16),
            pltpu.VMEM(w_uk.shape, jnp.bfloat16),
            pltpu.VMEM(w_uv.shape, jnp.bfloat16),
            pltpu.VMEM((1, 128), jnp.float32),
            dma((12,)),
        ]
        + gather_scratch()
        + [dma((heads,)), dma((2,))]
        + gather_scratch()
        + [dma((2,)), dma((2,)), dma((2,)), dma((2,)), dma((2,)), dma((2,))]
        + [dma(()), dma(()), dma((heads,)), dma((heads // 2 + 2,)), dma((NX,)), dma((NX,))],
        compiler_params=pltpu.CompilerParams(
            collective_id=0, has_side_effects=True, vmem_limit_bytes=60 * 1024 * 1024
        ),
        name="attention_and_output",
    )(
        lengths,
        offset,
        q_nope,
        q_rope,
        prefix_latent,
        prefix_rope,
        group_latent,
        group_rope,
        frequency,
        w_uk,
        w_uv,
        w_out.T,
    )
    return mixed.T


def solution(mesh):
    return jax.shard_map(
        functools.partial(on_device, mesh.shape["head"]),
        mesh=mesh,
        in_specs=(
            P("ctx", "head"),
            P("ctx", "head"),
            P("ctx", None),
            P("ctx", None),
            P("ctx", None),
            P("ctx", None),
            P("ctx"),
            P(),
            P("head", None, None),
            P("head", None, None),
            P("head", "ctx"),
        ),
        out_specs=P("head", "ctx"),
        check_vma=False,
    )
```

```python
import functools
import math

import jax
import jax.numpy as jnp
import numpy as np
from jax import lax
from jax.experimental import pallas as pl
from jax.experimental.pallas import tpu as pltpu
from jax.sharding import PartitionSpec as P

ROPE = 64
NOPE = 128
VD = 128
NX = 4
NY = 4
HIDDEN = -1e30
UNUSED = 1024.0
MESH = pl.DeviceIdType.MESH


class Place:
    def __init__(self, heads):
        c = lax.axis_index("ctx")
        self.heads = heads
        self.head = lax.axis_index("head")
        self.core = lax.rem(c, 2)
        self.y = lax.rem(lax.div(c, 2), NY)
        self.x = lax.rem(lax.div(c, 2 * NY), NX)
        self.zh = lax.div(c, 2 * NX * NY)

    def ctx(self, zh=None, x=None, y=None, core=None):
        zh = self.zh if zh is None else zh
        x = self.x if x is None else x
        y = self.y if y is None else y
        core = self.core if core is None else core
        return ((zh * NX + x) * NY + y) * 2 + core

    def along(self, axis, step):
        if axis == 0:
            return (self.ctx(x=lax.rem(self.x + step + NX, NX)), self.head)
        return (self.ctx(y=lax.rem(self.y + step + NY, NY)), self.head)

    def sibling(self):
        return (self.ctx(core=1 - self.core), self.head)

    def across(self, head=None):
        return (self.ctx(zh=1 - self.zh), self.head if head is None else head)


    def up(self, step):
        z = lax.rem(self.zh * self.heads + self.head + step + 2 * self.heads, 2 * self.heads)
        return lax.div(z, self.heads), lax.rem(z, self.heads)


def greet(devices):
    barrier = pltpu.get_barrier_semaphore()
    for device in devices:
        pl.semaphore_signal(barrier, inc=1, device_id=device, device_id_type=MESH)


def plane_peers(place):
    return [place.along(axis, step) for axis in (0, 1) for step in (1, -1, 2)] + [place.sibling()]


RING = 16
OFFSETS = (0, -1, 1, 2)
STEPS = (1, -1, 2)


class Gather:
    def __init__(self, place, buf, ring_send, ring_recv, pair_send, pair_recv):
        self.place = place
        self.buf = buf
        self.ring_send, self.ring_recv = ring_send, ring_recv
        self.pair_send, self.pair_recv = pair_send, pair_recv

    def zh(self, plane):
        return self.place.zh if plane == 0 else 1 - self.place.zh

    def cell(self, kind, plane, first, second):
        place = self.place
        dx, dy = (second, first) if kind == 0 else (first, second)
        x = lax.rem(place.x + dx + NX, NX)
        y = lax.rem(place.y + dy + NY, NY)
        return self.buf.at[kind, self.zh(plane), x, y, place.core]

    def line(self, kind, plane, second):
        place, zh = self.place, self.zh(plane)
        if kind == 0:
            return self.buf.at[kind, zh, lax.rem(place.x + second + NX, NX), pl.ds(0, NY), place.core]
        return self.buf.at[kind, zh, pl.ds(0, NX), lax.rem(place.y + second + NY, NY), place.core]

    def copy(self, ref, kind, plane, slot, device):
        index = (kind * 2 + plane) * RING + slot
        return pltpu.make_async_remote_copy(
            src_ref=ref,
            dst_ref=ref,
            send_sem=self.ring_send.at[index],
            recv_sem=self.ring_recv.at[index],
            device_id=device,
            device_id_type=MESH,
        )

    def first(self, kind, plane, i):
        return self.copy(self.cell(kind, plane, 0, 0), kind, plane, i, self.place.along(1 - kind, STEPS[i]))

    def second(self, kind, plane, o, direction):
        ref = self.cell(kind, plane, OFFSETS[o], 0)
        return self.copy(ref, kind, plane, 3 + 2 * o + direction, self.place.along(kind, STEPS[direction]))

    def relay(self, kind, plane, o):
        direction = o // 2
        ref = self.cell(kind, plane, OFFSETS[o], -STEPS[direction])
        return self.copy(ref, kind, plane, 11 + o, self.place.along(kind, STEPS[direction]))

    def pair(self, kind, plane, piece):
        ref = self.line(kind, plane, OFFSETS[piece])
        index = (kind * 2 + plane) * 4 + piece
        return pltpu.make_async_remote_copy(
            src_ref=ref,
            dst_ref=ref,
            send_sem=self.pair_send.at[index],
            recv_sem=self.pair_recv.at[index],
            device_id=self.place.sibling(),
            device_id_type=MESH,
        )

    def start(self, plane):
        for i in range(3):
            for kind in (0, 1):
                self.first(kind, plane, i).start()
        for direction in (0, 1):
            for kind in (0, 1):
                self.second(kind, plane, 0, direction).start()

    def spread(self, plane):
        for i in range(3):
            for kind in (0, 1):
                self.first(kind, plane, i).wait_recv()
                for direction in (0, 1):
                    self.second(kind, plane, 1 + i, direction).start()
        for kind in (0, 1):
            self.pair(kind, plane, 0).start()

    def hand_on(self, plane, offsets=(0, 1, 2, 3)):
        for o in offsets:
            for kind in (0, 1):
                for direction in (0, 1):
                    self.second(kind, plane, o, direction).wait_recv()
                self.relay(kind, plane, o).start()

    def hand_over(self, plane):
        for piece in (1, 2):
            for kind in (0, 1):
                self.pair(kind, plane, piece).start()

    def complete(self, plane):
        for kind in (0, 1):
            for o in range(4):
                self.relay(kind, plane, o).wait_recv()
            self.pair(kind, plane, 3).start()

    def from_sibling(self, plane, pieces=(0, 1, 2, 3)):
        for kind in (0, 1):
            for piece in pieces:
                self.pair(kind, plane, piece).wait_recv()

    def finish(self, plane):
        for kind in (0, 1):
            for i in range(3):
                self.first(kind, plane, i).wait_send()
            for o in range(4):
                for direction in (0, 1):
                    self.second(kind, plane, o, direction).wait_send()
                self.relay(kind, plane, o).wait_send()
                self.pair(kind, plane, o).wait_send()


def last_dims(a, b):
    return lax.dot_general(a, b, (((1,), (1,)), ((), ())), preferred_element_type=jnp.float32)


def cos_sin(angle):
    turns = jnp.floor(angle * (2.0 / math.pi) + 0.5)
    rest = ((angle - turns * 1.5703125) - turns * 4.837512969970703125e-4) - turns * 7.54978995489188216e-8
    square = rest * rest
    sine = ((-1.9515295891e-4 * square + 8.3321608736e-3) * square - 1.6666654611e-1) * square * rest + rest
    cosine = (2.443315711809948e-5 * square - 1.388731625493765e-3) * square + 4.166664568298827e-2
    cosine = cosine * square * square - 0.5 * square + 1.0
    quarter = jnp.bitwise_and(turns.astype(jnp.int32), 3)
    swap = jnp.bitwise_and(quarter, 1) == 1
    cos_part = jnp.where(swap, sine, cosine)
    sin_part = jnp.where(swap, cosine, sine)
    cos_part = jnp.where(jnp.logical_or(quarter == 1, quarter == 2), -cos_part, cos_part)
    sin_part = jnp.where(quarter >= 2, -sin_part, sin_part)
    return cos_part, sin_part


def kernel(
    heads,
    lengths,
    offset,
    q_nope_any,
    q_rope_any,
    prefix_latent,
    prefix_rope_any,
    group_latent,
    group_rope_any,
    frequency_any,
    w_uk_any,
    w_uv_any,
    w_out_any,
    mixed,
    keys,
    prefix_query,
    group_query,
    row_max,
    row_sum,
    accum,
    outs,
    staged,
    passing,
    w_out,
    shares,
    arrived,
    passed,
    own_part,
    q_nope,
    q_rope,
    prefix_rope,
    group_rope,
    w_uk,
    w_uv,
    frequency,
    load_sem,
    k_ring_send,
    k_ring_recv,
    k_pair_send,
    k_pair_recv,
    k_cross_send,
    k_cross_recv,
    o_ring_send,
    o_ring_recv,
    o_pair_send,
    o_pair_recv,
    leg_send,
    leg_recv,
    o_cross_send,
    o_cross_recv,
    swap_send,
    swap_recv,
    w_send,
    w_recv,
    share_send,
    share_recv,
    hop_send,
    hop_recv,
):
    place = Place(heads)
    rows, lat = prefix_latent.shape
    h_dev = w_uk.shape[0]
    part = rows // 2
    half = staged.shape[-1]
    half_heads = heads // 2
    me = place.ctx()
    own = (place.zh, place.x, place.y, place.core)
    odd = lax.rem(place.head, 2)
    paired = place.head + 1 - 2 * odd
    stays = place.core == odd
    moves = place.core != odd
    is_end = jnp.logical_or(place.head == 0, place.head == heads - 1)

    quarter = heads // 2
    legs = []
    for step in (quarter, -quarter):
        leg_zh, leg_head = place.up(step)
        legs.append((place.ctx(zh=leg_zh), leg_head))
    swap_device = (place.ctx(core=1 - place.core), paired)
    swap_across = (place.ctx(zh=1 - place.zh, core=1 - place.core), paired)
    others = [(me, lax.rem(place.head + j, heads)) for j in range(1, heads)]
    far_end = jnp.where(place.head < half_heads, heads - 1, 0)
    served = [jnp.where(place.head == 0, heads - 1 - j, j) for j in range(half_heads)]
    peers = plane_peers(place) + others + [place.across(far_end)]

    loads = [
        pltpu.make_async_copy(src, dst, load_sem.at[i])
        for i, (src, dst) in enumerate(
            (
                (prefix_latent.at[pl.ds(0, part)], keys.at[(0,) + own + (slice(None), pl.ds(0, lat))]),
                (group_latent.at[pl.ds(0, part)], keys.at[(0,) + own + (slice(None), pl.ds(lat + 128, lat))]),
                (q_nope_any, q_nope),
                (q_rope_any, q_rope),
                (prefix_rope_any, prefix_rope),
                (group_rope_any, group_rope),
                (w_uk_any, w_uk),
                (w_uv_any, w_uv),
                (w_out_any, w_out.at[odd]),
                (frequency_any, frequency),
                (prefix_latent.at[pl.ds(part, part)], keys.at[(1,) + own + (slice(None), pl.ds(0, lat))]),
                (group_latent.at[pl.ds(part, part)], keys.at[(1,) + own + (slice(None), pl.ds(lat + 128, lat))]),
            )
        )
    ]
    early = (9, 4, 5, 0, 1, 10, 11)
    greet(peers[:7])
    for i in early:
        loads[i].start()
    greet(peers[7:])

    @pl.when(stays)
    def _():
        greet(legs)

    @pl.when(moves)
    def _():
        greet([swap_device, swap_across])

    @pl.when(is_end)
    def _():
        greet([place.across(head) for head in served])

    for i, load in enumerate(loads):
        if i not in early:
            load.start()
    lane = lax.broadcasted_iota(jnp.int32, (rows, 128), 1)
    row = lax.broadcasted_iota(jnp.int32, (rows, 128), 0)
    for i in (9, 4, 5):
        loads[i].wait()
    positions = (offset[0] + me * rows + row).astype(jnp.float32)
    cos_part, sin_part = cos_sin(positions * frequency[...])
    first_half = lax.rem(lane, ROPE) < ROPE // 2
    sin_part = jnp.where(first_half, -sin_part, sin_part)

    def turn(tile):
        swapped = jnp.where(first_half, pltpu.roll(tile, 128 - ROPE // 2, 1), pltpu.roll(tile, ROPE // 2, 1))
        return tile * cos_part + swapped * sin_part

    def twice(ref):
        value = ref[...].astype(jnp.float32)
        return jnp.concatenate([value, value], axis=1)

    unused = jnp.where(lane == 0, UNUSED, 0.0)
    ropes = jnp.where(row < lengths[0], twice(prefix_rope), unused)
    ropes = jnp.where(lane < ROPE, ropes, turn(twice(group_rope))).astype(jnp.bfloat16)
    for kind in (0, 1):
        keys[(kind,) + own + (slice(None), pl.ds(lat, 128))] = ropes[kind * part : (kind + 1) * part]
    for i in (0, 1, 10, 11):
        loads[i].wait()

    pl.semaphore_wait(pltpu.get_barrier_semaphore(), len(peers) + 2 + half_heads * is_end.astype(jnp.int32))

    gather = Gather(place, keys, k_ring_send, k_ring_recv, k_pair_send, k_pair_recv)

    def key_cross(kind, j):
        ref = keys.at[(kind,) + own]
        return pltpu.make_async_remote_copy(
            src_ref=ref,
            dst_ref=ref,
            send_sem=k_cross_send.at[kind * half_heads + j],
            recv_sem=k_cross_recv.at[kind],
            device_id=place.across(served[j]),
            device_id_type=MESH,
        )

    @pl.when(is_end)
    def _():
        for j in reversed(range(half_heads)):
            for kind in (0, 1):
                key_cross(kind, j).start()

    gather.start(0)

    scale = (NOPE + ROPE) ** -0.5 * math.log2(math.e)

    q_rows = h_dev * rows
    loads[2].wait()
    loads[3].wait()
    loads[6].wait()
    mark = jnp.logical_and(lane[:16] == 0, row[:16] == 0)
    prefix_query[pl.ds(q_rows, 16), pl.ds(0, lat)] = jnp.zeros((16, lat), jnp.bfloat16)
    prefix_query[pl.ds(q_rows, 16), pl.ds(lat, 128)] = jnp.where(mark, 1.0, 0.0).astype(jnp.bfloat16)
    for pair in range(h_dev // 2):
        turned = turn(q_rope[:, pair * 128 : (pair + 1) * 128].astype(jnp.float32)) * scale
        other = pltpu.roll(turned, ROPE, 1)
        for side in (0, 1):
            head = 2 * pair + side
            at = pl.ds(head * rows, rows)
            low_part, high_part = (turned, other) if side == 0 else (other, turned)
            prefix_query[at, pl.ds(lat, 128)] = jnp.where(lane < ROPE, low_part, 0.0).astype(jnp.bfloat16)
            group_query[at, pl.ds(0, 128)] = jnp.where(lane >= ROPE, high_part, 0.0).astype(jnp.bfloat16)
            latent = jnp.dot(
                q_nope[:, head * NOPE : (head + 1) * NOPE], w_uk[head], preferred_element_type=jnp.float32
            )
            latent = (latent * scale).astype(jnp.bfloat16)
            prefix_query[at, pl.ds(0, lat)] = latent
            group_query[at, pl.ds(128, lat)] = latent

    row_max[...] = jnp.full(row_max.shape, HIDDEN, jnp.float32)
    row_sum[...] = jnp.zeros(row_sum.shape, jnp.float32)
    accum[...] = jnp.zeros(accum.shape, jnp.float32)
    my_token = me * rows + lax.rem(lax.broadcasted_iota(jnp.int32, (q_rows, 1), 0), rows)

    def attend(plane, lines):
        zh = gather.zh(plane)
        span = NY * part
        index = lax.broadcasted_iota(jnp.int32, (1, span * len(lines)), 1)
        inside = lax.rem(index, span)
        key_token = jnp.zeros(index.shape, jnp.int32)
        blocks = []
        for i, (kind, step, sibling) in enumerate(lines):
            core = 1 - place.core if sibling else place.core
            if kind == 0:
                x = lax.rem(place.x + step + NX, NX)
                blocks.append(keys[0, zh, x, :, core])
                first, stride = place.ctx(zh=zh, x=x, y=0, core=core), 2
            else:
                y = lax.rem(place.y + step + NY, NY)
                blocks.append(keys[1, zh, :, y, core])
                first, stride = place.ctx(zh=zh, x=0, y=y, core=core), 2 * NY
            token = (first + stride * lax.div(inside, part)) * rows + kind * part + lax.rem(inside, part)
            key_token = jnp.where(lax.div(index, span) == i, token, key_token)
        rows_in = jnp.concatenate([block.reshape(span, block.shape[-1]) for block in blocks], axis=0)
        prefix_all = last_dims(prefix_query[...], rows_in[:, : lat + 128])
        hidden = prefix_all[q_rows : q_rows + 1] > UNUSED / 2
        prefix_scores = jnp.where(hidden, HIDDEN, prefix_all[:q_rows])
        group_scores = last_dims(group_query[...], rows_in[:, lat:])
        group_scores = jnp.where(key_token <= my_token, group_scores, HIDDEN)
        old_max = row_max[...]
        new_max = jnp.max(jnp.maximum(prefix_scores, group_scores), axis=1, keepdims=True)
        new_max = jnp.maximum(old_max, new_max)
        prefix_weights = jnp.exp2(prefix_scores - new_max)
        group_weights = jnp.exp2(group_scores - new_max)
        factor = jnp.exp2(old_max - new_max)
        row_max[...] = new_max
        weights = prefix_weights + group_weights
        lanes = weights[:, :128]
        for j in range(1, weights.shape[1] // 128):
            lanes = lanes + weights[:, j * 128 : (j + 1) * 128]
        row_sum[...] = row_sum[...] * factor + lanes
        taken = jnp.dot(prefix_weights.astype(jnp.bfloat16), rows_in[:, :lat], preferred_element_type=jnp.float32)
        taken = taken + jnp.dot(
            group_weights.astype(jnp.bfloat16), rows_in[:, lat + 128 :], preferred_element_type=jnp.float32
        )
        accum[...] = accum[...] * factor + taken

    w_copy = pltpu.make_async_remote_copy(
        src_ref=w_out_any,
        dst_ref=w_out.at[odd],
        send_sem=w_send,
        recv_sem=w_recv,
        device_id=(me, paired),
        device_id_type=MESH,
    )

    def pick(steps, sibling):
        return [(kind, step, sibling) for kind in (0, 1) for step in steps]

    gather.spread(0)
    attend(0, pick((0,), False))
    gather.hand_on(0)
    gather.hand_over(0)
    for kind in (0, 1):
        key_cross(kind, 0).wait_recv()
    gather.start(1)
    w_copy.start()
    attend(0, pick((-1, 1), False))
    gather.complete(0)
    gather.spread(1)
    gather.from_sibling(0, (0, 1, 2))
    attend(0, pick((0, -1), True))
    gather.hand_on(1, (0,))
    attend(0, [(kind, 2, False) for kind in (0, 1)] + [(kind, 1, True) for kind in (0, 1)])
    gather.hand_on(1, (1, 2))
    gather.hand_on(1, (3,))
    gather.hand_over(1)
    attend(1, pick((0, -1, 1), False))
    gather.complete(1)
    gather.from_sibling(0, (3,))
    gather.from_sibling(1, (0, 1, 2))
    attend(1, pick((0, -1, 1), True))
    attend(0, pick((2,), True))
    gather.from_sibling(1, (3,))
    attend(1, pick((2,), False) + pick((2,), True))

    loads[7].wait()
    latent_out = (accum[...] / jnp.sum(row_sum[...], axis=1, keepdims=True)).astype(jnp.bfloat16)
    per_kind = half // VD

    def head_outputs(kind):
        for head in range(kind * per_kind, (kind + 1) * per_kind):
            staged[kind, :, pl.ds((head % per_kind) * VD, VD)] = jnp.dot(
                latent_out[head * rows : (head + 1) * rows], w_uv[head], preferred_element_type=jnp.float32
            ).astype(jnp.bfloat16)

    slot = (place.x, place.y, place.core)
    new_slot = (place.x, place.y, 1 - place.core)

    def leg(kind):
        return pltpu.make_async_remote_copy(
            src_ref=staged.at[kind],
            dst_ref=passing.at[kind],
            send_sem=leg_send.at[kind],
            recv_sem=leg_recv.at[kind],
            device_id=legs[kind],
            device_id_type=MESH,
        )

    def second_leg(kind):
        end_zh = place.up(quarter if kind == 0 else -quarter)[0]
        return pltpu.make_async_remote_copy(
            src_ref=passing.at[kind],
            dst_ref=outs.at[(kind, 1 - end_zh) + slot],
            send_sem=o_cross_send.at[kind],
            recv_sem=o_cross_recv.at[kind],
            device_id=legs[kind],
            device_id_type=MESH,
        )

    def swap(kind):
        return pltpu.make_async_remote_copy(
            src_ref=staged.at[kind],
            dst_ref=outs.at[(kind, place.zh) + new_slot],
            send_sem=swap_send.at[kind],
            recv_sem=swap_recv.at[kind],
            device_id=swap_device,
            device_id_type=MESH,
        )

    def direct(kind):
        return pltpu.make_async_remote_copy(
            src_ref=staged.at[kind],
            dst_ref=outs.at[(kind, place.zh) + new_slot],
            send_sem=o_cross_send.at[kind],
            recv_sem=o_cross_recv.at[kind],
            device_id=swap_across,
            device_id_type=MESH,
        )

    for kind in (0, 1):
        head_outputs(kind)

        @pl.when(stays)
        def _():
            leg(kind).start()
            outs[(kind, place.zh) + slot] = staged[kind]

        @pl.when(moves)
        def _():
            swap(kind).start()
            direct(kind).start()

    @pl.when(moves)
    def _():
        for kind in (0, 1):
            swap(kind).wait_recv()

    spread = Gather(place, outs, o_ring_send, o_ring_recv, o_pair_send, o_pair_recv)
    spread.start(0)
    gather.finish(0)

    @pl.when(stays)
    def _():
        for kind in (0, 1):
            leg(kind).wait_recv()
            second_leg(kind).start()

    block = shares.shape[-1]

    quad = heads // 2
    my_quad = lax.div(place.head, quad)
    inner = jnp.logical_and(place.head >= quad // 2, place.head < quad + quad // 2)
    outer = jnp.logical_not(inner)

    def share(target, slot):
        return pltpu.make_async_remote_copy(
            src_ref=shares.at[target],
            dst_ref=arrived.at[slot],
            send_sem=share_send.at[target],
            recv_sem=share_recv.at[slot],
            device_id=(me, target),
            device_id_type=MESH,
        )

    def near_share(target):
        return share(target, lax.rem(place.head, quad))

    def far_share(target):
        return share(target, quad + lax.rem(place.head, 2))

    def hop(target, x):
        return pltpu.make_async_remote_copy(
            src_ref=shares.at[target],
            dst_ref=passed.at[x],
            send_sem=hop_send.at[x],
            recv_sem=hop_recv.at[x],
            device_id=(me, jnp.where(place.head < quad, place.head + 2, place.head - 2)),
            device_id_type=MESH,
        )

    def part_share(zh, plane, first, count):
        total = jnp.zeros((count * block, w_out.shape[1]), jnp.float32)
        for kind in (0, 1):
            tokens = outs[kind, zh, pl.ds(first, count), :, plane].reshape(count * block, half)
            total = total + last_dims(tokens, w_out[plane, :, kind * half : (kind + 1) * half])
        return total

    def own_share(plane):
        own_part[...] = part_share(spread.zh(plane), place.core, 0, NX)

    def send_shares(plane):
        zh = spread.zh(plane)
        spread.from_sibling(plane)
        for x in range(NX):
            target = zh * NX + x
            if x % 2 == 0:
                total = part_share(zh, 1 - place.core, x, 2)
                total = total + own_part[x * block : (x + 2) * block]
            shares[target] = total[x % 2 * block : (x % 2 + 1) * block].T.astype(jnp.bfloat16)

            @pl.when(jnp.logical_and(my_quad == zh, target != place.head))
            def _():
                near_share(target).start()

            @pl.when(jnp.logical_and(my_quad != zh, outer))
            def _():
                hop(target, x).start()

    def forward_shares(plane):
        zh = spread.zh(plane)

        @pl.when(jnp.logical_and(my_quad != zh, inner))
        def _():
            for x in range(NX):
                target = zh * NX + x
                hop(target, x).wait_recv()
                total = shares[target].astype(jnp.float32) + passed[x].astype(jnp.float32)
                shares[target] = total.astype(jnp.bfloat16)
                far_share(target).start()

    spread.spread(0)
    spread.hand_on(0)
    spread.hand_over(0)
    gather.finish(1)
    for kind in (0, 1):
        direct(kind).wait_recv()
    spread.start(1)
    spread.complete(0)
    spread.spread(1)
    loads[8].wait()
    w_copy.wait_recv()
    own_share(0)
    spread.hand_on(1, (0, 1))
    spread.hand_on(1, (2, 3))
    spread.hand_over(1)
    send_shares(0)
    spread.complete(1)
    own_share(1)
    forward_shares(0)
    send_shares(1)
    forward_shares(1)
    spread.finish(0)
    spread.finish(1)

    own_slot = lax.rem(place.head, quad)
    arrived[own_slot] = shares[place.head]
    for source in range(quad):

        @pl.when(source != own_slot)
        def _():
            share(place.head, source).wait_recv()

    for source in (quad, quad + 1):
        share(place.head, source).wait_recv()

    total = jnp.zeros(mixed.shape, jnp.float32)
    source_lane = lax.broadcasted_iota(jnp.int32, (block, mixed.shape[1]), 0)
    token = lax.broadcasted_iota(jnp.int32, (block, mixed.shape[1]), 1)
    for plane in (0, 1):
        summed = jnp.zeros(shares.shape[1:], jnp.float32)
        for source in range(plane, quad + 2, 2):
            summed = summed + arrived[source].astype(jnp.float32)
        lane_of = lax.div(token, 2 * rows) * rows + lax.rem(token, rows)
        here = jnp.logical_and(lane_of == source_lane, lax.rem(lax.div(token, rows), 2) == plane)
        total = total + jnp.dot(
            summed.astype(jnp.bfloat16), jnp.where(here, 1.0, 0.0).astype(jnp.bfloat16), preferred_element_type=jnp.float32
        )
    mixed[...] = total.astype(jnp.bfloat16)

    w_copy.wait_send()

    @pl.when(is_end)
    def _():
        for j in range(half_heads):
            for kind in (0, 1):
                key_cross(kind, j).wait_send()

    @pl.when(stays)
    def _():
        for kind in (0, 1):
            leg(kind).wait_send()
            second_leg(kind).wait_send()

    @pl.when(moves)
    def _():
        for kind in (0, 1):
            swap(kind).wait_send()
            direct(kind).wait_send()

    for x in range(NX):

        @pl.when(x != own_slot)
        def _():
            near_share(my_quad * quad + x).wait_send()

        @pl.when(inner)
        def _():
            far_share((1 - my_quad) * quad + x).wait_send()

        @pl.when(outer)
        def _():
            hop((1 - my_quad) * quad + x, x).wait_send()


def gather_scratch():
    return [
        pltpu.SemaphoreType.DMA((4 * RING,)),
        pltpu.SemaphoreType.DMA((4 * RING,)),
        pltpu.SemaphoreType.DMA((16,)),
        pltpu.SemaphoreType.DMA((16,)),
    ]


def on_device(
    heads,
    q_nope,
    q_rope,
    prefix_latent,
    prefix_rope,
    group_latent,
    group_rope,
    lengths,
    offset,
    w_uk,
    w_uv,
    w_out,
):
    rows, lat = prefix_latent.shape
    h_dev = w_uk.shape[0]
    q_rows = rows * h_dev
    width = 2 * lat + 128
    columns = w_out.shape[1]
    half = h_dev * VD // 2
    frequency = 10000.0 ** (-2.0 * (np.arange(128) % (ROPE // 2)) / ROPE)
    frequency = jnp.asarray(frequency[None, :], jnp.float32)

    tokens = rows * 2 * 2 * NX * NY
    block = rows * NY
    vmem = pl.BlockSpec(memory_space=pltpu.VMEM)
    smem = pl.BlockSpec(memory_space=pltpu.SMEM)
    anywhere = pl.BlockSpec(memory_space=pl.ANY)
    dma = pltpu.SemaphoreType.DMA
    mixed = pl.pallas_call(
        functools.partial(kernel, heads),
        out_shape=pltpu.VMEM((columns, tokens // heads), jnp.bfloat16),
        in_specs=[smem] * 2 + [anywhere] * 10,
        out_specs=vmem,
        scratch_shapes=[
            pltpu.VMEM((2, 2, NX, NY, 2, rows // 2, width), jnp.bfloat16),
            pltpu.VMEM((q_rows + 16, lat + 128), jnp.bfloat16),
            pltpu.VMEM((q_rows, lat + 128), jnp.bfloat16),
            pltpu.VMEM((q_rows, 1), jnp.float32),
            pltpu.VMEM((q_rows, 128), jnp.float32),
            pltpu.VMEM((q_rows, lat), jnp.float32),
            pltpu.VMEM((2, 2, NX, NY, 2, rows, half), jnp.bfloat16),
            pltpu.VMEM((2, rows, half), jnp.bfloat16),
            pltpu.VMEM((2, rows, half), jnp.bfloat16),
            pltpu.VMEM((2, columns, 2 * half), jnp.bfloat16),
            pltpu.VMEM((heads, columns, block), jnp.bfloat16),
            pltpu.VMEM((heads // 2 + 2, columns, block), jnp.bfloat16),
            pltpu.VMEM((NX, columns, block), jnp.bfloat16),
            pltpu.VMEM((NX * block, columns), jnp.float32),
            pltpu.VMEM(q_nope.shape, jnp.bfloat16),
            pltpu.VMEM(q_rope.shape, jnp.bfloat16),
            pltpu.VMEM(prefix_rope.shape, jnp.bfloat16),
            pltpu.VMEM(group_rope.shape, jnp.bfloat16),
            pltpu.VMEM(w_uk.shape, jnp.bfloat16),
            pltpu.VMEM(w_uv.shape, jnp.bfloat16),
            pltpu.VMEM((1, 128), jnp.float32),
            dma((12,)),
        ]
        + gather_scratch()
        + [dma((heads,)), dma((2,))]
        + gather_scratch()
        + [dma((2,)), dma((2,)), dma((2,)), dma((2,)), dma((2,)), dma((2,))]
        + [dma(()), dma(()), dma((heads,)), dma((heads // 2 + 2,)), dma((NX,)), dma((NX,))],
        compiler_params=pltpu.CompilerParams(
            collective_id=0, has_side_effects=True, vmem_limit_bytes=60 * 1024 * 1024
        ),
        name="attention_and_output",
    )(
        lengths,
        offset,
        q_nope,
        q_rope,
        prefix_latent,
        prefix_rope,
        group_latent,
        group_rope,
        frequency,
        w_uk,
        w_uv,
        w_out.T,
    )
    return mixed.T


def solution(mesh):
    return jax.shard_map(
        functools.partial(on_device, mesh.shape["head"]),
        mesh=mesh,
        in_specs=(
            P("ctx", "head"),
            P("ctx", "head"),
            P("ctx", None),
            P("ctx", None),
            P("ctx", None),
            P("ctx", None),
            P("ctx"),
            P(),
            P("head", None, None),
            P("head", None, None),
            P("head", "ctx"),
        ),
        out_specs=P("head", "ctx"),
        check_vma=False,
    )
```

```python
import functools
import math

import jax
import jax.numpy as jnp
import numpy as np
from jax import lax
from jax.experimental import pallas as pl
from jax.experimental.pallas import tpu as pltpu
from jax.sharding import PartitionSpec as P

ROPE = 64
NOPE = 128
VD = 128
NX = 4
NY = 4
HIDDEN = -1e30
UNUSED = 1024.0
MESH = pl.DeviceIdType.MESH


class Place:
    def __init__(self, heads):
        c = lax.axis_index("ctx")
        self.heads = heads
        self.head = lax.axis_index("head")
        self.core = lax.rem(c, 2)
        self.y = lax.rem(lax.div(c, 2), NY)
        self.x = lax.rem(lax.div(c, 2 * NY), NX)
        self.zh = lax.div(c, 2 * NX * NY)

    def ctx(self, zh=None, x=None, y=None, core=None):
        zh = self.zh if zh is None else zh
        x = self.x if x is None else x
        y = self.y if y is None else y
        core = self.core if core is None else core
        return ((zh * NX + x) * NY + y) * 2 + core

    def along(self, axis, step):
        if axis == 0:
            return (self.ctx(x=lax.rem(self.x + step + NX, NX)), self.head)
        return (self.ctx(y=lax.rem(self.y + step + NY, NY)), self.head)

    def sibling(self):
        return (self.ctx(core=1 - self.core), self.head)

    def across(self, head=None):
        return (self.ctx(zh=1 - self.zh), self.head if head is None else head)


def greet(devices):
    barrier = pltpu.get_barrier_semaphore()
    for device in devices:
        pl.semaphore_signal(barrier, inc=1, device_id=device, device_id_type=MESH)


def plane_peers(place):
    return [place.along(axis, step) for axis in (0, 1) for step in (1, -1, 2)] + [place.sibling()]


RING = 16
OFFSETS = (0, -1, 1, 2)
STEPS = (1, -1, 2)


class Gather:
    def __init__(self, place, buf, ring_send, ring_recv, pair_send, pair_recv):
        self.place = place
        self.buf = buf
        self.ring_send, self.ring_recv = ring_send, ring_recv
        self.pair_send, self.pair_recv = pair_send, pair_recv

    def zh(self, plane):
        return self.place.zh if plane == 0 else 1 - self.place.zh

    def cell(self, kind, plane, first, second):
        place = self.place
        dx, dy = (second, first) if kind == 0 else (first, second)
        x = lax.rem(place.x + dx + NX, NX)
        y = lax.rem(place.y + dy + NY, NY)
        return self.buf.at[kind, self.zh(plane), x, y, place.core]

    def line(self, kind, plane, second):
        place, zh = self.place, self.zh(plane)
        if kind == 0:
            return self.buf.at[kind, zh, lax.rem(place.x + second + NX, NX), pl.ds(0, NY), place.core]
        return self.buf.at[kind, zh, pl.ds(0, NX), lax.rem(place.y + second + NY, NY), place.core]

    def copy(self, ref, kind, plane, slot, device):
        index = (kind * 2 + plane) * RING + slot
        return pltpu.make_async_remote_copy(
            src_ref=ref,
            dst_ref=ref,
            send_sem=self.ring_send.at[index],
            recv_sem=self.ring_recv.at[index],
            device_id=device,
            device_id_type=MESH,
        )

    def first(self, kind, plane, i):
        return self.copy(self.cell(kind, plane, 0, 0), kind, plane, i, self.place.along(1 - kind, STEPS[i]))

    def second(self, kind, plane, o, direction):
        ref = self.cell(kind, plane, OFFSETS[o], 0)
        return self.copy(ref, kind, plane, 3 + 2 * o + direction, self.place.along(kind, STEPS[direction]))

    def relay(self, kind, plane, o):
        direction = o // 2
        ref = self.cell(kind, plane, OFFSETS[o], -STEPS[direction])
        return self.copy(ref, kind, plane, 11 + o, self.place.along(kind, STEPS[direction]))

    def pair(self, kind, plane, piece):
        ref = self.line(kind, plane, OFFSETS[piece])
        index = (kind * 2 + plane) * 4 + piece
        return pltpu.make_async_remote_copy(
            src_ref=ref,
            dst_ref=ref,
            send_sem=self.pair_send.at[index],
            recv_sem=self.pair_recv.at[index],
            device_id=self.place.sibling(),
            device_id_type=MESH,
        )

    def start(self, plane):
        for i in range(3):
            for kind in (0, 1):
                self.first(kind, plane, i).start()
        for direction in (0, 1):
            for kind in (0, 1):
                self.second(kind, plane, 0, direction).start()

    def spread(self, plane):
        for i in range(3):
            for kind in (0, 1):
                self.first(kind, plane, i).wait_recv()
                for direction in (0, 1):
                    self.second(kind, plane, 1 + i, direction).start()
        for kind in (0, 1):
            self.pair(kind, plane, 0).start()

    def hand_on(self, plane, offsets=(0, 1, 2, 3)):
        for o in offsets:
            for kind in (0, 1):
                for direction in (0, 1):
                    self.second(kind, plane, o, direction).wait_recv()
                self.relay(kind, plane, o).start()

    def hand_over(self, plane):
        for piece in (1, 2):
            for kind in (0, 1):
                self.pair(kind, plane, piece).start()

    def complete(self, plane):
        for kind in (0, 1):
            for o in range(4):
                self.relay(kind, plane, o).wait_recv()
            self.pair(kind, plane, 3).start()

    def from_sibling(self, plane, pieces=(0, 1, 2, 3)):
        for kind in (0, 1):
            for piece in pieces:
                self.pair(kind, plane, piece).wait_recv()

    def finish(self, plane):
        for kind in (0, 1):
            for i in range(3):
                self.first(kind, plane, i).wait_send()
            for o in range(4):
                for direction in (0, 1):
                    self.second(kind, plane, o, direction).wait_send()
                self.relay(kind, plane, o).wait_send()
                self.pair(kind, plane, o).wait_send()


def last_dims(a, b):
    return lax.dot_general(a, b, (((1,), (1,)), ((), ())), preferred_element_type=jnp.float32)


def cos_sin(angle):
    turns = jnp.floor(angle * (2.0 / math.pi) + 0.5)
    rest = ((angle - turns * 1.5703125) - turns * 4.837512969970703125e-4) - turns * 7.54978995489188216e-8
    square = rest * rest
    sine = ((-1.9515295891e-4 * square + 8.3321608736e-3) * square - 1.6666654611e-1) * square * rest + rest
    cosine = (2.443315711809948e-5 * square - 1.388731625493765e-3) * square + 4.166664568298827e-2
    cosine = cosine * square * square - 0.5 * square + 1.0
    quarter = jnp.bitwise_and(turns.astype(jnp.int32), 3)
    swap = jnp.bitwise_and(quarter, 1) == 1
    cos_part = jnp.where(swap, sine, cosine)
    sin_part = jnp.where(swap, cosine, sine)
    cos_part = jnp.where(jnp.logical_or(quarter == 1, quarter == 2), -cos_part, cos_part)
    sin_part = jnp.where(quarter >= 2, -sin_part, sin_part)
    return cos_part, sin_part


def kernel(
    heads,
    lengths,
    offset,
    q_nope_any,
    q_rope_any,
    prefix_latent,
    prefix_rope_any,
    group_latent,
    group_rope_any,
    frequency_any,
    w_uk_any,
    w_uv_any,
    w_out_any,
    mixed,
    keys,
    prefix_query,
    group_query,
    row_max,
    row_sum,
    accum,
    outs,
    staged,
    w_out,
    shares,
    arrived,
    passed,
    q_nope,
    q_rope,
    prefix_rope,
    group_rope,
    w_uk,
    w_uv,
    frequency,
    load_sem,
    k_ring_send,
    k_ring_recv,
    k_pair_send,
    k_pair_recv,
    k_cross_send,
    k_cross_recv,
    o_ring_send,
    o_ring_recv,
    o_pair_send,
    o_pair_recv,
    o_cross_send,
    o_cross_recv,
    swap_send,
    swap_recv,
    w_send,
    w_recv,
    share_send,
    share_recv,
    hop_send,
    hop_recv,
):
    place = Place(heads)
    rows, lat = prefix_latent.shape
    h_dev = w_uk.shape[0]
    part = rows // 2
    half = staged.shape[-1]
    half_heads = heads // 2
    me = place.ctx()
    own = (place.zh, place.x, place.y, place.core)
    odd = lax.rem(place.head, 2)
    paired = place.head + 1 - 2 * odd
    stays = place.core == odd
    moves = place.core != odd
    is_end = jnp.logical_or(place.head == 0, place.head == heads - 1)

    swap_device = (place.ctx(core=1 - place.core), paired)
    swap_across = (place.ctx(zh=1 - place.zh, core=1 - place.core), paired)
    others = [(me, lax.rem(place.head + j, heads)) for j in range(1, heads)]
    far_end = jnp.where(place.head < half_heads, heads - 1, 0)
    served = [jnp.where(place.head == 0, heads - 1 - j, j) for j in range(half_heads)]
    peers = plane_peers(place) + others + [place.across(far_end)]

    greet(peers)

    @pl.when(stays)
    def _():
        greet([place.across(), place.across()])

    @pl.when(moves)
    def _():
        greet([swap_device, swap_across])

    @pl.when(is_end)
    def _():
        greet([place.across(head) for head in served])

    loads = [
        pltpu.make_async_copy(src, dst, load_sem.at[i])
        for i, (src, dst) in enumerate(
            (
                (prefix_latent.at[pl.ds(0, part)], keys.at[(0,) + own + (slice(None), pl.ds(0, lat))]),
                (group_latent.at[pl.ds(0, part)], keys.at[(0,) + own + (slice(None), pl.ds(lat + 128, lat))]),
                (q_nope_any, q_nope),
                (q_rope_any, q_rope),
                (prefix_rope_any, prefix_rope),
                (group_rope_any, group_rope),
                (w_uk_any, w_uk),
                (w_uv_any, w_uv),
                (w_out_any, w_out.at[odd]),
                (frequency_any, frequency),
                (prefix_latent.at[pl.ds(part, part)], keys.at[(1,) + own + (slice(None), pl.ds(0, lat))]),
                (group_latent.at[pl.ds(part, part)], keys.at[(1,) + own + (slice(None), pl.ds(lat + 128, lat))]),
            )
        )
    ]
    for load in loads:
        load.start()
    lane = lax.broadcasted_iota(jnp.int32, (rows, 128), 1)
    row = lax.broadcasted_iota(jnp.int32, (rows, 128), 0)
    for i in (9, 4, 5):
        loads[i].wait()
    positions = (offset[0] + me * rows + row).astype(jnp.float32)
    cos_part, sin_part = cos_sin(positions * frequency[...])
    first_half = lax.rem(lane, ROPE) < ROPE // 2
    sin_part = jnp.where(first_half, -sin_part, sin_part)

    def turn(tile):
        swapped = jnp.where(first_half, pltpu.roll(tile, 128 - ROPE // 2, 1), pltpu.roll(tile, ROPE // 2, 1))
        return tile * cos_part + swapped * sin_part

    def twice(ref):
        value = ref[...].astype(jnp.float32)
        return jnp.concatenate([value, value], axis=1)

    unused = jnp.where(lane == 0, UNUSED, 0.0)
    ropes = jnp.where(row < lengths[0], twice(prefix_rope), unused)
    ropes = jnp.where(lane < ROPE, ropes, turn(twice(group_rope))).astype(jnp.bfloat16)
    for kind in (0, 1):
        keys[(kind,) + own + (slice(None), pl.ds(lat, 128))] = ropes[kind * part : (kind + 1) * part]
    for i in (0, 1, 10, 11):
        loads[i].wait()

    pl.semaphore_wait(pltpu.get_barrier_semaphore(), len(peers) + 2 + half_heads * is_end.astype(jnp.int32))

    gather = Gather(place, keys, k_ring_send, k_ring_recv, k_pair_send, k_pair_recv)

    def key_cross(kind, j):
        ref = keys.at[(kind,) + own]
        return pltpu.make_async_remote_copy(
            src_ref=ref,
            dst_ref=ref,
            send_sem=k_cross_send.at[kind * half_heads + j],
            recv_sem=k_cross_recv.at[kind],
            device_id=place.across(served[j]),
            device_id_type=MESH,
        )

    @pl.when(is_end)
    def _():
        for j in reversed(range(half_heads)):
            for kind in (0, 1):
                key_cross(kind, j).start()

    gather.start(0)

    scale = (NOPE + ROPE) ** -0.5 * math.log2(math.e)

    q_rows = h_dev * rows
    loads[2].wait()
    loads[3].wait()
    loads[6].wait()
    mark = jnp.logical_and(lane[:16] == 0, row[:16] == 0)
    prefix_query[pl.ds(q_rows, 16), pl.ds(0, lat)] = jnp.zeros((16, lat), jnp.bfloat16)
    prefix_query[pl.ds(q_rows, 16), pl.ds(lat, 128)] = jnp.where(mark, 1.0, 0.0).astype(jnp.bfloat16)
    for pair in range(h_dev // 2):
        turned = turn(q_rope[:, pair * 128 : (pair + 1) * 128].astype(jnp.float32)) * scale
        other = pltpu.roll(turned, ROPE, 1)
        for side in (0, 1):
            head = 2 * pair + side
            at = pl.ds(head * rows, rows)
            low_part, high_part = (turned, other) if side == 0 else (other, turned)
            prefix_query[at, pl.ds(lat, 128)] = jnp.where(lane < ROPE, low_part, 0.0).astype(jnp.bfloat16)
            group_query[at, pl.ds(0, 128)] = jnp.where(lane >= ROPE, high_part, 0.0).astype(jnp.bfloat16)
            latent = jnp.dot(
                q_nope[:, head * NOPE : (head + 1) * NOPE], w_uk[head], preferred_element_type=jnp.float32
            )
            latent = (latent * scale).astype(jnp.bfloat16)
            prefix_query[at, pl.ds(0, lat)] = latent
            group_query[at, pl.ds(128, lat)] = latent

    row_max[...] = jnp.full(row_max.shape, HIDDEN, jnp.float32)
    row_sum[...] = jnp.zeros(row_sum.shape, jnp.float32)
    accum[...] = jnp.zeros(accum.shape, jnp.float32)
    my_token = me * rows + lax.rem(lax.broadcasted_iota(jnp.int32, (q_rows, 1), 0), rows)

    def attend(plane, lines):
        zh = gather.zh(plane)
        span = NY * part
        index = lax.broadcasted_iota(jnp.int32, (1, span * len(lines)), 1)
        inside = lax.rem(index, span)
        key_token = jnp.zeros(index.shape, jnp.int32)
        blocks = []
        for i, (kind, step, sibling) in enumerate(lines):
            core = 1 - place.core if sibling else place.core
            if kind == 0:
                x = lax.rem(place.x + step + NX, NX)
                blocks.append(keys[0, zh, x, :, core])
                first, stride = place.ctx(zh=zh, x=x, y=0, core=core), 2
            else:
                y = lax.rem(place.y + step + NY, NY)
                blocks.append(keys[1, zh, :, y, core])
                first, stride = place.ctx(zh=zh, x=0, y=y, core=core), 2 * NY
            token = (first + stride * lax.div(inside, part)) * rows + kind * part + lax.rem(inside, part)
            key_token = jnp.where(lax.div(index, span) == i, token, key_token)
        rows_in = jnp.concatenate([block.reshape(span, block.shape[-1]) for block in blocks], axis=0)
        prefix_all = last_dims(prefix_query[...], rows_in[:, : lat + 128])
        hidden = prefix_all[q_rows : q_rows + 1] > UNUSED / 2
        prefix_scores = jnp.where(hidden, HIDDEN, prefix_all[:q_rows])
        group_scores = last_dims(group_query[...], rows_in[:, lat:])
        group_scores = jnp.where(key_token <= my_token, group_scores, HIDDEN)
        old_max = row_max[...]
        new_max = jnp.max(jnp.maximum(prefix_scores, group_scores), axis=1, keepdims=True)
        new_max = jnp.maximum(old_max, new_max)
        prefix_weights = jnp.exp2(prefix_scores - new_max)
        group_weights = jnp.exp2(group_scores - new_max)
        factor = jnp.exp2(old_max - new_max)
        row_max[...] = new_max
        weights = prefix_weights + group_weights
        lanes = weights[:, :128]
        for j in range(1, weights.shape[1] // 128):
            lanes = lanes + weights[:, j * 128 : (j + 1) * 128]
        row_sum[...] = row_sum[...] * factor + lanes
        taken = jnp.dot(prefix_weights.astype(jnp.bfloat16), rows_in[:, :lat], preferred_element_type=jnp.float32)
        taken = taken + jnp.dot(
            group_weights.astype(jnp.bfloat16), rows_in[:, lat + 128 :], preferred_element_type=jnp.float32
        )
        accum[...] = accum[...] * factor + taken

    w_copy = pltpu.make_async_remote_copy(
        src_ref=w_out_any,
        dst_ref=w_out.at[odd],
        send_sem=w_send,
        recv_sem=w_recv,
        device_id=(me, paired),
        device_id_type=MESH,
    )

    def pick(steps, sibling):
        return [(kind, step, sibling) for kind in (0, 1) for step in steps]

    gather.spread(0)
    attend(0, pick((0,), False))
    gather.hand_on(0)
    gather.hand_over(0)
    for kind in (0, 1):
        key_cross(kind, 0).wait_recv()
    gather.start(1)
    w_copy.start()
    attend(0, pick((-1, 1), False))
    gather.complete(0)
    gather.spread(1)
    gather.from_sibling(0, (0, 1, 2))
    attend(0, pick((0, -1), True))
    gather.hand_on(1, (0,))
    attend(0, [(kind, 2, False) for kind in (0, 1)] + [(kind, 1, True) for kind in (0, 1)])
    gather.hand_on(1, (1, 2))
    gather.hand_on(1, (3,))
    gather.hand_over(1)
    attend(1, pick((0, -1, 1), False))
    gather.complete(1)
    gather.from_sibling(0, (3,))
    gather.from_sibling(1, (0, 1, 2))
    attend(1, pick((0, -1, 1), True))
    attend(0, pick((2,), True))
    gather.from_sibling(1, (3,))
    attend(1, pick((2,), False) + pick((2,), True))

    loads[7].wait()
    latent_out = (accum[...] / jnp.sum(row_sum[...], axis=1, keepdims=True)).astype(jnp.bfloat16)
    per_kind = half // VD
    for head in range(h_dev):
        staged[head // per_kind, :, pl.ds((head % per_kind) * VD, VD)] = jnp.dot(
            latent_out[head * rows : (head + 1) * rows], w_uv[head], preferred_element_type=jnp.float32
        ).astype(jnp.bfloat16)

    slot = (place.x, place.y, place.core)
    new_slot = (place.x, place.y, 1 - place.core)

    def stay(kind):
        return pltpu.make_async_remote_copy(
            src_ref=staged.at[kind],
            dst_ref=outs.at[(kind, place.zh) + slot],
            send_sem=o_cross_send.at[kind],
            recv_sem=o_cross_recv.at[kind],
            device_id=place.across(),
            device_id_type=MESH,
        )

    def swap(kind):
        return pltpu.make_async_remote_copy(
            src_ref=staged.at[kind],
            dst_ref=outs.at[(kind, place.zh) + new_slot],
            send_sem=swap_send.at[kind],
            recv_sem=swap_recv.at[kind],
            device_id=swap_device,
            device_id_type=MESH,
        )

    def direct(kind):
        return pltpu.make_async_remote_copy(
            src_ref=staged.at[kind],
            dst_ref=outs.at[(kind, place.zh) + new_slot],
            send_sem=o_cross_send.at[kind],
            recv_sem=o_cross_recv.at[kind],
            device_id=swap_across,
            device_id_type=MESH,
        )

    @pl.when(stays)
    def _():
        for kind in (0, 1):
            stay(kind).start()
        for kind in (0, 1):
            outs[(kind, place.zh) + slot] = staged[kind]

    @pl.when(moves)
    def _():
        for kind in (0, 1):
            swap(kind).start()
        for kind in (0, 1):
            direct(kind).start()
        for kind in (0, 1):
            swap(kind).wait_recv()

    spread = Gather(place, outs, o_ring_send, o_ring_recv, o_pair_send, o_pair_recv)
    spread.start(0)
    gather.finish(0)

    block = shares.shape[-1]

    quad = heads // 2
    my_quad = lax.div(place.head, quad)
    inner = jnp.logical_and(place.head >= quad // 2, place.head < quad + quad // 2)
    outer = jnp.logical_not(inner)

    def share(target, slot):
        return pltpu.make_async_remote_copy(
            src_ref=shares.at[target],
            dst_ref=arrived.at[slot],
            send_sem=share_send.at[target],
            recv_sem=share_recv.at[slot],
            device_id=(me, target),
            device_id_type=MESH,
        )

    def near_share(target):
        return share(target, lax.rem(place.head, quad))

    def far_share(target):
        return share(target, quad + lax.rem(place.head, 2))

    def hop(target, x):
        return pltpu.make_async_remote_copy(
            src_ref=shares.at[target],
            dst_ref=passed.at[x],
            send_sem=hop_send.at[x],
            recv_sem=hop_recv.at[x],
            device_id=(me, jnp.where(place.head < quad, place.head + 2, place.head - 2)),
            device_id_type=MESH,
        )

    def part_share(zh, plane):
        total = jnp.zeros((NX * block, w_out.shape[1]), jnp.float32)
        for kind in (0, 1):
            tokens = outs[kind, zh, :, :, plane].reshape(NX * block, half)
            total = total + last_dims(tokens, w_out[plane, :, kind * half : (kind + 1) * half])
        return total

    def send_shares(plane):
        zh = spread.zh(plane)
        total = part_share(zh, place.core)
        spread.from_sibling(plane)
        total = total + part_share(zh, 1 - place.core)
        for x in range(NX):
            target = zh * NX + x
            shares[target] = total[x * block : (x + 1) * block].T.astype(jnp.bfloat16)

            @pl.when(jnp.logical_and(my_quad == zh, target != place.head))
            def _():
                near_share(target).start()

            @pl.when(jnp.logical_and(my_quad != zh, outer))
            def _():
                hop(target, x).start()

    def forward_shares(plane):
        zh = spread.zh(plane)

        @pl.when(jnp.logical_and(my_quad != zh, inner))
        def _():
            for x in range(NX):
                target = zh * NX + x
                hop(target, x).wait_recv()
                total = shares[target].astype(jnp.float32) + passed[x].astype(jnp.float32)
                shares[target] = total.astype(jnp.bfloat16)
                far_share(target).start()

    spread.spread(0)
    gather.finish(1)
    spread.hand_on(0)
    spread.hand_over(0)
    for kind in (0, 1):
        direct(kind).wait_recv()
    spread.start(1)
    spread.complete(0)
    spread.spread(1)
    loads[8].wait()
    w_copy.wait_recv()
    send_shares(0)
    spread.hand_on(1, (0, 1))
    spread.hand_on(1, (2, 3))
    spread.hand_over(1)
    forward_shares(0)
    spread.complete(1)
    send_shares(1)
    forward_shares(1)
    spread.finish(0)
    spread.finish(1)

    own_slot = lax.rem(place.head, quad)
    arrived[own_slot] = shares[place.head]
    for source in range(quad):

        @pl.when(source != own_slot)
        def _():
            share(place.head, source).wait_recv()

    for source in (quad, quad + 1):
        share(place.head, source).wait_recv()

    total = jnp.zeros(mixed.shape, jnp.float32)
    source_lane = lax.broadcasted_iota(jnp.int32, (block, mixed.shape[1]), 0)
    token = lax.broadcasted_iota(jnp.int32, (block, mixed.shape[1]), 1)
    for plane in (0, 1):
        summed = jnp.zeros(shares.shape[1:], jnp.float32)
        for source in range(plane, quad + 2, 2):
            summed = summed + arrived[source].astype(jnp.float32)
        lane_of = lax.div(token, 2 * rows) * rows + lax.rem(token, rows)
        here = jnp.logical_and(lane_of == source_lane, lax.rem(lax.div(token, rows), 2) == plane)
        total = total + jnp.dot(
            summed.astype(jnp.bfloat16), jnp.where(here, 1.0, 0.0).astype(jnp.bfloat16), preferred_element_type=jnp.float32
        )
    mixed[...] = total.astype(jnp.bfloat16)

    w_copy.wait_send()

    @pl.when(is_end)
    def _():
        for j in range(half_heads):
            for kind in (0, 1):
                key_cross(kind, j).wait_send()

    @pl.when(stays)
    def _():
        for kind in (0, 1):
            stay(kind).wait_send()

    @pl.when(moves)
    def _():
        for kind in (0, 1):
            swap(kind).wait_send()
            direct(kind).wait_send()

    for x in range(NX):

        @pl.when(x != own_slot)
        def _():
            near_share(my_quad * quad + x).wait_send()

        @pl.when(inner)
        def _():
            far_share((1 - my_quad) * quad + x).wait_send()

        @pl.when(outer)
        def _():
            hop((1 - my_quad) * quad + x, x).wait_send()


def gather_scratch():
    return [
        pltpu.SemaphoreType.DMA((4 * RING,)),
        pltpu.SemaphoreType.DMA((4 * RING,)),
        pltpu.SemaphoreType.DMA((16,)),
        pltpu.SemaphoreType.DMA((16,)),
    ]


def on_device(
    heads,
    q_nope,
    q_rope,
    prefix_latent,
    prefix_rope,
    group_latent,
    group_rope,
    lengths,
    offset,
    w_uk,
    w_uv,
    w_out,
):
    rows, lat = prefix_latent.shape
    h_dev = w_uk.shape[0]
    q_rows = rows * h_dev
    width = 2 * lat + 128
    columns = w_out.shape[1]
    half = h_dev * VD // 2
    frequency = 10000.0 ** (-2.0 * (np.arange(128) % (ROPE // 2)) / ROPE)
    frequency = jnp.asarray(frequency[None, :], jnp.float32)

    tokens = rows * 2 * 2 * NX * NY
    block = rows * NY
    vmem = pl.BlockSpec(memory_space=pltpu.VMEM)
    smem = pl.BlockSpec(memory_space=pltpu.SMEM)
    anywhere = pl.BlockSpec(memory_space=pl.ANY)
    dma = pltpu.SemaphoreType.DMA
    mixed = pl.pallas_call(
        functools.partial(kernel, heads),
        out_shape=pltpu.VMEM((columns, tokens // heads), jnp.bfloat16),
        in_specs=[smem] * 2 + [anywhere] * 10,
        out_specs=vmem,
        scratch_shapes=[
            pltpu.VMEM((2, 2, NX, NY, 2, rows // 2, width), jnp.bfloat16),
            pltpu.VMEM((q_rows + 16, lat + 128), jnp.bfloat16),
            pltpu.VMEM((q_rows, lat + 128), jnp.bfloat16),
            pltpu.VMEM((q_rows, 1), jnp.float32),
            pltpu.VMEM((q_rows, 128), jnp.float32),
            pltpu.VMEM((q_rows, lat), jnp.float32),
            pltpu.VMEM((2, 2, NX, NY, 2, rows, half), jnp.bfloat16),
            pltpu.VMEM((2, rows, half), jnp.bfloat16),
            pltpu.VMEM((2, columns, 2 * half), jnp.bfloat16),
            pltpu.VMEM((heads, columns, block), jnp.bfloat16),
            pltpu.VMEM((heads // 2 + 2, columns, block), jnp.bfloat16),
            pltpu.VMEM((NX, columns, block), jnp.bfloat16),
            pltpu.VMEM(q_nope.shape, jnp.bfloat16),
            pltpu.VMEM(q_rope.shape, jnp.bfloat16),
            pltpu.VMEM(prefix_rope.shape, jnp.bfloat16),
            pltpu.VMEM(group_rope.shape, jnp.bfloat16),
            pltpu.VMEM(w_uk.shape, jnp.bfloat16),
            pltpu.VMEM(w_uv.shape, jnp.bfloat16),
            pltpu.VMEM((1, 128), jnp.float32),
            dma((12,)),
        ]
        + gather_scratch()
        + [dma((heads,)), dma((2,))]
        + gather_scratch()
        + [dma((2,)), dma((2,)), dma((2,)), dma((2,))]
        + [dma(()), dma(()), dma((heads,)), dma((heads // 2 + 2,)), dma((NX,)), dma((NX,))],
        compiler_params=pltpu.CompilerParams(
            collective_id=0, has_side_effects=True, vmem_limit_bytes=60 * 1024 * 1024
        ),
        name="attention_and_output",
    )(
        lengths,
        offset,
        q_nope,
        q_rope,
        prefix_latent,
        prefix_rope,
        group_latent,
        group_rope,
        frequency,
        w_uk,
        w_uv,
        w_out.T,
    )
    return mixed.T


def solution(mesh):
    return jax.shard_map(
        functools.partial(on_device, mesh.shape["head"]),
        mesh=mesh,
        in_specs=(
            P("ctx", "head"),
            P("ctx", "head"),
            P("ctx", None),
            P("ctx", None),
            P("ctx", None),
            P("ctx", None),
            P("ctx"),
            P(),
            P("head", None, None),
            P("head", None, None),
            P("head", "ctx"),
        ),
        out_specs=P("head", "ctx"),
        check_vma=False,
    )
```

```python
import functools
import math

import jax
import jax.numpy as jnp
import numpy as np
from jax import lax
from jax.experimental import pallas as pl
from jax.experimental.pallas import tpu as pltpu
from jax.sharding import PartitionSpec as P

ROPE = 64
NOPE = 128
VD = 128
NX = 4
NY = 4
HIDDEN = -1e30
UNUSED = 1024.0
MESH = pl.DeviceIdType.MESH


class Place:
    def __init__(self, heads):
        c = lax.axis_index("ctx")
        self.heads = heads
        self.head = lax.axis_index("head")
        self.core = lax.rem(c, 2)
        self.y = lax.rem(lax.div(c, 2), NY)
        self.x = lax.rem(lax.div(c, 2 * NY), NX)
        self.zh = lax.div(c, 2 * NX * NY)

    def ctx(self, zh=None, x=None, y=None, core=None):
        zh = self.zh if zh is None else zh
        x = self.x if x is None else x
        y = self.y if y is None else y
        core = self.core if core is None else core
        return ((zh * NX + x) * NY + y) * 2 + core

    def along(self, axis, step):
        if axis == 0:
            return (self.ctx(x=lax.rem(self.x + step + NX, NX)), self.head)
        return (self.ctx(y=lax.rem(self.y + step + NY, NY)), self.head)

    def sibling(self):
        return (self.ctx(core=1 - self.core), self.head)

    def across(self, head=None):
        return (self.ctx(zh=1 - self.zh), self.head if head is None else head)


    def up(self, step):
        z = lax.rem(self.zh * self.heads + self.head + step + 2 * self.heads, 2 * self.heads)
        return lax.div(z, self.heads), lax.rem(z, self.heads)


def greet(devices):
    barrier = pltpu.get_barrier_semaphore()
    for device in devices:
        pl.semaphore_signal(barrier, inc=1, device_id=device, device_id_type=MESH)


def plane_peers(place):
    return [place.along(axis, step) for axis in (0, 1) for step in (1, -1, 2)] + [place.sibling()]


RING = 16
OFFSETS = (0, -1, 1, 2)
STEPS = (1, -1, 2)


class Gather:
    def __init__(self, place, buf, ring_send, ring_recv, pair_send, pair_recv):
        self.place = place
        self.buf = buf
        self.ring_send, self.ring_recv = ring_send, ring_recv
        self.pair_send, self.pair_recv = pair_send, pair_recv

    def zh(self, plane):
        return self.place.zh if plane == 0 else 1 - self.place.zh

    def cell(self, kind, plane, first, second):
        place = self.place
        dx, dy = (second, first) if kind == 0 else (first, second)
        x = lax.rem(place.x + dx + NX, NX)
        y = lax.rem(place.y + dy + NY, NY)
        return self.buf.at[kind, self.zh(plane), x, y, place.core]

    def line(self, kind, plane, second):
        place, zh = self.place, self.zh(plane)
        if kind == 0:
            return self.buf.at[kind, zh, lax.rem(place.x + second + NX, NX), pl.ds(0, NY), place.core]
        return self.buf.at[kind, zh, pl.ds(0, NX), lax.rem(place.y + second + NY, NY), place.core]

    def copy(self, ref, kind, plane, slot, device):
        index = (kind * 2 + plane) * RING + slot
        return pltpu.make_async_remote_copy(
            src_ref=ref,
            dst_ref=ref,
            send_sem=self.ring_send.at[index],
            recv_sem=self.ring_recv.at[index],
            device_id=device,
            device_id_type=MESH,
        )

    def first(self, kind, plane, i):
        return self.copy(self.cell(kind, plane, 0, 0), kind, plane, i, self.place.along(1 - kind, STEPS[i]))

    def second(self, kind, plane, o, direction):
        ref = self.cell(kind, plane, OFFSETS[o], 0)
        return self.copy(ref, kind, plane, 3 + 2 * o + direction, self.place.along(kind, STEPS[direction]))

    def relay(self, kind, plane, o):
        direction = o // 2
        ref = self.cell(kind, plane, OFFSETS[o], -STEPS[direction])
        return self.copy(ref, kind, plane, 11 + o, self.place.along(kind, STEPS[direction]))

    def pair(self, kind, plane, piece):
        ref = self.line(kind, plane, OFFSETS[piece])
        index = (kind * 2 + plane) * 4 + piece
        return pltpu.make_async_remote_copy(
            src_ref=ref,
            dst_ref=ref,
            send_sem=self.pair_send.at[index],
            recv_sem=self.pair_recv.at[index],
            device_id=self.place.sibling(),
            device_id_type=MESH,
        )

    def start(self, plane):
        for i in range(3):
            for kind in (0, 1):
                self.first(kind, plane, i).start()
        for direction in (0, 1):
            for kind in (0, 1):
                self.second(kind, plane, 0, direction).start()

    def spread(self, plane):
        for i in range(3):
            for kind in (0, 1):
                self.first(kind, plane, i).wait_recv()
                for direction in (0, 1):
                    self.second(kind, plane, 1 + i, direction).start()
        for kind in (0, 1):
            self.pair(kind, plane, 0).start()

    def hand_on(self, plane, offsets=(0, 1, 2, 3)):
        for o in offsets:
            for kind in (0, 1):
                for direction in (0, 1):
                    self.second(kind, plane, o, direction).wait_recv()
                self.relay(kind, plane, o).start()

    def hand_over(self, plane):
        for piece in (1, 2):
            for kind in (0, 1):
                self.pair(kind, plane, piece).start()

    def complete(self, plane):
        for kind in (0, 1):
            for o in range(4):
                self.relay(kind, plane, o).wait_recv()
            self.pair(kind, plane, 3).start()

    def from_sibling(self, plane, pieces=(0, 1, 2, 3)):
        for kind in (0, 1):
            for piece in pieces:
                self.pair(kind, plane, piece).wait_recv()

    def finish(self, plane):
        for kind in (0, 1):
            for i in range(3):
                self.first(kind, plane, i).wait_send()
            for o in range(4):
                for direction in (0, 1):
                    self.second(kind, plane, o, direction).wait_send()
                self.relay(kind, plane, o).wait_send()
                self.pair(kind, plane, o).wait_send()


def last_dims(a, b):
    return lax.dot_general(a, b, (((1,), (1,)), ((), ())), preferred_element_type=jnp.float32)


def cos_sin(angle):
    turns = jnp.floor(angle * (2.0 / math.pi) + 0.5)
    rest = ((angle - turns * 1.5703125) - turns * 4.837512969970703125e-4) - turns * 7.54978995489188216e-8
    square = rest * rest
    sine = ((-1.9515295891e-4 * square + 8.3321608736e-3) * square - 1.6666654611e-1) * square * rest + rest
    cosine = (2.443315711809948e-5 * square - 1.388731625493765e-3) * square + 4.166664568298827e-2
    cosine = cosine * square * square - 0.5 * square + 1.0
    quarter = jnp.bitwise_and(turns.astype(jnp.int32), 3)
    swap = jnp.bitwise_and(quarter, 1) == 1
    cos_part = jnp.where(swap, sine, cosine)
    sin_part = jnp.where(swap, cosine, sine)
    cos_part = jnp.where(jnp.logical_or(quarter == 1, quarter == 2), -cos_part, cos_part)
    sin_part = jnp.where(quarter >= 2, -sin_part, sin_part)
    return cos_part, sin_part


def kernel(
    heads,
    lengths,
    offset,
    q_nope_any,
    q_rope_any,
    prefix_latent,
    prefix_rope_any,
    group_latent,
    group_rope_any,
    frequency_any,
    w_uk_any,
    w_uv_any,
    w_out_any,
    mixed,
    keys,
    prefix_query,
    group_query,
    row_max,
    row_sum,
    accum,
    outs,
    staged,
    passing,
    w_out,
    shares,
    arrived,
    passed,
    q_nope,
    q_rope,
    prefix_rope,
    group_rope,
    w_uk,
    w_uv,
    frequency,
    load_sem,
    k_ring_send,
    k_ring_recv,
    k_pair_send,
    k_pair_recv,
    k_cross_send,
    k_cross_recv,
    o_ring_send,
    o_ring_recv,
    o_pair_send,
    o_pair_recv,
    leg_send,
    leg_recv,
    o_cross_send,
    o_cross_recv,
    swap_send,
    swap_recv,
    w_send,
    w_recv,
    share_send,
    share_recv,
    hop_send,
    hop_recv,
):
    place = Place(heads)
    rows, lat = prefix_latent.shape
    h_dev = w_uk.shape[0]
    part = rows // 2
    half = staged.shape[-1]
    half_heads = heads // 2
    me = place.ctx()
    own = (place.zh, place.x, place.y, place.core)
    odd = lax.rem(place.head, 2)
    paired = place.head + 1 - 2 * odd
    stays = place.core == odd
    moves = place.core != odd
    is_end = jnp.logical_or(place.head == 0, place.head == heads - 1)

    quarter = heads // 2
    legs = []
    for step in (quarter, -quarter):
        leg_zh, leg_head = place.up(step)
        legs.append((place.ctx(zh=leg_zh), leg_head))
    swap_device = (place.ctx(core=1 - place.core), paired)
    swap_across = (place.ctx(zh=1 - place.zh, core=1 - place.core), paired)
    others = [(me, lax.rem(place.head + j, heads)) for j in range(1, heads)]
    far_end = jnp.where(place.head < half_heads, heads - 1, 0)
    served = [jnp.where(place.head == 0, heads - 1 - j, j) for j in range(half_heads)]
    peers = plane_peers(place) + others + [place.across(far_end)]

    greet(peers)

    @pl.when(stays)
    def _():
        greet(legs)

    @pl.when(moves)
    def _():
        greet([swap_device, swap_across])

    @pl.when(is_end)
    def _():
        greet([place.across(head) for head in served])

    loads = [
        pltpu.make_async_copy(src, dst, load_sem.at[i])
        for i, (src, dst) in enumerate(
            (
                (prefix_latent.at[pl.ds(0, part)], keys.at[(0,) + own + (slice(None), pl.ds(0, lat))]),
                (group_latent.at[pl.ds(0, part)], keys.at[(0,) + own + (slice(None), pl.ds(lat + 128, lat))]),
                (q_nope_any, q_nope),
                (q_rope_any, q_rope),
                (prefix_rope_any, prefix_rope),
                (group_rope_any, group_rope),
                (w_uk_any, w_uk),
                (w_uv_any, w_uv),
                (w_out_any, w_out.at[odd]),
                (frequency_any, frequency),
                (prefix_latent.at[pl.ds(part, part)], keys.at[(1,) + own + (slice(None), pl.ds(0, lat))]),
                (group_latent.at[pl.ds(part, part)], keys.at[(1,) + own + (slice(None), pl.ds(lat + 128, lat))]),
            )
        )
    ]
    for load in loads:
        load.start()
    lane = lax.broadcasted_iota(jnp.int32, (rows, 128), 1)
    row = lax.broadcasted_iota(jnp.int32, (rows, 128), 0)
    for i in (9, 4, 5):
        loads[i].wait()
    positions = (offset[0] + me * rows + row).astype(jnp.float32)
    cos_part, sin_part = cos_sin(positions * frequency[...])
    first_half = lax.rem(lane, ROPE) < ROPE // 2
    sin_part = jnp.where(first_half, -sin_part, sin_part)

    def turn(tile):
        swapped = jnp.where(first_half, pltpu.roll(tile, 128 - ROPE // 2, 1), pltpu.roll(tile, ROPE // 2, 1))
        return tile * cos_part + swapped * sin_part

    def twice(ref):
        value = ref[...].astype(jnp.float32)
        return jnp.concatenate([value, value], axis=1)

    unused = jnp.where(lane == 0, UNUSED, 0.0)
    ropes = jnp.where(row < lengths[0], twice(prefix_rope), unused)
    ropes = jnp.where(lane < ROPE, ropes, turn(twice(group_rope))).astype(jnp.bfloat16)
    for kind in (0, 1):
        keys[(kind,) + own + (slice(None), pl.ds(lat, 128))] = ropes[kind * part : (kind + 1) * part]
    for i in (0, 1, 10, 11):
        loads[i].wait()

    pl.semaphore_wait(pltpu.get_barrier_semaphore(), len(peers) + 2 + half_heads * is_end.astype(jnp.int32))

    gather = Gather(place, keys, k_ring_send, k_ring_recv, k_pair_send, k_pair_recv)

    def key_cross(kind, j):
        ref = keys.at[(kind,) + own]
        return pltpu.make_async_remote_copy(
            src_ref=ref,
            dst_ref=ref,
            send_sem=k_cross_send.at[kind * half_heads + j],
            recv_sem=k_cross_recv.at[kind],
            device_id=place.across(served[j]),
            device_id_type=MESH,
        )

    @pl.when(is_end)
    def _():
        for j in reversed(range(half_heads)):
            for kind in (0, 1):
                key_cross(kind, j).start()

    gather.start(0)

    scale = (NOPE + ROPE) ** -0.5 * math.log2(math.e)

    q_rows = h_dev * rows
    loads[2].wait()
    loads[3].wait()
    loads[6].wait()
    mark = jnp.logical_and(lane[:16] == 0, row[:16] == 0)
    prefix_query[pl.ds(q_rows, 16), pl.ds(0, lat)] = jnp.zeros((16, lat), jnp.bfloat16)
    prefix_query[pl.ds(q_rows, 16), pl.ds(lat, 128)] = jnp.where(mark, 1.0, 0.0).astype(jnp.bfloat16)
    for pair in range(h_dev // 2):
        turned = turn(q_rope[:, pair * 128 : (pair + 1) * 128].astype(jnp.float32)) * scale
        other = pltpu.roll(turned, ROPE, 1)
        for side in (0, 1):
            head = 2 * pair + side
            at = pl.ds(head * rows, rows)
            low_part, high_part = (turned, other) if side == 0 else (other, turned)
            prefix_query[at, pl.ds(lat, 128)] = jnp.where(lane < ROPE, low_part, 0.0).astype(jnp.bfloat16)
            group_query[at, pl.ds(0, 128)] = jnp.where(lane >= ROPE, high_part, 0.0).astype(jnp.bfloat16)
            latent = jnp.dot(
                q_nope[:, head * NOPE : (head + 1) * NOPE], w_uk[head], preferred_element_type=jnp.float32
            )
            latent = (latent * scale).astype(jnp.bfloat16)
            prefix_query[at, pl.ds(0, lat)] = latent
            group_query[at, pl.ds(128, lat)] = latent

    row_max[...] = jnp.full(row_max.shape, HIDDEN, jnp.float32)
    row_sum[...] = jnp.zeros(row_sum.shape, jnp.float32)
    accum[...] = jnp.zeros(accum.shape, jnp.float32)
    my_token = me * rows + lax.rem(lax.broadcasted_iota(jnp.int32, (q_rows, 1), 0), rows)

    def attend(plane, lines):
        zh = gather.zh(plane)
        span = NY * part
        index = lax.broadcasted_iota(jnp.int32, (1, span * len(lines)), 1)
        inside = lax.rem(index, span)
        key_token = jnp.zeros(index.shape, jnp.int32)
        blocks = []
        for i, (kind, step, sibling) in enumerate(lines):
            core = 1 - place.core if sibling else place.core
            if kind == 0:
                x = lax.rem(place.x + step + NX, NX)
                blocks.append(keys[0, zh, x, :, core])
                first, stride = place.ctx(zh=zh, x=x, y=0, core=core), 2
            else:
                y = lax.rem(place.y + step + NY, NY)
                blocks.append(keys[1, zh, :, y, core])
                first, stride = place.ctx(zh=zh, x=0, y=y, core=core), 2 * NY
            token = (first + stride * lax.div(inside, part)) * rows + kind * part + lax.rem(inside, part)
            key_token = jnp.where(lax.div(index, span) == i, token, key_token)
        rows_in = jnp.concatenate([block.reshape(span, block.shape[-1]) for block in blocks], axis=0)
        prefix_all = last_dims(prefix_query[...], rows_in[:, : lat + 128])
        hidden = prefix_all[q_rows : q_rows + 1] > UNUSED / 2
        prefix_scores = jnp.where(hidden, HIDDEN, prefix_all[:q_rows])
        group_scores = last_dims(group_query[...], rows_in[:, lat:])
        group_scores = jnp.where(key_token <= my_token, group_scores, HIDDEN)
        old_max = row_max[...]
        new_max = jnp.max(jnp.maximum(prefix_scores, group_scores), axis=1, keepdims=True)
        new_max = jnp.maximum(old_max, new_max)
        prefix_weights = jnp.exp2(prefix_scores - new_max)
        group_weights = jnp.exp2(group_scores - new_max)
        factor = jnp.exp2(old_max - new_max)
        row_max[...] = new_max
        weights = prefix_weights + group_weights
        lanes = weights[:, :128]
        for j in range(1, weights.shape[1] // 128):
            lanes = lanes + weights[:, j * 128 : (j + 1) * 128]
        row_sum[...] = row_sum[...] * factor + lanes
        taken = jnp.dot(prefix_weights.astype(jnp.bfloat16), rows_in[:, :lat], preferred_element_type=jnp.float32)
        taken = taken + jnp.dot(
            group_weights.astype(jnp.bfloat16), rows_in[:, lat + 128 :], preferred_element_type=jnp.float32
        )
        accum[...] = accum[...] * factor + taken

    w_copy = pltpu.make_async_remote_copy(
        src_ref=w_out_any,
        dst_ref=w_out.at[odd],
        send_sem=w_send,
        recv_sem=w_recv,
        device_id=(me, paired),
        device_id_type=MESH,
    )

    def pick(steps, sibling):
        return [(kind, step, sibling) for kind in (0, 1) for step in steps]

    gather.spread(0)
    attend(0, pick((0,), False))
    gather.hand_on(0)
    gather.hand_over(0)
    for kind in (0, 1):
        key_cross(kind, 0).wait_recv()
    gather.start(1)
    w_copy.start()
    attend(0, pick((-1, 1), False))
    gather.complete(0)
    gather.spread(1)
    gather.from_sibling(0, (0, 1, 2))
    attend(0, pick((0, -1), True))
    gather.hand_on(1, (0,))
    attend(0, [(kind, 2, False) for kind in (0, 1)] + [(kind, 1, True) for kind in (0, 1)])
    gather.hand_on(1, (1, 2))
    gather.hand_on(1, (3,))
    gather.hand_over(1)
    attend(1, pick((0, -1, 1), False))
    gather.complete(1)
    gather.from_sibling(0, (3,))
    gather.from_sibling(1, (0, 1, 2))
    attend(1, pick((0, -1, 1), True))
    attend(0, pick((2,), True))
    gather.from_sibling(1, (3,))
    attend(1, pick((2,), False) + pick((2,), True))

    loads[7].wait()
    latent_out = (accum[...] / jnp.sum(row_sum[...], axis=1, keepdims=True)).astype(jnp.bfloat16)
    per_kind = half // VD
    for head in range(h_dev):
        staged[head // per_kind, :, pl.ds((head % per_kind) * VD, VD)] = jnp.dot(
            latent_out[head * rows : (head + 1) * rows], w_uv[head], preferred_element_type=jnp.float32
        ).astype(jnp.bfloat16)

    slot = (place.x, place.y, place.core)
    new_slot = (place.x, place.y, 1 - place.core)

    def leg(kind):
        return pltpu.make_async_remote_copy(
            src_ref=staged.at[kind],
            dst_ref=passing.at[kind],
            send_sem=leg_send.at[kind],
            recv_sem=leg_recv.at[kind],
            device_id=legs[kind],
            device_id_type=MESH,
        )

    def second_leg(kind):
        end_zh = place.up(quarter if kind == 0 else -quarter)[0]
        return pltpu.make_async_remote_copy(
            src_ref=passing.at[kind],
            dst_ref=outs.at[(kind, 1 - end_zh) + slot],
            send_sem=o_cross_send.at[kind],
            recv_sem=o_cross_recv.at[kind],
            device_id=legs[kind],
            device_id_type=MESH,
        )

    def swap(kind):
        return pltpu.make_async_remote_copy(
            src_ref=staged.at[kind],
            dst_ref=outs.at[(kind, place.zh) + new_slot],
            send_sem=swap_send.at[kind],
            recv_sem=swap_recv.at[kind],
            device_id=swap_device,
            device_id_type=MESH,
        )

    def direct(kind):
        return pltpu.make_async_remote_copy(
            src_ref=staged.at[kind],
            dst_ref=outs.at[(kind, place.zh) + new_slot],
            send_sem=o_cross_send.at[kind],
            recv_sem=o_cross_recv.at[kind],
            device_id=swap_across,
            device_id_type=MESH,
        )

    @pl.when(stays)
    def _():
        for kind in (0, 1):
            leg(kind).start()
        for kind in (0, 1):
            outs[(kind, place.zh) + slot] = staged[kind]

    @pl.when(moves)
    def _():
        for kind in (0, 1):
            swap(kind).start()
        for kind in (0, 1):
            direct(kind).start()
        for kind in (0, 1):
            swap(kind).wait_recv()

    spread = Gather(place, outs, o_ring_send, o_ring_recv, o_pair_send, o_pair_recv)
    spread.start(0)
    gather.finish(0)

    @pl.when(stays)
    def _():
        for kind in (0, 1):
            leg(kind).wait_recv()
            second_leg(kind).start()

    block = shares.shape[-1]

    quad = heads // 2
    my_quad = lax.div(place.head, quad)
    inner = jnp.logical_and(place.head >= quad // 2, place.head < quad + quad // 2)
    outer = jnp.logical_not(inner)

    def share(target, slot):
        return pltpu.make_async_remote_copy(
            src_ref=shares.at[target],
            dst_ref=arrived.at[slot],
            send_sem=share_send.at[target],
            recv_sem=share_recv.at[slot],
            device_id=(me, target),
            device_id_type=MESH,
        )

    def near_share(target):
        return share(target, lax.rem(place.head, quad))

    def far_share(target):
        return share(target, quad + lax.rem(place.head, 2))

    def hop(target, x):
        return pltpu.make_async_remote_copy(
            src_ref=shares.at[target],
            dst_ref=passed.at[x],
            send_sem=hop_send.at[x],
            recv_sem=hop_recv.at[x],
            device_id=(me, jnp.where(place.head < quad, place.head + 2, place.head - 2)),
            device_id_type=MESH,
        )

    def part_share(zh, plane):
        total = jnp.zeros((NX * block, w_out.shape[1]), jnp.float32)
        for kind in (0, 1):
            tokens = outs[kind, zh, :, :, plane].reshape(NX * block, half)
            total = total + last_dims(tokens, w_out[plane, :, kind * half : (kind + 1) * half])
        return total

    def send_shares(plane):
        zh = spread.zh(plane)
        total = part_share(zh, place.core)
        spread.from_sibling(plane)
        total = total + part_share(zh, 1 - place.core)
        for x in range(NX):
            target = zh * NX + x
            shares[target] = total[x * block : (x + 1) * block].T.astype(jnp.bfloat16)
        for i in range(NX):
            x = jnp.where(zh == 0, i, NX - 1 - i)
            target = zh * NX + x

            @pl.when(jnp.logical_and(my_quad == zh, target != place.head))
            def _():
                near_share(target).start()

            @pl.when(jnp.logical_and(my_quad != zh, outer))
            def _():
                hop(target, x).start()

    def forward_shares(plane):
        zh = spread.zh(plane)

        @pl.when(jnp.logical_and(my_quad != zh, inner))
        def _():
            for i in range(NX):
                x = jnp.where(zh == 0, i, NX - 1 - i)
                target = zh * NX + x
                hop(target, x).wait_recv()
                total = shares[target].astype(jnp.float32) + passed[x].astype(jnp.float32)
                shares[target] = total.astype(jnp.bfloat16)
                far_share(target).start()

    spread.spread(0)
    gather.finish(1)
    spread.hand_on(0)
    spread.hand_over(0)
    for kind in (0, 1):
        direct(kind).wait_recv()
    spread.start(1)
    spread.complete(0)
    spread.spread(1)
    loads[8].wait()
    w_copy.wait_recv()
    send_shares(0)
    spread.hand_on(1, (0, 1))
    spread.hand_on(1, (2, 3))
    spread.hand_over(1)
    forward_shares(0)
    spread.complete(1)
    send_shares(1)
    forward_shares(1)
    spread.finish(0)
    spread.finish(1)

    own_slot = lax.rem(place.head, quad)
    arrived[own_slot] = shares[place.head]
    for source in range(quad):

        @pl.when(source != own_slot)
        def _():
            share(place.head, source).wait_recv()

    for source in (quad, quad + 1):
        share(place.head, source).wait_recv()

    total = jnp.zeros(mixed.shape, jnp.float32)
    source_lane = lax.broadcasted_iota(jnp.int32, (block, mixed.shape[1]), 0)
    token = lax.broadcasted_iota(jnp.int32, (block, mixed.shape[1]), 1)
    for plane in (0, 1):
        summed = jnp.zeros(shares.shape[1:], jnp.float32)
        for source in range(plane, quad + 2, 2):
            summed = summed + arrived[source].astype(jnp.float32)
        lane_of = lax.div(token, 2 * rows) * rows + lax.rem(token, rows)
        here = jnp.logical_and(lane_of == source_lane, lax.rem(lax.div(token, rows), 2) == plane)
        total = total + jnp.dot(
            summed.astype(jnp.bfloat16), jnp.where(here, 1.0, 0.0).astype(jnp.bfloat16), preferred_element_type=jnp.float32
        )
    mixed[...] = total.astype(jnp.bfloat16)

    w_copy.wait_send()

    @pl.when(is_end)
    def _():
        for j in range(half_heads):
            for kind in (0, 1):
                key_cross(kind, j).wait_send()

    @pl.when(stays)
    def _():
        for kind in (0, 1):
            leg(kind).wait_send()
            second_leg(kind).wait_send()

    @pl.when(moves)
    def _():
        for kind in (0, 1):
            swap(kind).wait_send()
            direct(kind).wait_send()

    for x in range(NX):

        @pl.when(x != own_slot)
        def _():
            near_share(my_quad * quad + x).wait_send()

        @pl.when(inner)
        def _():
            far_share((1 - my_quad) * quad + x).wait_send()

        @pl.when(outer)
        def _():
            hop((1 - my_quad) * quad + x, x).wait_send()


def gather_scratch():
    return [
        pltpu.SemaphoreType.DMA((4 * RING,)),
        pltpu.SemaphoreType.DMA((4 * RING,)),
        pltpu.SemaphoreType.DMA((16,)),
        pltpu.SemaphoreType.DMA((16,)),
    ]


def on_device(
    heads,
    q_nope,
    q_rope,
    prefix_latent,
    prefix_rope,
    group_latent,
    group_rope,
    lengths,
    offset,
    w_uk,
    w_uv,
    w_out,
):
    rows, lat = prefix_latent.shape
    h_dev = w_uk.shape[0]
    q_rows = rows * h_dev
    width = 2 * lat + 128
    columns = w_out.shape[1]
    half = h_dev * VD // 2
    frequency = 10000.0 ** (-2.0 * (np.arange(128) % (ROPE // 2)) / ROPE)
    frequency = jnp.asarray(frequency[None, :], jnp.float32)

    tokens = rows * 2 * 2 * NX * NY
    block = rows * NY
    vmem = pl.BlockSpec(memory_space=pltpu.VMEM)
    smem = pl.BlockSpec(memory_space=pltpu.SMEM)
    anywhere = pl.BlockSpec(memory_space=pl.ANY)
    dma = pltpu.SemaphoreType.DMA
    mixed = pl.pallas_call(
        functools.partial(kernel, heads),
        out_shape=pltpu.VMEM((columns, tokens // heads), jnp.bfloat16),
        in_specs=[smem] * 2 + [anywhere] * 10,
        out_specs=vmem,
        scratch_shapes=[
            pltpu.VMEM((2, 2, NX, NY, 2, rows // 2, width), jnp.bfloat16),
            pltpu.VMEM((q_rows + 16, lat + 128), jnp.bfloat16),
            pltpu.VMEM((q_rows, lat + 128), jnp.bfloat16),
            pltpu.VMEM((q_rows, 1), jnp.float32),
            pltpu.VMEM((q_rows, 128), jnp.float32),
            pltpu.VMEM((q_rows, lat), jnp.float32),
            pltpu.VMEM((2, 2, NX, NY, 2, rows, half), jnp.bfloat16),
            pltpu.VMEM((2, rows, half), jnp.bfloat16),
            pltpu.VMEM((2, rows, half), jnp.bfloat16),
            pltpu.VMEM((2, columns, 2 * half), jnp.bfloat16),
            pltpu.VMEM((heads, columns, block), jnp.bfloat16),
            pltpu.VMEM((heads // 2 + 2, columns, block), jnp.bfloat16),
            pltpu.VMEM((NX, columns, block), jnp.bfloat16),
            pltpu.VMEM(q_nope.shape, jnp.bfloat16),
            pltpu.VMEM(q_rope.shape, jnp.bfloat16),
            pltpu.VMEM(prefix_rope.shape, jnp.bfloat16),
            pltpu.VMEM(group_rope.shape, jnp.bfloat16),
            pltpu.VMEM(w_uk.shape, jnp.bfloat16),
            pltpu.VMEM(w_uv.shape, jnp.bfloat16),
            pltpu.VMEM((1, 128), jnp.float32),
            dma((12,)),
        ]
        + gather_scratch()
        + [dma((heads,)), dma((2,))]
        + gather_scratch()
        + [dma((2,)), dma((2,)), dma((2,)), dma((2,)), dma((2,)), dma((2,))]
        + [dma(()), dma(()), dma((heads,)), dma((heads // 2 + 2,)), dma((NX,)), dma((NX,))],
        compiler_params=pltpu.CompilerParams(
            collective_id=0, has_side_effects=True, vmem_limit_bytes=60 * 1024 * 1024
        ),
        name="attention_and_output",
    )(
        lengths,
        offset,
        q_nope,
        q_rope,
        prefix_latent,
        prefix_rope,
        group_latent,
        group_rope,
        frequency,
        w_uk,
        w_uv,
        w_out.T,
    )
    return mixed.T


def solution(mesh):
    return jax.shard_map(
        functools.partial(on_device, mesh.shape["head"]),
        mesh=mesh,
        in_specs=(
            P("ctx", "head"),
            P("ctx", "head"),
            P("ctx", None),
            P("ctx", None),
            P("ctx", None),
            P("ctx", None),
            P("ctx"),
            P(),
            P("head", None, None),
            P("head", None, None),
            P("head", "ctx"),
        ),
        out_specs=P("head", "ctx"),
        check_vma=False,
    )
```
